32 devices in a mesh: slab: 4 (over y, core), col: 8 (over z, x).
Axes of the slice: x: 2, y: 2, z: 4, core: 2. Of those that a mesh axis runs over, the one named last changes fastest.
Arguments:
- load: float32 [3, 64, 128, 128], P(None, 'slab', 'col'), may hold values from -6 to 6
- density: int32 [64, 128, 128], P('slab', 'col'), may hold values from 0 to 7
- moduli: float32 [8], replicated, may hold values from 0.1 to 10
- fixed: int32 [64, 128, 128], P('slab', 'col'), may hold values 0 or 1
Outputs:
- solution_field: float32 [3, 64, 128, 128], P(None, 'slab', 'col')
- residual: float32 [3, 64, 128, 128], P(None, 'slab', 'col')
The draws below stay inside these ranges and needn't reach their ends.
All inputs are finite; a program needn't handle non-finite values. No bound on the sum of `fixed` on one device may be relied on, other than what follows from the above.
Results may differ from the reference program's by a relative error of at most 0.0001.
Values sent between devices are 32-bit elements; how exact they have to be, the bound alone decides.
A program may use at most 128 MiB of HBM per device.

```python
import math
import jax
import jax.numpy as jnp

NX = 128
LEVELS = 3
PRE = 2
POST = 2
COARSE_SWEEPS = 8
CLASSES = 8
NZ = 64
NY = 128


def set_ends(array, rng, least, high):
    place = [jax.random.randint(jax.random.fold_in(rng, axis), (), 0, length) for axis, length in enumerate(array.shape)]
    widest = array.shape.index(max(array.shape))
    neighbour = place[:widest] + [(place[widest] + 1) % array.shape[widest]] + place[widest + 1:]
    return array.at[tuple(place)].set(least).at[tuple(neighbour)].set(high)


def steps_of(own_key, dims, pieces, smallest, top_value):
    loudness = 1.0
    for dim, parts in pieces:
        heights = jax.random.uniform(jax.random.fold_in(jax.random.fold_in(own_key, 6), dim), (parts,), jnp.float32, smallest / len(pieces), top_value / len(pieces))
        loudness = loudness * jnp.repeat(jnp.exp(heights), dims[dim] // parts).reshape((-1,) + (1,) * (len(dims) - 1 - dim))
    return loudness


def centred(rng, shape, scale, bound, split=(), held_as=jnp.bfloat16):
    drawn = jax.random.normal(rng, shape, jnp.float32) * scale
    if len(split) > 0:
        drawn = steps_of(rng, shape, split, -0.22, 0.18) * drawn
    return jnp.clip(drawn, min=-bound, max=bound).astype(held_as)


def setup_inputs(seed: int = 0) -> dict:
    key_list = jax.random.split(jax.random.key(seed), 5)
    return {
        "load": centred(key_list[0], (3, NZ, NY, NX), 1.0, 6.0, ((1, 4), (2, 8)), jnp.float32),
        "density": set_ends(jax.random.randint(key_list[1], (NZ, NY, NX), 0, CLASSES), jax.random.fold_in(key_list[1], 1), 0, CLASSES - 1).astype(jnp.int32),
        "moduli": jnp.clip(jnp.exp(jax.random.uniform(key_list[2], (CLASSES,), jnp.float32, math.log(0.1), math.log(10.0))), 0.1, 10.0),
        "fixed": set_ends((jax.random.randint(key_list[3], (NZ, NY, NX), 0, 8) < 1).astype(jnp.int32), jax.random.fold_in(key_list[3], 1), 0, 1),
    }


OMEGA = 0.6
COUPLE = 0.05


def shrink(arr):
    lead = arr.shape[:-3]
    za, yb, xc = arr.shape[-3:]
    blocks = arr.reshape(tuple(lead) + (za // 2, 2, yb // 2, 2, xc // 2, 2))
    return blocks.mean(axis=(-5, -3, -1))


def grow(arr):
    return jnp.repeat(jnp.repeat(jnp.repeat(arr, 2, axis=-3), 2, axis=-2), 2, axis=-1)


def beside_all(padded):
    return [padded[..., 2:, 1:-1, 1:-1], padded[..., :-2, 1:-1, 1:-1],
            padded[..., 1:-1, 2:, 1:-1], padded[..., 1:-1, :-2, 1:-1],
            padded[..., 1:-1, 1:-1, 2:], padded[..., 1:-1, 1:-1, :-2]]


def diagonal_of(stiff_pad, scale):
    centre = stiff_pad[1:-1, 1:-1, 1:-1]
    total = jnp.zeros_like(centre)
    for near in beside_all(stiff_pad):
        total = total + 0.5 * (centre + near)
    return scale * total + 2.0 * COUPLE * centre


def apply_op(field_pad, stiff_pad, scale):
    centre = stiff_pad[1:-1, 1:-1, 1:-1]
    field = field_pad[:, 1:-1, 1:-1, 1:-1]
    total = jnp.zeros_like(field)
    for near_k, near_u in zip(beside_all(stiff_pad), beside_all(field_pad)):
        total = total + 0.5 * (centre + near_k) * (field - near_u)
    return scale * total + COUPLE * centre * (field + jnp.sum(field, axis=0, keepdims=True))


def pad_field(field):
    return jnp.pad(field, ((0, 0), (1, 1), (1, 1), (1, 1)))


def sweeps(field, rhs, stiff_pad, diag, scale, weight, count):
    if field is None:
        field = OMEGA * weight * rhs / diag
        count = count - 1
    for turn in range(count):
        field = field + OMEGA * weight * (rhs - apply_op(pad_field(field), stiff_pad, scale)) / diag
    return field


def reference(load, density, moduli, fixed):
    stiff = jnp.zeros(density.shape, jnp.float32)
    for klass in range(CLASSES):
        stiff = stiff + jnp.where(density == klass, moduli[klass], jnp.float32(0.0))
    mask = 1.0 - fixed.astype(jnp.float32)
    pads, diags = [], []
    for level in range(LEVELS + 1):
        padded = jnp.pad(stiff, 1)
        pads.append(padded)
        diags.append(diagonal_of(padded, 0.25 ** level))
        if level < LEVELS:
            stiff = shrink(stiff)
    saved = []
    rhs = load
    for level in range(LEVELS):
        weight = mask if level == 0 else 1.0
        scale = 0.25 ** level
        field = sweeps(None, rhs, pads[level], diags[level], scale, weight, PRE)
        resid = weight * (rhs - apply_op(pad_field(field), pads[level], scale))
        saved.append((field, rhs))
        rhs = shrink(resid)
    field = sweeps(None, rhs, pads[LEVELS], diags[LEVELS], 0.25 ** LEVELS, 1.0, COARSE_SWEEPS)
    for level in range(LEVELS - 1, -1, -1):
        weight = mask if level == 0 else 1.0
        fine, rhs = saved[level]
        field = fine + weight * grow(field)
        field = sweeps(field, rhs, pads[level], diags[level], 0.25 ** level, weight, POST)
    residual = mask * (load - apply_op(pad_field(field), pads[0], 1.0))
    return field, residual
```

```python
import jax
import jax.numpy as jnp
from jax import lax
from jax.experimental import pallas as pl
from jax.experimental.pallas import tpu as pltpu
from jax.sharding import PartitionSpec as P

OMEGA = 0.6
COUPLE = 0.05
CLASSES = 8
COARSE_SWEEPS = 8
LANES = 128
F32 = jnp.float32
DIRS = ((0, 1), (0, -1), (1, 0), (-1, 0), (1, 1), (1, -1), (-1, 1), (-1, -1))


class Grid:
    def __init__(self, nz, ny, oz, oy):
        self.nz, self.ny, self.oz, self.oy = nz, ny, oz, oy
        self.z, self.y = nz + 2 * oz, ny + 2 * oy
        self.rows = self.z * self.y

    def row(self, comp, z, y):
        return comp * self.rows + (z + self.oz) * self.y + y + self.oy

    def plane(self, comp, z):
        start = comp * self.rows + z * self.y
        if not isinstance(start, int):
            start = pl.multiple_of(start, 8)
        return pl.ds(start, self.y)


def segments(grid, dz, dy, depth):
    nz, ny = grid.nz, grid.ny

    def cell(step, d, n):
        return (n - step, -step) if d > 0 else (step - 1, n - 1 + step)

    out = []
    if dz == 0:
        for i in range(1, depth + 1):
            mine, there = cell(i, dy, ny)
            out.append((0, mine, 0, there, nz, True))
    elif dy == 0:
        for i in range(1, depth + 1):
            mine, there = cell(i, dz, nz)
            out.append((mine, 0, there, 0, ny, False))
    else:
        for i in range(1, depth):
            for j in range(1, depth + 1 - i):
                mz, tz = cell(i, dz, nz)
                my, ty = cell(j, dy, ny)
                out.append((mz, my, tz, ty, 1, False))
    return out


def message(grid, dz, dy, fields):
    out, at = [], 0
    for field, (comps, depth) in enumerate(fields):
        for comp in range(comps):
            for seg in segments(grid, dz, dy, depth):
                out.append((field, comp, seg, at))
                at += seg[4]
    return out, -(-at // 8) * 8


def window(grid, comp, z, y, count, along_z):
    start = grid.row(comp, z, y)
    if along_z:
        return pl.ds(start, count, stride=grid.y)
    return pl.ds(start, count)


class Exchange:
    def __init__(self, grid, fields, where, send, recv, ssem, rsem):
        self.grid, self.fields, self.where = grid, fields, where
        self.send, self.recv, self.ssem, self.rsem = send, recv, ssem, rsem

    def copy(self, d):
        dz, dy = DIRS[d]
        s, c, ns, nc = self.where
        target = (lax.rem(s + dz + ns, ns), lax.rem(c + dy + nc, nc))
        return pltpu.make_async_remote_copy(
            src_ref=self.send[d], dst_ref=self.recv[d], send_sem=self.ssem.at[d], recv_sem=self.rsem.at[d],
            device_id=target, device_id_type=pl.DeviceIdType.MESH)

    def exists(self, dz, dy):
        s, c, ns, nc = self.where
        ok = None
        for here, d, n in ((s, dz, ns), (c, dy, nc)):
            if d:
                near = here < n - 1 if d > 0 else here > 0
                ok = near if ok is None else jnp.logical_and(ok, near)
        return ok

    def start(self, refs):
        for d, (dz, dy) in enumerate(DIRS):
            rows, _ = message(self.grid, dz, dy, self.fields)

            @pl.when(self.exists(dz, dy))
            def _():
                for field, comp, (z, y, _, _, count, along), at in rows:
                    self.send[d][pl.ds(at, count), :] = refs[field][window(self.grid, comp, z, y, count, along), :]
                self.copy(d).start()

    def finish(self, refs):
        for d, (dz, dy) in enumerate(DIRS):
            rows, _ = message(self.grid, dz, dy, self.fields)

            @pl.when(self.exists(-dz, -dy))
            def _():
                self.copy(d).wait_recv()
                for field, comp, (_, _, z, y, count, along), at in rows:
                    refs[field][window(self.grid, comp, z, y, count, along), :] = self.recv[d][pl.ds(at, count), :]

    def drain(self):
        for d, (dz, dy) in enumerate(DIRS):
            @pl.when(self.exists(dz, dy))
            def _():
                self.copy(d).wait_send()


def lane_iota(rows):
    return lax.broadcasted_iota(jnp.int32, (rows, LANES), 1)


def right(v, step):
    return pltpu.roll(v, step % LANES, 1)


def left(v, step):
    return pltpu.roll(v, LANES - step, 1)


def down(v):
    return pltpu.roll(v, 1, 0)


def up(v):
    return pltpu.roll(v, v.shape[0] - 1, 0)


def pair_sum(v, step):
    lane = lane_iota(v.shape[0])
    first = lane % (2 * step) < step
    return v + jnp.where(first, left(v, step), right(v, step))


def rows_of(start, count):
    if not isinstance(start, int):
        start = pl.multiple_of(start, 8)
    return pl.ds(start, count)


class Level:
    def __init__(self, scale, xs, zs, group, ny, closed, plane, k, coef, size):
        self.scale, self.xs, self.zs, self.group, self.ny, self.closed = scale, xs, zs, group, ny, closed
        self.plane, self.k, self.coef, self.size = plane, k, coef, size

    def at(self, which, z):
        p = self.plane(0, z)
        return self.coef[which][p, :]

    def z_sides(self, get, z):
        after, before = get(z + 1), get(z - 1)
        if not self.group:
            return after, before
        here = get(z)
        lane = lane_iota(self.ny) % self.group
        turn = self.group - self.zs
        return (jnp.where(lane < turn, left(here, self.zs), right(after, turn)),
                jnp.where(lane >= self.zs, right(here, self.zs), left(before, turn)))

    def setup(self, low, high, mask):
        def body(z, carry):
            get = lambda i: self.k[self.plane(0, i), :]
            k = get(z)
            lane = lane_iota(self.ny)
            zp, zm = self.z_sides(get, z)
            inx = lane < LANES - self.xs
            inm = lane >= self.xs
            xp = jnp.where(inx, left(k, self.xs), 0.0)
            xm = jnp.where(inm, right(k, self.xs), 0.0)
            yp, ym = up(k), down(k)
            half = F32(0.5 * self.scale)
            if self.closed:
                row = lax.broadcasted_iota(jnp.int32, (self.ny, LANES), 0)
                iny, inw = row < self.ny - 1, row >= 1
                yp, ym = jnp.where(iny, yp, 0.0), jnp.where(inw, ym, 0.0)
            kzp, kzm = half * (k + zp), half * (k + zm)
            kyp, kym = half * (k + yp), half * (k + ym)
            kxp, kxm = half * (k + xp), half * (k + xm)
            total = kzp + kzm + kyp + kym + kxp + kxm
            if self.closed:
                kyp, kym = jnp.where(iny, kyp, 0.0), jnp.where(inw, kym, 0.0)
            kxp, kxm = jnp.where(inx, kxp, 0.0), jnp.where(inm, kxm, 0.0)
            inside = k > 0.0
            diag = jnp.where(inside, total + F32(2.0 * COUPLE) * k, 1.0)
            weight = jnp.where(inside, F32(OMEGA) / diag, 0.0)
            p = self.plane(0, z)
            if mask is not None:
                weight = weight * mask[p, :]
            for which, value in enumerate((kzp, kzm, kyp, kym, kxp, kxm, total + F32(COUPLE) * k, weight)):
                self.coef[which][p, :] = value
            return carry

        lax.fori_loop(low, high, body, 0)

    def first(self, low, high, rhs, out):
        def body(z, carry):
            weight = self.at(7, z)
            for c in range(3):
                p = self.plane(c, z)
                out[p, :] = weight * rhs[p, :]
            return carry

        lax.fori_loop(low, high, body, 0)

    def defect(self, z, u, rhs):
        kzp, kzm, kyp, kym, kxp, kxm, own = [self.at(i, z) for i in range(7)]
        couple = F32(COUPLE) * self.k[self.plane(0, z), :]
        field = [u[self.plane(c, z), :] for c in range(3)]
        shared = couple * (field[0] + field[1] + field[2])
        out = []
        for c in range(3):
            v = field[c]
            zp, zm = self.z_sides(lambda i: u[self.plane(c, i), :], z)
            near = (kzp * zp + kzm * zm) + (kyp * up(v) + kym * down(v))
            near = near + (kxp * left(v, self.xs) + kxm * right(v, self.xs))
            out.append((rhs[self.plane(c, z), :] - shared) + (near - own * v))
        return field, out

    def sweep(self, low, high, u, rhs, out, out_plane=None):
        place = out_plane or self.plane

        def body(z, carry):
            field, out_d = self.defect(z, u, rhs)
            weight = self.at(7, z)
            for c in range(3):
                out[place(c, z), :] = field[c] + weight * out_d[c]
            return carry

        lax.fori_loop(low, high, body, 0)

    def residual(self, low, high, u, rhs, mask, out):
        def body(z, carry):
            _, out_d = self.defect(z, u, rhs)
            for c in range(3):
                value = out_d[c]
                if mask is not None:
                    value = mask[self.plane(0, z), :] * value
                out(c, z, value)
            return carry

        lax.fori_loop(low, high, body, 0)


def kernel(ns, nc, g0, g1, ex, load, dens, moduli, fixed, out_u, out_r, *scratch):
    it = iter(scratch)
    take = lambda n: [next(it) for _ in range(n)]
    k0, m0, b0, ua, ub = take(5)
    c0 = take(8)
    k1, b1, va, vb = take(4)
    c1 = take(8)
    k2, b2, wa, wb, wf = take(5)
    c2 = take(8)
    k3, b3, xa, xb = take(4)
    c3 = take(8)
    pack, gather, stage = take(3)
    s, c = lax.axis_index("slab"), lax.axis_index("col")
    where = (s, c, ns, nc)
    rounds = []
    for grid, fields in ex:
        send, recv = take(8), take(8)
        ssem, rsem = take(2)
        rounds.append(Exchange(grid, fields, where, send, recv, ssem, rsem))
    gsend, grecv = take(2)
    ex_a, ex_k, ex_b, ex_u, ex_v = rounds
    n0, y0, n1, y1 = g0.nz, g0.ny, g1.nz, g1.ny

    def zero(ref):
        rows = ref.shape[0]
        ref[...] = jnp.zeros((rows, LANES), F32)

    for ref in (k0, m0, b0, k1):
        zero(ref)

    def fill(z, carry):
        src = pl.ds(pl.multiple_of(z * y0, 8), y0)
        d = dens[src, :]
        value = jnp.zeros((y0, LANES), F32)
        for klass in range(CLASSES):
            value = jnp.where(d == klass, moduli[klass], value)
        keep = 1.0 - fixed[src, :].astype(F32)
        wide = lambda v: jnp.concatenate(
            [jnp.zeros((g0.oy, LANES), F32), v, jnp.zeros((g0.oy, LANES), F32)], axis=0)
        k0[g0.plane(0, z + g0.oz), :] = wide(value)
        m0[g0.plane(0, z + g0.oz), :] = wide(keep)
        for comp in range(3):
            at = pl.ds(pl.multiple_of((comp * n0 + z) * y0, 8), y0)
            b0[g0.plane(comp, z + g0.oz), :] = wide(load[at, :])
        return carry

    lax.fori_loop(0, n0, fill, 0)
    ex_a.start([k0, m0, b0])

    def coarser(src, grid, comp, z, y, count, steps):
        total = None
        for dz in range(2):
            for dy in range(2):
                part = src[pl.ds(grid.row(comp, 2 * z + dz, 2 * y + dy), count, stride=2), :]
                total = part if total is None else total + part
        for step in steps:
            total = pair_sum(total, step)
        return total * F32(0.125)

    for z in range(n1):
        k1[pl.ds(g1.row(0, z, 0), y1), :] = coarser(k0, g0, 0, z, 0, y1, (1,))
    ex_k.start([k1])

    lane4 = lane_iota(4) % 4

    def packed(src, comp, slot):
        value = jnp.zeros((4, LANES), F32)
        for z in range(n1 // 2):
            value = jnp.where(lane4 == z, coarser(src, g1, comp, z, 0, y1 // 2, (2,)), value)
        pack[pl.ds(4 * slot, 4), :] = value

    packed(k1, 0, 3)
    for ref in (ua, ub, b1, va, vb):
        zero(ref)

    level0 = Level(1.0, 1, 0, 0, g0.y, False, g0.plane, k0, c0, g0.z)
    level1 = Level(0.25, 2, 0, 0, g1.y, False, g1.plane, k1, c1, g1.z)
    y2, y3 = 4 * nc, 2 * nc
    plane2 = lambda comp, z: rows_of((comp * (ns + 2) + z) * y2, y2)
    plane3 = lambda comp, z: rows_of((comp * (ns + 2) + z) * y3, y3)
    wide2 = lambda comp, z: rows_of((comp * (ns + 2) + z) * (y2 + 16) + 8, y2)
    level2 = Level(0.25**2, 4, 1, 4, y2, True, plane2, k2, c2, ns)
    level3 = Level(0.25**3, 8, 2, 4, y3, True, plane3, k3, c3, ns)
    for ref, comps, plane, rows in ((k2, 1, plane2, y2), (wa, 3, plane2, y2), (wb, 3, plane2, y2),
                                    (k3, 1, plane3, y3), (xa, 3, plane3, y3), (xb, 3, plane3, y3),
                                    (wf, 3, lambda comp, z: rows_of((comp * (ns + 2) + z) * (y2 + 16), y2 + 16), y2 + 16)):
        for comp in range(comps):
            for z in (0, ns + 1):
                ref[plane(comp, z), :] = jnp.zeros((rows, LANES), F32)

    ex_a.finish([k0, m0, b0])
    level0.setup(g0.oz - 2, g0.oz + n0 + 2, m0)
    level0.first(g0.oz - 2, g0.oz + n0 + 2, b0, ua)
    level0.sweep(g0.oz - 1, g0.oz + n0 + 1, ua, b0, ub)

    def keep0(comp, z, value):
        ua[g0.plane(comp, z), :] = value

    level0.residual(g0.oz, g0.oz + n0, ub, b0, m0, keep0)
    for comp in range(3):
        for z in range(n1):
            b1[pl.ds(g1.row(comp, z, 0), y1), :] = coarser(ua, g0, comp, z, 0, y1, (1,))
    ex_b.start([b1])
    ex_u.start([ub, m0])

    ex_k.finish([k1])
    level1.setup(g1.oz - 3, g1.oz + n1 + 3, None)
    ex_b.finish([b1])
    level1.first(g1.oz - 2, g1.oz + n1 + 2, b1, va)
    level1.sweep(g1.oz - 1, g1.oz + n1 + 1, va, b1, vb)

    def keep1(comp, z, value):
        va[g1.plane(comp, z), :] = value

    level1.residual(g1.oz, g1.oz + n1, vb, b1, None, keep1)
    for comp in range(3):
        packed(va, comp, comp)

    here = pl.ds(pl.multiple_of((s * nc + c) * 16, 16), 16)
    gather[here, :] = pack[...]

    def spread(t):
        target = (lax.rem(s + t // nc, ns), lax.rem(c + t % nc, nc))
        return pltpu.make_async_remote_copy(
            src_ref=gather.at[here], dst_ref=gather.at[here], send_sem=gsend.at[t], recv_sem=grecv.at[t],
            device_id=target, device_id_type=pl.DeviceIdType.MESH)

    def start_one(t, carry):
        spread(t).start()
        return carry

    lax.fori_loop(1, ns * nc, start_one, 0)
    ex_v.start([vb])

    def wait_one(t, carry):
        spread(t).wait_recv()
        return carry

    lax.fori_loop(1, ns * nc, wait_one, 0)

    def assemble(t, carry):
        z, pair = t // (nc // 2), t % (nc // 2)
        first = gather[pl.ds(pl.multiple_of(t * 32, 32), 16), :]
        second = gather[pl.ds(pl.multiple_of(t * 32 + 16, 16), 16), :]
        for f in range(4):
            value = jnp.concatenate([first[4 * f:4 * f + 4], second[4 * f:4 * f + 4]], axis=0)
            ref, comp = (k2, 0) if f == 3 else (b2, f)
            ref[pl.ds(pl.multiple_of((comp * (ns + 2) + z + 1) * y2 + pair * 8, 8), 8), :] = value
        return carry

    lax.fori_loop(0, ns * nc // 2, assemble, 0)
    level2.setup(1, ns + 1, None)
    level2.first(1, ns + 1, b2, wa)
    level2.sweep(1, ns + 1, wa, b2, wb)

    def keep2(comp, z, value):
        wa[plane2(comp, z), :] = value

    level2.residual(1, ns + 1, wb, b2, None, keep2)

    def shrink3(z, carry):
        for src, dst, comp in ((k2, k3, 0), (wa, b3, 0), (wa, b3, 1), (wa, b3, 2)):
            start = (comp * (ns + 2) + z) * y2
            total = src[pl.ds(start, y3, stride=2), :] + src[pl.ds(start + 1, y3, stride=2), :]
            dst[plane3(comp, z), :] = pair_sum(pair_sum(total, 1), 4) * F32(0.125)
        return carry

    lax.fori_loop(1, ns + 1, shrink3, 0)
    level3.setup(1, ns + 1, None)
    level3.first(1, ns + 1, b3, xa)
    old, new = xa, xb
    for turn in range(COARSE_SWEEPS - 1):
        level3.sweep(1, ns + 1, old, b3, new)
        old, new = new, old
    coarse = old

    def add2(z, carry):
        for comp in range(3):
            value = coarse[plane3(comp, z), :]
            stage[pl.ds(0, y3, stride=2), :] = value
            stage[pl.ds(1, y3, stride=2), :] = value
            p = plane2(comp, z)
            wb[p, :] = wb[p, :] + stage[pl.ds(0, y2), :]
        return carry

    lax.fori_loop(1, ns + 1, add2, 0)

    def clear(ref):
        for comp in range(3):
            for z in (0, ns + 1):
                ref[plane2(comp, z), :] = jnp.zeros((y2, LANES), F32)

    clear(wa)
    level2.sweep(1, ns + 1, wb, b2, wa)
    level2.sweep(1, ns + 1, wa, b2, wf, wide2)

    ex_v.finish([vb])
    lane8 = lane_iota(8)
    odd = c % 2 == 1

    def add1(i, carry):
        z2 = i + 4 * s + 2
        block, j = z2 // 4, z2 % 4
        for comp in range(3):
            at = (comp * (ns + 2) + block) * (y2 + 16) + (c // 2) * 8
            rows = wf[pl.ds(pl.multiple_of(at, 8), 24), :]
            value = jnp.where(odd, rows[10:18], rows[6:14])
            lane = lane8 % 4
            value = jnp.where(lane == j, value, 0.0)
            value = pair_sum(pair_sum(value, 1), 2)
            stage[pl.ds(0, 8, stride=2), :] = value
            stage[pl.ds(1, 8, stride=2), :] = value
            grown = stage[pl.ds(0, 16), :]
            for dz in range(2):
                p = g1.plane(comp, 2 * i + dz)
                inside = k1[g1.plane(0, 2 * i + dz), :] > 0.0
                va[p, :] = vb[p, :] + jnp.where(inside, grown, 0.0)
        return carry

    lax.fori_loop(0, g1.z // 2, add1, 0)
    level1.sweep(g1.oz - 3, g1.oz + n1 + 3, va, b1, vb)
    level1.sweep(g1.oz - 2, g1.oz + n1 + 2, vb, b1, va)

    ex_u.finish([ub, m0])

    def add0(z, carry):
        for comp in range(3):
            near = (z - g0.oz + 2 * g1.oz) // 2
            value = va[g1.plane(comp, near), :][2:14]
            stage[pl.ds(0, 12, stride=2), :] = value
            stage[pl.ds(1, 12, stride=2), :] = value
            p = g0.plane(comp, z)
            ua[p, :] = ub[p, :] + m0[g0.plane(0, z), :] * stage[pl.ds(0, g0.y), :]
        return carry

    lax.fori_loop(0, g0.z, add0, 0)
    level0.sweep(g0.oz - 2, g0.oz + n0 + 2, ua, b0, ub)
    level0.sweep(g0.oz - 1, g0.oz + n0 + 1, ub, b0, ua)

    def emit(comp, z, value):
        at = pl.ds(pl.multiple_of((comp * n0 + z - g0.oz) * y0, 8), y0)
        out_r[at, :] = value[g0.oy:g0.oy + y0]
        out_u[at, :] = ua[g0.plane(comp, z), :][g0.oy:g0.oy + y0]

    level0.residual(g0.oz, g0.oz + n0, ua, b0, m0, emit)

    def drain_one(t, carry):
        spread(t).wait_send()
        return carry

    lax.fori_loop(1, ns * nc, drain_one, 0)
    for ex_one in rounds:
        ex_one.drain()


def on_device(ns, nc, load, density, moduli, fixed):
    _, nz, ny, nx = load.shape
    g0 = Grid(nz, ny, 3, 4)
    g1 = Grid(nz // 2, ny // 2, 4, 4)
    ex = (
        (g0, ((1, 3), (1, 2), (3, 2))),
        (g1, ((1, 4),)),
        (g1, ((3, 3),)),
        (g0, ((3, 3), (1, 3))),
        (g1, ((3, 4),)),
    )
    buf = lambda rows: pltpu.VMEM((rows, LANES), F32)
    y2, y3 = 4 * nc, 2 * nc
    s2, s3 = (ns + 2) * y2, (ns + 2) * y3
    scratch = [buf(g0.rows)] * 2 + [buf(3 * g0.rows)] * 3 + [buf(g0.rows)] * 8
    scratch += [buf(g1.rows)] + [buf(3 * g1.rows)] * 3 + [buf(g1.rows)] * 8
    scratch += [buf(s2)] + [buf(3 * s2)] * 3 + [buf(3 * (ns + 2) * (y2 + 16))] + [buf(s2)] * 8
    scratch += [buf(s3)] + [buf(3 * s3)] * 3 + [buf(s3)] * 8
    scratch += [buf(16), buf(ns * nc * 16), buf(max(y2, 32))]
    for grid, fields in ex:
        sizes = [message(grid, dz, dy, fields)[1] for dz, dy in DIRS]
        scratch += [buf(n) for n in sizes] * 2
        scratch += [pltpu.SemaphoreType.DMA((8,))] * 2
    scratch += [pltpu.SemaphoreType.DMA((ns * nc,))] * 2

    def run(*args):
        kernel(ns, nc, g0, g1, ex, *args)

    rows = 3 * nz * ny
    vmem = pl.BlockSpec(memory_space=pltpu.VMEM)
    u, r = pl.pallas_call(
        run,
        out_shape=[jax.ShapeDtypeStruct((rows, nx), F32)] * 2,
        in_specs=[vmem, vmem, pl.BlockSpec(memory_space=pltpu.SMEM), vmem],
        out_specs=[vmem, vmem],
        scratch_shapes=scratch,
        compiler_params=pltpu.CompilerParams(has_side_effects=True, vmem_limit_bytes=56 * 1024 * 1024),
        name="vcycle",
    )(load.reshape(rows, nx), density.reshape(nz * ny, nx), moduli, fixed.reshape(nz * ny, nx))
    shape = (3, nz, ny, nx)
    return u.reshape(shape), r.reshape(shape)


def solution(mesh):
    ns, nc = mesh.shape["slab"], mesh.shape["col"]
    placed = (P(None, "slab", "col", None), P("slab", "col", None), P(), P("slab", "col", None))

    def body(load, density, moduli, fixed):
        return on_device(ns, nc, load, density, moduli, fixed)

    return jax.shard_map(
        body,
        mesh=mesh,
        in_specs=placed,
        out_specs=(P(None, "slab", "col", None), P(None, "slab", "col", None)),
        check_vma=False,
    )
```

```python
import jax
import jax.numpy as jnp
from jax import lax
from jax.experimental import pallas as pl
from jax.experimental.pallas import tpu as pltpu
from jax.sharding import PartitionSpec as P

OMEGA = 0.6
COUPLE = 0.05
CLASSES = 8
COARSE_SWEEPS = 8
LANES = 128
F32 = jnp.float32
DIRS = ((0, 1), (0, -1), (1, 0), (-1, 0), (1, 1), (1, -1), (-1, 1), (-1, -1))


class Grid:
    def __init__(self, nz, ny, oz, oy):
        self.nz, self.ny, self.oz, self.oy = nz, ny, oz, oy
        self.z, self.y = nz + 2 * oz, ny + 2 * oy
        self.rows = self.z * self.y

    def row(self, comp, z, y):
        return comp * self.rows + (z + self.oz) * self.y + y + self.oy

    def plane(self, comp, z):
        start = comp * self.rows + z * self.y
        if not isinstance(start, int):
            start = pl.multiple_of(start, 8)
        return pl.ds(start, self.y)


def segments(grid, dz, dy, depth):
    nz, ny = grid.nz, grid.ny

    def cell(step, d, n):
        return (n - step, -step) if d > 0 else (step - 1, n - 1 + step)

    out = []
    if dz == 0:
        for i in range(1, depth + 1):
            mine, there = cell(i, dy, ny)
            out.append((0, mine, 0, there, nz, True))
    elif dy == 0:
        for i in range(1, depth + 1):
            mine, there = cell(i, dz, nz)
            out.append((mine, 0, there, 0, ny, False))
    else:
        for i in range(1, depth):
            for j in range(1, depth + 1 - i):
                mz, tz = cell(i, dz, nz)
                my, ty = cell(j, dy, ny)
                out.append((mz, my, tz, ty, 1, False))
    return out


def message(grid, dz, dy, fields):
    out, at = [], 0
    for field, (comps, depth) in enumerate(fields):
        for comp in range(comps):
            for seg in segments(grid, dz, dy, depth):
                out.append((field, comp, seg, at))
                at += seg[4]
    return out, -(-at // 8) * 8


def window(grid, comp, z, y, count, along_z):
    start = grid.row(comp, z, y)
    if along_z:
        return pl.ds(start, count, stride=grid.y)
    return pl.ds(start, count)


class Exchange:
    def __init__(self, grid, fields, where, send, recv, ssem, rsem):
        self.grid, self.fields, self.where = grid, fields, where
        self.send, self.recv, self.ssem, self.rsem = send, recv, ssem, rsem

    def copy(self, d):
        dz, dy = DIRS[d]
        s, c, ns, nc = self.where
        target = (lax.rem(s + dz + ns, ns), lax.rem(c + dy + nc, nc))
        return pltpu.make_async_remote_copy(
            src_ref=self.send[d], dst_ref=self.recv[d], send_sem=self.ssem.at[d], recv_sem=self.rsem.at[d],
            device_id=target, device_id_type=pl.DeviceIdType.MESH)

    def exists(self, dz, dy):
        s, c, ns, nc = self.where
        ok = None
        for here, d, n in ((s, dz, ns), (c, dy, nc)):
            if d:
                near = here < n - 1 if d > 0 else here > 0
                ok = near if ok is None else jnp.logical_and(ok, near)
        return ok

    def start(self, refs):
        for d, (dz, dy) in enumerate(DIRS):
            rows, _ = message(self.grid, dz, dy, self.fields)

            @pl.when(self.exists(dz, dy))
            def _():
                for field, comp, (z, y, _, _, count, along), at in rows:
                    self.send[d][pl.ds(at, count), :] = refs[field][window(self.grid, comp, z, y, count, along), :]
                self.copy(d).start()

    def finish(self, refs):
        for d, (dz, dy) in enumerate(DIRS):
            rows, _ = message(self.grid, dz, dy, self.fields)

            @pl.when(self.exists(-dz, -dy))
            def _():
                self.copy(d).wait_recv()
                for field, comp, (_, _, z, y, count, along), at in rows:
                    refs[field][window(self.grid, comp, z, y, count, along), :] = self.recv[d][pl.ds(at, count), :]

    def drain(self):
        for d, (dz, dy) in enumerate(DIRS):
            @pl.when(self.exists(dz, dy))
            def _():
                self.copy(d).wait_send()


def lane_iota(rows):
    return lax.broadcasted_iota(jnp.int32, (rows, LANES), 1)


def right(v, step):
    return pltpu.roll(v, step % LANES, 1)


def left(v, step):
    return pltpu.roll(v, LANES - step, 1)


def down(v):
    return pltpu.roll(v, 1, 0)


def up(v):
    return pltpu.roll(v, v.shape[0] - 1, 0)


def pair_sum(v, step):
    lane = lane_iota(v.shape[0])
    first = lane % (2 * step) < step
    return v + jnp.where(first, left(v, step), right(v, step))


def rows_of(start, count):
    if not isinstance(start, int):
        start = pl.multiple_of(start, 8)
    return pl.ds(start, count)


class Level:
    def __init__(self, scale, xs, zs, group, ny, closed, plane, k, coef, size):
        self.scale, self.xs, self.zs, self.group, self.ny, self.closed = scale, xs, zs, group, ny, closed
        self.plane, self.k, self.coef, self.size = plane, k, coef, size

    def at(self, which, z):
        p = self.plane(0, z)
        return self.coef[which][p, :]

    def z_sides(self, get, z):
        after, before = get(z + 1), get(z - 1)
        if not self.group:
            return after, before
        here = get(z)
        lane = lane_iota(self.ny) % self.group
        turn = self.group - self.zs
        return (jnp.where(lane < turn, left(here, self.zs), right(after, turn)),
                jnp.where(lane >= self.zs, right(here, self.zs), left(before, turn)))

    def setup(self, low, high, mask):
        def body(z, carry):
            get = lambda i: self.k[self.plane(0, i), :]
            k = get(z)
            lane = lane_iota(self.ny)
            zp, zm = self.z_sides(get, z)
            inx = lane < LANES - self.xs
            inm = lane >= self.xs
            xp = jnp.where(inx, left(k, self.xs), 0.0)
            xm = jnp.where(inm, right(k, self.xs), 0.0)
            yp, ym = up(k), down(k)
            half = F32(0.5 * self.scale)
            if self.closed:
                row = lax.broadcasted_iota(jnp.int32, (self.ny, LANES), 0)
                iny, inw = row < self.ny - 1, row >= 1
                yp, ym = jnp.where(iny, yp, 0.0), jnp.where(inw, ym, 0.0)
            kzp, kzm = half * (k + zp), half * (k + zm)
            kyp, kym = half * (k + yp), half * (k + ym)
            kxp, kxm = half * (k + xp), half * (k + xm)
            total = kzp + kzm + kyp + kym + kxp + kxm
            if self.closed:
                kyp, kym = jnp.where(iny, kyp, 0.0), jnp.where(inw, kym, 0.0)
            kxp, kxm = jnp.where(inx, kxp, 0.0), jnp.where(inm, kxm, 0.0)
            inside = k > 0.0
            diag = jnp.where(inside, total + F32(2.0 * COUPLE) * k, 1.0)
            weight = jnp.where(inside, F32(OMEGA) / diag, 0.0)
            p = self.plane(0, z)
            if mask is not None:
                weight = weight * mask[p, :]
            for which, value in enumerate((kzp, kzm, kyp, kym, kxp, kxm, total + F32(COUPLE) * k, weight)):
                self.coef[which][p, :] = value
            return carry

        lax.fori_loop(low, high, body, 0)

    def first(self, low, high, rhs, out):
        def body(z, carry):
            weight = self.at(7, z)
            for c in range(3):
                p = self.plane(c, z)
                out[p, :] = weight * rhs[p, :]
            return carry

        lax.fori_loop(low, high, body, 0)

    def defect(self, z, u, rhs):
        kzp, kzm, kyp, kym, kxp, kxm, own = [self.at(i, z) for i in range(7)]
        couple = F32(COUPLE) * self.k[self.plane(0, z), :]
        field = [u[self.plane(c, z), :] for c in range(3)]
        shared = couple * (field[0] + field[1] + field[2])
        out = []
        for c in range(3):
            v = field[c]
            zp, zm = self.z_sides(lambda i: u[self.plane(c, i), :], z)
            near = (kzp * zp + kzm * zm) + (kyp * up(v) + kym * down(v))
            near = near + (kxp * left(v, self.xs) + kxm * right(v, self.xs))
            out.append((rhs[self.plane(c, z), :] - shared) + (near - own * v))
        return field, out

    def sweep(self, low, high, u, rhs, out, out_plane=None):
        place = out_plane or self.plane

        def body(z, carry):
            field, out_d = self.defect(z, u, rhs)
            weight = self.at(7, z)
            for c in range(3):
                out[place(c, z), :] = field[c] + weight * out_d[c]
            return carry

        lax.fori_loop(low, high, body, 0)

    def residual(self, low, high, u, rhs, mask, out):
        def body(z, carry):
            _, out_d = self.defect(z, u, rhs)
            for c in range(3):
                value = out_d[c]
                if mask is not None:
                    value = mask[self.plane(0, z), :] * value
                out(c, z, value)
            return carry

        lax.fori_loop(low, high, body, 0)


def kernel(ns, nc, g0, g1, ex, load, dens, moduli, fixed, out_u, out_r, *scratch):
    it = iter(scratch)
    take = lambda n: [next(it) for _ in range(n)]
    k0, m0, b0, ua, ub = take(5)
    c0 = take(8)
    k1, b1, va, vb = take(4)
    c1 = take(8)
    k2, b2, wa, wb, wf = take(5)
    c2 = take(8)
    k3, b3, xa, xb = take(4)
    c3 = take(8)
    pack, gather, stage = take(3)
    s, c = lax.axis_index("slab"), lax.axis_index("col")
    where = (s, c, ns, nc)
    rounds = []
    for grid, fields in ex:
        send, recv = take(8), take(8)
        ssem, rsem = take(2)
        rounds.append(Exchange(grid, fields, where, send, recv, ssem, rsem))
    gsend, grecv = take(2)
    ex_a, ex_k, ex_b, ex_u, ex_v = rounds
    n0, y0, n1, y1 = g0.nz, g0.ny, g1.nz, g1.ny

    def zero(ref):
        rows = ref.shape[0]
        ref[...] = jnp.zeros((rows, LANES), F32)

    barrier = pltpu.get_barrier_semaphore()

    def greet(t, carry):
        target = (lax.rem(s + t // nc, ns), lax.rem(c + t % nc, nc))
        pl.semaphore_signal(barrier, inc=1, device_id=target, device_id_type=pl.DeviceIdType.MESH)
        return carry

    lax.fori_loop(1, ns * nc, greet, 0)

    for ref in (k0, m0, b0, k1):
        zero(ref)

    def fill(z, carry):
        src = pl.ds(pl.multiple_of(z * y0, 8), y0)
        d = dens[src, :]
        value = jnp.zeros((y0, LANES), F32)
        for klass in range(CLASSES):
            value = jnp.where(d == klass, moduli[klass], value)
        keep = 1.0 - fixed[src, :].astype(F32)
        wide = lambda v: jnp.concatenate(
            [jnp.zeros((g0.oy, LANES), F32), v, jnp.zeros((g0.oy, LANES), F32)], axis=0)
        k0[g0.plane(0, z + g0.oz), :] = wide(value)
        m0[g0.plane(0, z + g0.oz), :] = wide(keep)
        for comp in range(3):
            at = pl.ds(pl.multiple_of((comp * n0 + z) * y0, 8), y0)
            b0[g0.plane(comp, z + g0.oz), :] = wide(load[at, :])
        return carry

    lax.fori_loop(0, n0, fill, 0)
    pl.semaphore_wait(barrier, ns * nc - 1)
    ex_a.start([k0, m0, b0])

    def coarser(src, grid, comp, z, y, count, steps):
        total = None
        for dz in range(2):
            for dy in range(2):
                part = src[pl.ds(grid.row(comp, 2 * z + dz, 2 * y + dy), count, stride=2), :]
                total = part if total is None else total + part
        for step in steps:
            total = pair_sum(total, step)
        return total * F32(0.125)

    for z in range(n1):
        k1[pl.ds(g1.row(0, z, 0), y1), :] = coarser(k0, g0, 0, z, 0, y1, (1,))
    ex_k.start([k1])

    lane4 = lane_iota(4) % 4

    def packed(src, comp, slot):
        value = jnp.zeros((4, LANES), F32)
        for z in range(n1 // 2):
            value = jnp.where(lane4 == z, coarser(src, g1, comp, z, 0, y1 // 2, (2,)), value)
        pack[pl.ds(4 * slot, 4), :] = value

    packed(k1, 0, 3)
    for ref in (ua, ub, b1, va, vb):
        zero(ref)

    level0 = Level(1.0, 1, 0, 0, g0.y, False, g0.plane, k0, c0, g0.z)
    level1 = Level(0.25, 2, 0, 0, g1.y, False, g1.plane, k1, c1, g1.z)
    y2, y3 = 4 * nc, 2 * nc
    plane2 = lambda comp, z: rows_of((comp * (ns + 2) + z) * y2, y2)
    plane3 = lambda comp, z: rows_of((comp * (ns + 2) + z) * y3, y3)
    wide2 = lambda comp, z: rows_of((comp * (ns + 2) + z) * (y2 + 16) + 8, y2)
    level2 = Level(0.25**2, 4, 1, 4, y2, True, plane2, k2, c2, ns)
    level3 = Level(0.25**3, 8, 2, 4, y3, True, plane3, k3, c3, ns)
    for ref, comps, plane, rows in ((k2, 1, plane2, y2), (wa, 3, plane2, y2), (wb, 3, plane2, y2),
                                    (k3, 1, plane3, y3), (xa, 3, plane3, y3), (xb, 3, plane3, y3),
                                    (wf, 3, lambda comp, z: rows_of((comp * (ns + 2) + z) * (y2 + 16), y2 + 16), y2 + 16)):
        for comp in range(comps):
            for z in (0, ns + 1):
                ref[plane(comp, z), :] = jnp.zeros((rows, LANES), F32)

    ex_a.finish([k0, m0, b0])
    level0.setup(g0.oz - 2, g0.oz + n0 + 2, m0)
    level0.first(g0.oz - 2, g0.oz + n0 + 2, b0, ua)
    level0.sweep(g0.oz - 1, g0.oz + n0 + 1, ua, b0, ub)

    def keep0(comp, z, value):
        ua[g0.plane(comp, z), :] = value

    level0.residual(g0.oz, g0.oz + n0, ub, b0, m0, keep0)
    for comp in range(3):
        for z in range(n1):
            b1[pl.ds(g1.row(comp, z, 0), y1), :] = coarser(ua, g0, comp, z, 0, y1, (1,))
    ex_b.start([b1])

    ex_k.finish([k1])
    level1.setup(g1.oz - 3, g1.oz + n1 + 3, None)
    ex_b.finish([b1])
    level1.first(g1.oz - 2, g1.oz + n1 + 2, b1, va)
    level1.sweep(g1.oz - 1, g1.oz + n1 + 1, va, b1, vb)

    def keep1(comp, z, value):
        va[g1.plane(comp, z), :] = value

    level1.residual(g1.oz, g1.oz + n1, vb, b1, None, keep1)
    for comp in range(3):
        packed(va, comp, comp)

    here = pl.ds(pl.multiple_of((s * nc + c) * 16, 16), 16)
    gather[here, :] = pack[...]

    def spread(t):
        target = (lax.rem(s + t // nc, ns), lax.rem(c + t % nc, nc))
        return pltpu.make_async_remote_copy(
            src_ref=gather.at[here], dst_ref=gather.at[here], send_sem=gsend, recv_sem=grecv,
            device_id=target, device_id_type=pl.DeviceIdType.MESH)

    def start_one(t, carry):
        spread(t).start()
        return carry

    lax.fori_loop(1, ns * nc, start_one, 0)
    all_others = pl.ds(0, (ns * nc - 1) * 16)
    everything = pltpu.make_async_remote_copy(
        src_ref=gather.at[all_others], dst_ref=gather.at[all_others], send_sem=gsend, recv_sem=grecv,
        device_id=(lax.rem(s + 1, ns), c), device_id_type=pl.DeviceIdType.MESH)
    everything.wait_recv()
    ex_v.start([vb])
    ex_u.start([ub, m0])

    def assemble(t, carry):
        z, pair = t // (nc // 2), t % (nc // 2)
        first = gather[pl.ds(pl.multiple_of(t * 32, 32), 16), :]
        second = gather[pl.ds(pl.multiple_of(t * 32 + 16, 16), 16), :]
        for f in range(4):
            value = jnp.concatenate([first[4 * f:4 * f + 4], second[4 * f:4 * f + 4]], axis=0)
            ref, comp = (k2, 0) if f == 3 else (b2, f)
            ref[pl.ds(pl.multiple_of((comp * (ns + 2) + z + 1) * y2 + pair * 8, 8), 8), :] = value
        return carry

    lax.fori_loop(0, ns * nc // 2, assemble, 0)
    level2.setup(1, ns + 1, None)
    level2.first(1, ns + 1, b2, wa)
    level2.sweep(1, ns + 1, wa, b2, wb)

    def keep2(comp, z, value):
        wa[plane2(comp, z), :] = value

    level2.residual(1, ns + 1, wb, b2, None, keep2)

    def shrink3(z, carry):
        for src, dst, comp in ((k2, k3, 0), (wa, b3, 0), (wa, b3, 1), (wa, b3, 2)):
            start = (comp * (ns + 2) + z) * y2
            total = src[pl.ds(start, y3, stride=2), :] + src[pl.ds(start + 1, y3, stride=2), :]
            dst[plane3(comp, z), :] = pair_sum(pair_sum(total, 1), 4) * F32(0.125)
        return carry

    lax.fori_loop(1, ns + 1, shrink3, 0)
    level3.setup(1, ns + 1, None)
    level3.first(1, ns + 1, b3, xa)
    old, new = xa, xb
    for turn in range(COARSE_SWEEPS - 1):
        level3.sweep(1, ns + 1, old, b3, new)
        old, new = new, old
    coarse = old

    def add2(z, carry):
        for comp in range(3):
            value = coarse[plane3(comp, z), :]
            stage[pl.ds(0, y3, stride=2), :] = value
            stage[pl.ds(1, y3, stride=2), :] = value
            p = plane2(comp, z)
            wb[p, :] = wb[p, :] + stage[pl.ds(0, y2), :]
        return carry

    lax.fori_loop(1, ns + 1, add2, 0)

    def clear(ref):
        for comp in range(3):
            for z in (0, ns + 1):
                ref[plane2(comp, z), :] = jnp.zeros((y2, LANES), F32)

    clear(wa)
    level2.sweep(1, ns + 1, wb, b2, wa)
    level2.sweep(1, ns + 1, wa, b2, wf, wide2)

    ex_v.finish([vb])
    lane8 = lane_iota(8)
    odd = c % 2 == 1

    def add1(i, carry):
        z2 = i + 4 * s + 2
        block, j = z2 // 4, z2 % 4
        for comp in range(3):
            at = (comp * (ns + 2) + block) * (y2 + 16) + (c // 2) * 8
            rows = wf[pl.ds(pl.multiple_of(at, 8), 24), :]
            value = jnp.where(odd, rows[10:18], rows[6:14])
            lane = lane8 % 4
            value = jnp.where(lane == j, value, 0.0)
            value = pair_sum(pair_sum(value, 1), 2)
            stage[pl.ds(0, 8, stride=2), :] = value
            stage[pl.ds(1, 8, stride=2), :] = value
            grown = stage[pl.ds(0, 16), :]
            for dz in range(2):
                p = g1.plane(comp, 2 * i + dz)
                inside = k1[g1.plane(0, 2 * i + dz), :] > 0.0
                va[p, :] = vb[p, :] + jnp.where(inside, grown, 0.0)
        return carry

    lax.fori_loop(0, g1.z // 2, add1, 0)
    level1.sweep(g1.oz - 3, g1.oz + n1 + 3, va, b1, vb)
    level1.sweep(g1.oz - 2, g1.oz + n1 + 2, vb, b1, va)

    ex_u.finish([ub, m0])

    def add0(z, carry):
        for comp in range(3):
            near = (z - g0.oz + 2 * g1.oz) // 2
            value = va[g1.plane(comp, near), :][2:14]
            stage[pl.ds(0, 12, stride=2), :] = value
            stage[pl.ds(1, 12, stride=2), :] = value
            p = g0.plane(comp, z)
            ua[p, :] = ub[p, :] + m0[g0.plane(0, z), :] * stage[pl.ds(0, g0.y), :]
        return carry

    lax.fori_loop(0, g0.z, add0, 0)
    level0.sweep(g0.oz - 2, g0.oz + n0 + 2, ua, b0, ub)
    level0.sweep(g0.oz - 1, g0.oz + n0 + 1, ub, b0, ua)

    def emit(comp, z, value):
        at = pl.ds(pl.multiple_of((comp * n0 + z - g0.oz) * y0, 8), y0)
        out_r[at, :] = value[g0.oy:g0.oy + y0]
        out_u[at, :] = ua[g0.plane(comp, z), :][g0.oy:g0.oy + y0]

    level0.residual(g0.oz, g0.oz + n0, ua, b0, m0, emit)

    everything.wait_send()
    for ex_one in rounds:
        ex_one.drain()


def on_device(ns, nc, load, density, moduli, fixed):
    _, nz, ny, nx = load.shape
    g0 = Grid(nz, ny, 3, 4)
    g1 = Grid(nz // 2, ny // 2, 4, 4)
    ex = (
        (g0, ((1, 3), (1, 2), (3, 2))),
        (g1, ((1, 4),)),
        (g1, ((3, 3),)),
        (g0, ((3, 3), (1, 3))),
        (g1, ((3, 4),)),
    )
    buf = lambda rows: pltpu.VMEM((rows, LANES), F32)
    y2, y3 = 4 * nc, 2 * nc
    s2, s3 = (ns + 2) * y2, (ns + 2) * y3
    scratch = [buf(g0.rows)] * 2 + [buf(3 * g0.rows)] * 3 + [buf(g0.rows)] * 8
    scratch += [buf(g1.rows)] + [buf(3 * g1.rows)] * 3 + [buf(g1.rows)] * 8
    scratch += [buf(s2)] + [buf(3 * s2)] * 3 + [buf(3 * (ns + 2) * (y2 + 16))] + [buf(s2)] * 8
    scratch += [buf(s3)] + [buf(3 * s3)] * 3 + [buf(s3)] * 8
    scratch += [buf(16), buf(ns * nc * 16), buf(max(y2, 32))]
    for grid, fields in ex:
        sizes = [message(grid, dz, dy, fields)[1] for dz, dy in DIRS]
        scratch += [buf(n) for n in sizes] * 2
        scratch += [pltpu.SemaphoreType.DMA((8,))] * 2
    scratch += [pltpu.SemaphoreType.DMA] * 2

    def run(*args):
        kernel(ns, nc, g0, g1, ex, *args)

    rows = 3 * nz * ny
    vmem = pl.BlockSpec(memory_space=pltpu.VMEM)
    u, r = pl.pallas_call(
        run,
        out_shape=[jax.ShapeDtypeStruct((rows, nx), F32)] * 2,
        in_specs=[vmem, vmem, pl.BlockSpec(memory_space=pltpu.SMEM), vmem],
        out_specs=[vmem, vmem],
        scratch_shapes=scratch,
        compiler_params=pltpu.CompilerParams(collective_id=0, has_side_effects=True, vmem_limit_bytes=56 * 1024 * 1024),
        name="vcycle",
    )(load.reshape(rows, nx), density.reshape(nz * ny, nx), moduli, fixed.reshape(nz * ny, nx))
    shape = (3, nz, ny, nx)
    return u.reshape(shape), r.reshape(shape)


def solution(mesh):
    ns, nc = mesh.shape["slab"], mesh.shape["col"]
    placed = (P(None, "slab", "col", None), P("slab", "col", None), P(), P("slab", "col", None))

    def body(load, density, moduli, fixed):
        return on_device(ns, nc, load, density, moduli, fixed)

    return jax.shard_map(
        body,
        mesh=mesh,
        in_specs=placed,
        out_specs=(P(None, "slab", "col", None), P(None, "slab", "col", None)),
        check_vma=False,
    )
```

```python
import jax
import jax.numpy as jnp
from jax import lax
from jax.experimental import pallas as pl
from jax.experimental.pallas import tpu as pltpu
from jax.sharding import PartitionSpec as P

OMEGA = 0.6
COUPLE = 0.05
CLASSES = 8
COARSE_SWEEPS = 8
LANES = 128
F32 = jnp.float32
LIVE = 27
DIRS = ((0, 1), (0, -1), (1, 0), (-1, 0), (1, 1), (1, -1), (-1, 1), (-1, -1))


class Grid:
    def __init__(self, nz, ny, oz, oy):
        self.nz, self.ny, self.oz, self.oy = nz, ny, oz, oy
        self.z, self.y = nz + 2 * oz, ny + 2 * oy
        self.rows = self.z * self.y

    def row(self, comp, z, y):
        return comp * self.rows + (z + self.oz) * self.y + y + self.oy

    def plane(self, comp, z):
        start = comp * self.rows + z * self.y
        if not isinstance(start, int):
            start = pl.multiple_of(start, 8)
        return pl.ds(start, self.y)


def segments(grid, dz, dy, depth):
    nz, ny = grid.nz, grid.ny

    def cell(step, d, n):
        return (n - step, -step) if d > 0 else (step - 1, n - 1 + step)

    out = []
    if dz == 0:
        for i in range(1, depth + 1):
            mine, there = cell(i, dy, ny)
            out.append((0, mine, 0, there, nz, True))
    elif dy == 0:
        for i in range(1, depth + 1):
            mine, there = cell(i, dz, nz)
            out.append((mine, 0, there, 0, ny, False))
    else:
        for i in range(1, depth):
            for j in range(1, depth + 1 - i):
                mz, tz = cell(i, dz, nz)
                my, ty = cell(j, dy, ny)
                out.append((mz, my, tz, ty, 1, False))
    return out


def message(grid, dz, dy, fields):
    out, at = [], 0
    for field, (comps, depth) in enumerate(fields):
        for comp in range(comps):
            for seg in segments(grid, dz, dy, depth):
                out.append((field, comp, seg, at))
                at += seg[4]
    return out, -(-at // 8) * 8


def window(grid, comp, z, y, count, along_z):
    start = grid.row(comp, z, y)
    if along_z:
        return pl.ds(start, count, stride=grid.y)
    return pl.ds(start, count)


class Exchange:
    def __init__(self, grid, fields, where, send, recv, ssem, rsem):
        self.grid, self.fields, self.where = grid, fields, where
        self.send, self.recv, self.ssem, self.rsem = send, recv, ssem, rsem

    def copy(self, d):
        dz, dy = DIRS[d]
        s, c, ns, nc = self.where
        target = (lax.rem(s + dz + ns, ns), lax.rem(c + dy + nc, nc))
        return pltpu.make_async_remote_copy(
            src_ref=self.send[d], dst_ref=self.recv[d], send_sem=self.ssem.at[d], recv_sem=self.rsem.at[d],
            device_id=target, device_id_type=pl.DeviceIdType.MESH)

    def exists(self, dz, dy):
        s, c, ns, nc = self.where
        ok = None
        for here, d, n in ((s, dz, ns), (c, dy, nc)):
            if d:
                near = here < n - 1 if d > 0 else here > 0
                ok = near if ok is None else jnp.logical_and(ok, near)
        return ok

    def start(self, refs):
        for d, (dz, dy) in enumerate(DIRS):
            rows, _ = message(self.grid, dz, dy, self.fields)

            @pl.when(self.exists(dz, dy))
            def _():
                for field, comp, (z, y, _, _, count, along), at in rows:
                    self.send[d][pl.ds(at, count), :] = refs[field][window(self.grid, comp, z, y, count, along), :]
                self.copy(d).start()

    def finish(self, refs):
        for d, (dz, dy) in enumerate(DIRS):
            rows, _ = message(self.grid, dz, dy, self.fields)

            @pl.when(self.exists(-dz, -dy))
            def _():
                self.copy(d).wait_recv()
                for field, comp, (_, _, z, y, count, along), at in rows:
                    refs[field][window(self.grid, comp, z, y, count, along), :] = self.recv[d][pl.ds(at, count), :]

    def drain(self):
        for d, (dz, dy) in enumerate(DIRS):
            @pl.when(self.exists(dz, dy))
            def _():
                self.copy(d).wait_send()


def lane_iota(rows):
    return lax.broadcasted_iota(jnp.int32, (rows, LANES), 1)


def right(v, step):
    return pltpu.roll(v, step % LANES, 1)


def left(v, step):
    return pltpu.roll(v, LANES - step, 1)


def down(v):
    return pltpu.roll(v, 1, 0)


def up(v):
    return pltpu.roll(v, v.shape[0] - 1, 0)


def pair_sum(v, step):
    lane = lane_iota(v.shape[0])
    first = lane % (2 * step) < step
    return v + jnp.where(first, left(v, step), right(v, step))


def rows_of(start, count):
    if not isinstance(start, int):
        start = pl.multiple_of(start, 8)
    return pl.ds(start, count)


def loop(low, high, rows, plane, body):
    count = high - low
    unit = max(u for u in range(1, count + 1) if count % u == 0 and (u == 1 or 3 * u * rows <= 8 * LIVE))

    def step(i, carry):
        base = low + i * unit
        held, todo = {}, []

        def get(ref, comp, off):
            key = (id(ref), comp, off)
            if key not in held:
                held[key] = ref[plane(comp, base + off), :]
            return held[key]

        for j in range(unit):
            todo += body(lambda ref, comp, off, j=j: get(ref, comp, off + j), base + j)
        for ref, at, value in todo:
            ref[at, :] = value
        return carry

    if count == unit:
        step(0, 0)
    else:
        lax.fori_loop(0, count // unit, step, 0)


class Level:
    def __init__(self, scale, xs, zs, group, ny, closed, plane, k, coef):
        self.scale, self.xs, self.zs, self.group, self.ny, self.closed = scale, xs, zs, group, ny, closed
        self.plane, self.k, self.coef = plane, k, coef

    def loop(self, low, high, body):
        loop(low, high, self.ny, self.plane, body)

    def z_sides(self, get):
        after, before = get(1), get(-1)
        if not self.group:
            return after, before
        here = get(0)
        lane = lane_iota(self.ny) % self.group
        turn = self.group - self.zs
        return (jnp.where(lane < turn, left(here, self.zs), right(after, turn)),
                jnp.where(lane >= self.zs, right(here, self.zs), left(before, turn)))

    def setup(self, low, high, mask, rhs, out):
        def body(get, z):
            k = get(self.k, 0, 0)
            lane = lane_iota(self.ny)
            zp, zm = self.z_sides(lambda off: get(self.k, 0, off))
            inx = lane < LANES - self.xs
            inm = lane >= self.xs
            xp = jnp.where(inx, left(k, self.xs), 0.0)
            xm = jnp.where(inm, right(k, self.xs), 0.0)
            yp, ym = up(k), down(k)
            half = F32(0.5 * self.scale)
            if self.closed:
                row = lax.broadcasted_iota(jnp.int32, (self.ny, LANES), 0)
                iny, inw = row < self.ny - 1, row >= 1
                yp, ym = jnp.where(iny, yp, 0.0), jnp.where(inw, ym, 0.0)
            kzp, kzm = half * (k + zp), half * (k + zm)
            kyp, kym = half * (k + yp), half * (k + ym)
            kxp, kxm = half * (k + xp), half * (k + xm)
            total = kzp + kzm + kyp + kym + kxp + kxm
            if self.closed:
                kyp, kym = jnp.where(iny, kyp, 0.0), jnp.where(inw, kym, 0.0)
            kxp, kxm = jnp.where(inx, kxp, 0.0), jnp.where(inm, kxm, 0.0)
            inside = k > 0.0
            diag = jnp.where(inside, total + F32(2.0 * COUPLE) * k, 1.0)
            weight = jnp.where(inside, F32(OMEGA) / diag, 0.0)
            if mask is not None:
                weight = weight * get(mask, 0, 0)
            p = self.plane(0, z)
            todo = [(self.coef[i], p, value) for i, value in
                    enumerate((kzp, kzm, kyp, kym, kxp, kxm, total + F32(COUPLE) * k, weight))]
            if rhs is not None:
                todo += [(out, self.plane(c, z), weight * get(rhs, c, 0)) for c in range(3)]
            return todo

        self.loop(low, high, body)

    def first(self, low, high, rhs, out):
        self.loop(low, high, lambda get, z: [
            (out, self.plane(c, z), get(self.coef[7], 0, 0) * get(rhs, c, 0)) for c in range(3)])

    def defect(self, get, u, rhs):
        kzp, kzm, kyp, kym, kxp, kxm, own = [get(self.coef[i], 0, 0) for i in range(7)]
        couple = F32(COUPLE) * get(self.k, 0, 0)
        field = [get(u, c, 0) for c in range(3)]
        shared = couple * (field[0] + field[1] + field[2])
        out = []
        for c in range(3):
            v = field[c]
            zp, zm = self.z_sides(lambda off: get(u, c, off))
            near = (kzp * zp + kzm * zm) + (kyp * up(v) + kym * down(v))
            near = near + (kxp * left(v, self.xs) + kxm * right(v, self.xs))
            out.append((get(rhs, c, 0) - shared) + (near - own * v))
        return field, out

    def sweep(self, low, high, u, rhs, out, out_plane=None):
        place = out_plane or self.plane

        def body(get, z):
            field, delta = self.defect(get, u, rhs)
            weight = get(self.coef[7], 0, 0)
            return [(out, place(c, z), field[c] + weight * delta[c]) for c in range(3)]

        self.loop(low, high, body)

    def residual(self, low, high, u, rhs, mask, emit):
        def body(get, z):
            field, delta = self.defect(get, u, rhs)
            todo = []
            for c in range(3):
                value = delta[c] if mask is None else get(mask, 0, 0) * delta[c]
                todo += emit(c, z, value, field[c])
            return todo

        self.loop(low, high, body)


def kernel(ns, nc, g0, g1, ex, load, dens, moduli, fixed, out_u, out_r, *scratch):
    it = iter(scratch)
    take = lambda n: [next(it) for _ in range(n)]
    k0, m0, b0, ua, ub = take(5)
    c0 = take(8)
    k1, b1, va, vb = take(4)
    c1 = take(8)
    k2, b2, wa, wb, wf = take(5)
    c2 = take(8)
    k3, b3, xa, xb = take(4)
    c3 = take(8)
    pack, gather, stage = take(3)
    s, c = lax.axis_index("slab"), lax.axis_index("col")
    where = (s, c, ns, nc)
    rounds = []
    for grid, fields in ex:
        send, recv = take(8), take(8)
        ssem, rsem = take(2)
        rounds.append(Exchange(grid, fields, where, send, recv, ssem, rsem))
    gsend, grecv = take(2)
    ex_a, ex_k, ex_b, ex_u, ex_v = rounds
    n0, y0, n1, y1 = g0.nz, g0.ny, g1.nz, g1.ny

    def zero(ref):
        rows = ref.shape[0]
        ref[...] = jnp.zeros((rows, LANES), F32)

    barrier = pltpu.get_barrier_semaphore()

    def greet(t, carry):
        target = (lax.rem(s + t // nc, ns), lax.rem(c + t % nc, nc))
        pl.semaphore_signal(barrier, inc=1, device_id=target, device_id_type=pl.DeviceIdType.MESH)
        return carry

    lax.fori_loop(1, ns * nc, greet, 0)

    for ref in (k0, m0, b0, k1):
        zero(ref)

    def fill(get, z):
        d = get(dens, 0, 0)
        value = jnp.zeros((y0, LANES), F32)
        for klass in range(CLASSES):
            value = jnp.where(d == klass, moduli[klass], value)
        keep = 1.0 - get(fixed, 0, 0).astype(F32)
        wide = lambda v: jnp.concatenate(
            [jnp.zeros((g0.oy, LANES), F32), v, jnp.zeros((g0.oy, LANES), F32)], axis=0)
        p = g0.plane(0, z + g0.oz)
        return [(k0, p, wide(value)), (m0, p, wide(keep))] + [
            (b0, g0.plane(comp, z + g0.oz), wide(get(load, comp, 0))) for comp in range(3)]

    loop(0, n0, y0, lambda comp, z: rows_of((comp * n0 + z) * y0, y0), fill)
    pl.semaphore_wait(barrier, ns * nc - 1)
    ex_a.start([k0, m0, b0])

    def coarser(src, grid, comp, z, y, count, steps):
        total = None
        for dz in range(2):
            for dy in range(2):
                part = src[pl.ds(grid.row(comp, 2 * z + dz, 2 * y + dy), count, stride=2), :]
                total = part if total is None else total + part
        for step in steps:
            total = pair_sum(total, step)
        return total * F32(0.125)

    for z in range(n1):
        k1[pl.ds(g1.row(0, z, 0), y1), :] = coarser(k0, g0, 0, z, 0, y1, (1,))
    ex_k.start([k1])

    lane4 = lane_iota(4) % 4

    def packed(src, comp, slot):
        value = jnp.zeros((4, LANES), F32)
        for z in range(n1 // 2):
            value = jnp.where(lane4 == z, coarser(src, g1, comp, z, 0, y1 // 2, (2,)), value)
        pack[pl.ds(4 * slot, 4), :] = value

    packed(k1, 0, 3)
    for ref in (ua, ub, b1, va, vb):
        zero(ref)

    level0 = Level(1.0, 1, 0, 0, g0.y, False, g0.plane, k0, c0)
    level1 = Level(0.25, 2, 0, 0, g1.y, False, g1.plane, k1, c1)
    y2, y3 = 4 * nc, 2 * nc
    plane2 = lambda comp, z: rows_of((comp * (ns + 2) + z) * y2, y2)
    plane3 = lambda comp, z: rows_of((comp * (ns + 2) + z) * y3, y3)
    wide2 = lambda comp, z: rows_of((comp * (ns + 2) + z) * (y2 + 16) + 8, y2)
    level2 = Level(0.25**2, 4, 1, 4, y2, True, plane2, k2, c2)
    level3 = Level(0.25**3, 8, 2, 4, y3, True, plane3, k3, c3)
    for ref, comps, plane, rows in ((k2, 1, plane2, y2), (wa, 3, plane2, y2), (wb, 3, plane2, y2),
                                    (k3, 1, plane3, y3), (xa, 3, plane3, y3), (xb, 3, plane3, y3),
                                    (wf, 3, lambda comp, z: rows_of((comp * (ns + 2) + z) * (y2 + 16), y2 + 16), y2 + 16)):
        for comp in range(comps):
            for z in (0, ns + 1):
                ref[plane(comp, z), :] = jnp.zeros((rows, LANES), F32)

    ex_a.finish([k0, m0, b0])
    level0.setup(g0.oz - 2, g0.oz + n0 + 2, m0, b0, ua)
    level0.sweep(g0.oz - 1, g0.oz + n0 + 1, ua, b0, ub)

    def keep0(comp, z, value, field):
        return [(ua, g0.plane(comp, z), value)]

    level0.residual(g0.oz, g0.oz + n0, ub, b0, m0, keep0)
    for comp in range(3):
        for z in range(n1):
            b1[pl.ds(g1.row(comp, z, 0), y1), :] = coarser(ua, g0, comp, z, 0, y1, (1,))
    ex_b.start([b1])

    ex_k.finish([k1])
    level1.setup(g1.oz - 3, g1.oz + n1 + 3, None, None, None)
    ex_b.finish([b1])
    level1.first(g1.oz - 2, g1.oz + n1 + 2, b1, va)
    level1.sweep(g1.oz - 1, g1.oz + n1 + 1, va, b1, vb)

    def keep1(comp, z, value, field):
        return [(va, g1.plane(comp, z), value)]

    level1.residual(g1.oz, g1.oz + n1, vb, b1, None, keep1)
    for comp in range(3):
        packed(va, comp, comp)

    here = pl.ds(pl.multiple_of((s * nc + c) * 16, 16), 16)
    gather[here, :] = pack[...]

    def spread(t):
        target = (lax.rem(s + t // nc, ns), lax.rem(c + t % nc, nc))
        return pltpu.make_async_remote_copy(
            src_ref=gather.at[here], dst_ref=gather.at[here], send_sem=gsend, recv_sem=grecv,
            device_id=target, device_id_type=pl.DeviceIdType.MESH)

    def start_one(t, carry):
        spread(t).start()
        return carry

    lax.fori_loop(1, ns * nc, start_one, 0)
    all_others = pl.ds(0, (ns * nc - 1) * 16)
    everything = pltpu.make_async_remote_copy(
        src_ref=gather.at[all_others], dst_ref=gather.at[all_others], send_sem=gsend, recv_sem=grecv,
        device_id=(lax.rem(s + 1, ns), c), device_id_type=pl.DeviceIdType.MESH)
    everything.wait_recv()
    ex_v.start([vb])
    ex_u.start([ub, m0])

    def assemble(t, carry):
        z, pair = t // (nc // 2), t % (nc // 2)
        first = gather[pl.ds(pl.multiple_of(t * 32, 32), 16), :]
        second = gather[pl.ds(pl.multiple_of(t * 32 + 16, 16), 16), :]
        for f in range(4):
            value = jnp.concatenate([first[4 * f:4 * f + 4], second[4 * f:4 * f + 4]], axis=0)
            ref, comp = (k2, 0) if f == 3 else (b2, f)
            ref[pl.ds(pl.multiple_of((comp * (ns + 2) + z + 1) * y2 + pair * 8, 8), 8), :] = value
        return carry

    lax.fori_loop(0, ns * nc // 2, assemble, 0)
    level2.setup(1, ns + 1, None, b2, wa)
    level2.sweep(1, ns + 1, wa, b2, wb)

    def keep2(comp, z, value, field):
        return [(wa, plane2(comp, z), value)]

    level2.residual(1, ns + 1, wb, b2, None, keep2)

    def shrink3(z, carry):
        for src, dst, comp in ((k2, k3, 0), (wa, b3, 0), (wa, b3, 1), (wa, b3, 2)):
            start = (comp * (ns + 2) + z) * y2
            total = src[pl.ds(start, y3, stride=2), :] + src[pl.ds(start + 1, y3, stride=2), :]
            dst[plane3(comp, z), :] = pair_sum(pair_sum(total, 1), 4) * F32(0.125)
        return carry

    lax.fori_loop(1, ns + 1, shrink3, 0)
    level3.setup(1, ns + 1, None, b3, xa)
    old, new = xa, xb
    for turn in range(COARSE_SWEEPS - 1):
        level3.sweep(1, ns + 1, old, b3, new)
        old, new = new, old
    coarse = old

    def twice(value, slot):
        rows = value.shape[0]
        stage[pl.ds(slot, rows, stride=2), :] = value
        stage[pl.ds(slot + 1, rows, stride=2), :] = value
        return slot, 2 * rows

    def staged(spot):
        return stage[pl.ds(spot[0], spot[1]), :]

    def add2(z, carry):
        spots = [twice(coarse[plane3(comp, z), :], comp * y2) for comp in range(3)]
        for comp in range(3):
            p = plane2(comp, z)
            wb[p, :] = wb[p, :] + staged(spots[comp])
        return carry

    lax.fori_loop(1, ns + 1, add2, 0)

    level2.sweep(1, ns + 1, wb, b2, wa)
    level2.sweep(1, ns + 1, wa, b2, wf, wide2)

    ex_v.finish([vb])
    lane8 = lane_iota(8)
    odd = c % 2 == 1

    def add1(i, carry):
        z2 = i + 4 * s + 2
        block, j = z2 // 4, z2 % 4
        spots = []
        for comp in range(3):
            at = (comp * (ns + 2) + block) * (y2 + 16) + (c // 2) * 8
            rows = wf[pl.ds(pl.multiple_of(at, 8), 24), :]
            value = jnp.where(odd, rows[10:18], rows[6:14])
            value = jnp.where(lane8 % 4 == j, value, 0.0)
            spots.append(twice(pair_sum(pair_sum(value, 1), 2), comp * 16))
        for comp in range(3):
            grown = staged(spots[comp])
            for dz in range(2):
                p = g1.plane(comp, 2 * i + dz)
                inside = k1[g1.plane(0, 2 * i + dz), :] > 0.0
                va[p, :] = vb[p, :] + jnp.where(inside, grown, 0.0)
        return carry

    lax.fori_loop(0, g1.z // 2, add1, 0)
    level1.sweep(g1.oz - 3, g1.oz + n1 + 3, va, b1, vb)
    level1.sweep(g1.oz - 2, g1.oz + n1 + 2, vb, b1, va)

    ex_u.finish([ub, m0])

    def add0(i, carry):
        spots = [twice(va[g1.plane(comp, i + g1.oz - 2), :][2:14], comp * g0.y) for comp in range(3)]
        for comp in range(3):
            grown = staged(spots[comp])
            for dz in range(2):
                p = g0.plane(comp, 2 * i + dz)
                ua[p, :] = ub[p, :] + m0[g0.plane(0, 2 * i + dz), :] * grown
        return carry

    lax.fori_loop(0, g0.z // 2, add0, 0)
    level0.sweep(g0.oz - 2, g0.oz + n0 + 2, ua, b0, ub)
    level0.sweep(g0.oz - 1, g0.oz + n0 + 1, ub, b0, ua)

    def emit(comp, z, value, field):
        at = pl.ds(pl.multiple_of((comp * n0 + z - g0.oz) * y0, 8), y0)
        own = slice(g0.oy, g0.oy + y0)
        return [(out_r, at, value[own]), (out_u, at, field[own])]

    level0.residual(g0.oz, g0.oz + n0, ua, b0, m0, emit)

    everything.wait_send()
    for ex_one in rounds:
        ex_one.drain()


def on_device(ns, nc, load, density, moduli, fixed):
    _, nz, ny, nx = load.shape
    g0 = Grid(nz, ny, 4, 4)
    g1 = Grid(nz // 2, ny // 2, 4, 4)
    ex = (
        (g0, ((1, 3), (1, 2), (3, 2))),
        (g1, ((1, 4),)),
        (g1, ((3, 3),)),
        (g0, ((3, 3), (1, 3))),
        (g1, ((3, 4),)),
    )
    buf = lambda rows: pltpu.VMEM((rows, LANES), F32)
    y2, y3 = 4 * nc, 2 * nc
    s2, s3 = (ns + 2) * y2, (ns + 2) * y3
    scratch = [buf(g0.rows)] * 2 + [buf(3 * g0.rows)] * 3 + [buf(g0.rows)] * 8
    scratch += [buf(g1.rows)] + [buf(3 * g1.rows)] * 3 + [buf(g1.rows)] * 8
    scratch += [buf(s2)] + [buf(3 * s2)] * 3 + [buf(3 * (ns + 2) * (y2 + 16))] + [buf(s2)] * 8
    scratch += [buf(s3)] + [buf(3 * s3)] * 3 + [buf(s3)] * 8
    scratch += [buf(16), buf(ns * nc * 16), buf(3 * max(y2, g0.y))]
    for grid, fields in ex:
        sizes = [message(grid, dz, dy, fields)[1] for dz, dy in DIRS]
        scratch += [buf(n) for n in sizes] * 2
        scratch += [pltpu.SemaphoreType.DMA((8,))] * 2
    scratch += [pltpu.SemaphoreType.DMA] * 2

    used = sum(4 * LANES * ref.shape[0] for ref in scratch if hasattr(ref, "shape"))

    def run(*args):
        kernel(ns, nc, g0, g1, ex, *args)

    rows = 3 * nz * ny
    vmem = pl.BlockSpec(memory_space=pltpu.VMEM)
    u, r = pl.pallas_call(
        run,
        out_shape=[jax.ShapeDtypeStruct((rows, nx), F32)] * 2,
        in_specs=[vmem, vmem, pl.BlockSpec(memory_space=pltpu.SMEM), vmem],
        out_specs=[vmem, vmem],
        scratch_shapes=scratch,
        compiler_params=pltpu.CompilerParams(collective_id=0, has_side_effects=True, vmem_limit_bytes=used + 8 * 1024 * 1024),
        name="vcycle",
    )(load.reshape(rows, nx), density.reshape(nz * ny, nx), moduli, fixed.reshape(nz * ny, nx))
    shape = (3, nz, ny, nx)
    return u.reshape(shape), r.reshape(shape)


def solution(mesh):
    ns, nc = mesh.shape["slab"], mesh.shape["col"]
    placed = (P(None, "slab", "col", None), P("slab", "col", None), P(), P("slab", "col", None))

    def body(load, density, moduli, fixed):
        return on_device(ns, nc, load, density, moduli, fixed)

    return jax.shard_map(
        body,
        mesh=mesh,
        in_specs=placed,
        out_specs=(P(None, "slab", "col", None), P(None, "slab", "col", None)),
        check_vma=False,
    )
```

```python
import jax
import jax.numpy as jnp
from jax import lax
from jax.experimental import pallas as pl
from jax.experimental.pallas import tpu as pltpu
from jax.sharding import PartitionSpec as P

OMEGA = 0.6
COUPLE = 0.05
CLASSES = 8
COARSE_SWEEPS = 8
LANES = 128
F32 = jnp.float32
LIVE = 27
DIRS = ((0, 1), (0, -1), (1, 0), (-1, 0), (1, 1), (1, -1), (-1, 1), (-1, -1))


class Grid:
    def __init__(self, nz, ny, oz, oy):
        self.nz, self.ny, self.oz, self.oy = nz, ny, oz, oy
        self.z, self.y = nz + 2 * oz, ny + 2 * oy
        self.rows = self.z * self.y

    def row(self, comp, z, y):
        return comp * self.rows + (z + self.oz) * self.y + y + self.oy

    def plane(self, comp, z):
        start = comp * self.rows + z * self.y
        if not isinstance(start, int):
            start = pl.multiple_of(start, 8)
        return pl.ds(start, self.y)


def segments(grid, dz, dy, depth):
    nz, ny = grid.nz, grid.ny

    def cell(step, d, n):
        return (n - step, -step) if d > 0 else (step - 1, n - 1 + step)

    out = []
    if dz == 0:
        for i in range(1, depth + 1):
            mine, there = cell(i, dy, ny)
            out.append((0, mine, 0, there, nz, True))
    elif dy == 0:
        for i in range(1, depth + 1):
            mine, there = cell(i, dz, nz)
            out.append((mine, 0, there, 0, ny, False))
    else:
        for i in range(1, depth):
            for j in range(1, depth + 1 - i):
                mz, tz = cell(i, dz, nz)
                my, ty = cell(j, dy, ny)
                out.append((mz, my, tz, ty, 1, False))
    return out


def message(grid, dz, dy, fields):
    out, at = [], 0
    for field, (comps, depth) in enumerate(fields):
        for comp in range(comps):
            for seg in segments(grid, dz, dy, depth):
                out.append((field, comp, seg, at))
                at += seg[4]
    return out, -(-at // 8) * 8


def window(grid, comp, z, y, count, along_z):
    start = grid.row(comp, z, y)
    if along_z:
        return pl.ds(start, count, stride=grid.y)
    return pl.ds(start, count)


def beside(here, step, count):
    if not isinstance(step, int):
        return lax.rem(here + step, count)
    if step == 0:
        return here
    if step > 0:
        return jnp.where(here >= count - step, here + (step - count), here + step)
    return jnp.where(here < -step, here + (step + count), here + step)


def others(ns, nc, body):
    if ns * nc <= 32:
        for a in range(ns):
            for b in range(nc):
                if a or b:
                    body(a, b)
        return

    def one(t, carry):
        body(t // nc, t % nc)
        return carry

    lax.fori_loop(1, ns * nc, one, 0)


class Exchange:
    def __init__(self, grid, fields, where, send, recv, ssem, rsem):
        self.grid, self.fields, self.where = grid, fields, where
        self.send, self.recv, self.ssem, self.rsem = send, recv, ssem, rsem

    def copy(self, d):
        dz, dy = DIRS[d]
        s, c, ns, nc = self.where
        target = (beside(s, dz, ns), beside(c, dy, nc))
        return pltpu.make_async_remote_copy(
            src_ref=self.send[d], dst_ref=self.recv[d], send_sem=self.ssem.at[d], recv_sem=self.rsem.at[d],
            device_id=target, device_id_type=pl.DeviceIdType.MESH)

    def exists(self, dz, dy):
        s, c, ns, nc = self.where
        ok = None
        for here, d, n in ((s, dz, ns), (c, dy, nc)):
            if d:
                near = here < n - 1 if d > 0 else here > 0
                ok = near if ok is None else jnp.logical_and(ok, near)
        return ok

    def start(self, refs):
        for d, (dz, dy) in enumerate(DIRS):
            rows, _ = message(self.grid, dz, dy, self.fields)

            @pl.when(self.exists(dz, dy))
            def _():
                for field, comp, (z, y, _, _, count, along), at in rows:
                    self.send[d][pl.ds(at, count), :] = refs[field][window(self.grid, comp, z, y, count, along), :]
                self.copy(d).start()

    def finish(self, refs):
        for d, (dz, dy) in enumerate(DIRS):
            rows, _ = message(self.grid, dz, dy, self.fields)

            @pl.when(self.exists(-dz, -dy))
            def _():
                self.copy(d).wait_recv()
                for field, comp, (_, _, z, y, count, along), at in rows:
                    refs[field][window(self.grid, comp, z, y, count, along), :] = self.recv[d][pl.ds(at, count), :]

    def drain(self):
        for d, (dz, dy) in enumerate(DIRS):
            @pl.when(self.exists(dz, dy))
            def _():
                self.copy(d).wait_send()


def lane_iota(rows):
    return lax.broadcasted_iota(jnp.int32, (rows, LANES), 1)


def right(v, step):
    return pltpu.roll(v, step % LANES, 1)


def left(v, step):
    return pltpu.roll(v, LANES - step, 1)


def down(v):
    return pltpu.roll(v, 1, 0)


def up(v):
    return pltpu.roll(v, v.shape[0] - 1, 0)


def pair_sum(v, step):
    lane = lane_iota(v.shape[0])
    first = lane % (2 * step) < step
    return v + jnp.where(first, left(v, step), right(v, step))


def rows_of(start, count):
    if not isinstance(start, int):
        start = pl.multiple_of(start, 8)
    return pl.ds(start, count)


def loop(low, high, rows, plane, body):
    count = high - low
    unit = max(u for u in range(1, count + 1) if count % u == 0 and (u == 1 or 3 * u * rows <= 8 * LIVE))

    def step(i, carry):
        base = low + i * unit
        held, todo = {}, []

        def get(ref, comp, off):
            key = (id(ref), comp, off)
            if key not in held:
                held[key] = ref[plane(comp, base + off), :]
            return held[key]

        for j in range(unit):
            todo += body(lambda ref, comp, off, j=j: get(ref, comp, off + j), base + j)
        for ref, at, value in todo:
            ref[at, :] = value
        return carry

    if count == unit:
        step(0, 0)
    else:
        lax.fori_loop(0, count // unit, step, 0)


class Level:
    def __init__(self, scale, xs, zs, group, ny, closed, plane, k, coef):
        self.scale, self.xs, self.zs, self.group, self.ny, self.closed = scale, xs, zs, group, ny, closed
        self.plane, self.k, self.coef = plane, k, coef

    def loop(self, low, high, body):
        loop(low, high, self.ny, self.plane, body)

    def z_sides(self, get):
        after, before = get(1), get(-1)
        if not self.group:
            return after, before
        here = get(0)
        lane = lane_iota(self.ny) % self.group
        turn = self.group - self.zs
        return (jnp.where(lane < turn, left(here, self.zs), right(after, turn)),
                jnp.where(lane >= self.zs, right(here, self.zs), left(before, turn)))

    def setup(self, low, high, mask, rhs, out):
        def body(get, z):
            k = get(self.k, 0, 0)
            lane = lane_iota(self.ny)
            zp, zm = self.z_sides(lambda off: get(self.k, 0, off))
            inx = lane < LANES - self.xs
            inm = lane >= self.xs
            xp = jnp.where(inx, left(k, self.xs), 0.0)
            xm = jnp.where(inm, right(k, self.xs), 0.0)
            yp, ym = up(k), down(k)
            half = F32(0.5 * self.scale)
            if self.closed:
                row = lax.broadcasted_iota(jnp.int32, (self.ny, LANES), 0)
                iny, inw = row < self.ny - 1, row >= 1
                yp, ym = jnp.where(iny, yp, 0.0), jnp.where(inw, ym, 0.0)
            kzp, kzm = half * (k + zp), half * (k + zm)
            kyp, kym = half * (k + yp), half * (k + ym)
            kxp, kxm = half * (k + xp), half * (k + xm)
            total = kzp + kzm + kyp + kym + kxp + kxm
            if self.closed:
                kyp, kym = jnp.where(iny, kyp, 0.0), jnp.where(inw, kym, 0.0)
            kxp, kxm = jnp.where(inx, kxp, 0.0), jnp.where(inm, kxm, 0.0)
            inside = k > 0.0
            diag = jnp.where(inside, total + F32(2.0 * COUPLE) * k, 1.0)
            weight = jnp.where(inside, F32(OMEGA) / diag, 0.0)
            if mask is not None:
                weight = weight * get(mask, 0, 0)
            p = self.plane(0, z)
            todo = [(self.coef[i], p, value) for i, value in
                    enumerate((kzp, kzm, kyp, kym, kxp, kxm, total + F32(COUPLE) * k, weight))]
            if rhs is not None:
                todo += [(out, self.plane(c, z), weight * get(rhs, c, 0)) for c in range(3)]
            return todo

        self.loop(low, high, body)

    def first(self, low, high, rhs, out):
        self.loop(low, high, lambda get, z: [
            (out, self.plane(c, z), get(self.coef[7], 0, 0) * get(rhs, c, 0)) for c in range(3)])

    def defect(self, get, u, rhs):
        kzp, kzm, kyp, kym, kxp, kxm, own = [get(self.coef[i], 0, 0) for i in range(7)]
        couple = F32(COUPLE) * get(self.k, 0, 0)
        field = [get(u, c, 0) for c in range(3)]
        shared = couple * (field[0] + field[1] + field[2])
        out = []
        for c in range(3):
            v = field[c]
            zp, zm = self.z_sides(lambda off: get(u, c, off))
            near = (kzp * zp + kzm * zm) + (kyp * up(v) + kym * down(v))
            near = near + (kxp * left(v, self.xs) + kxm * right(v, self.xs))
            out.append((get(rhs, c, 0) - shared) + (near - own * v))
        return field, out

    def sweep(self, low, high, u, rhs, out, out_plane=None):
        place = out_plane or self.plane

        def body(get, z):
            field, delta = self.defect(get, u, rhs)
            weight = get(self.coef[7], 0, 0)
            return [(out, place(c, z), field[c] + weight * delta[c]) for c in range(3)]

        self.loop(low, high, body)

    def residual(self, low, high, u, rhs, mask, emit):
        def body(get, z):
            field, delta = self.defect(get, u, rhs)
            todo = []
            for c in range(3):
                value = delta[c] if mask is None else get(mask, 0, 0) * delta[c]
                todo += emit(c, z, value, field[c])
            return todo

        self.loop(low, high, body)


def kernel(ns, nc, g0, g1, ex, load_in, dens_in, moduli_in, fixed_in, out_u, out_r, *scratch):
    it = iter(scratch)
    take = lambda n: [next(it) for _ in range(n)]
    k0, m0, b0, ua, ub = take(5)
    c0 = take(8)
    k1, b1, va, vb = take(4)
    c1 = take(8)
    k2, b2, wa, wb, wf = take(5)
    c2 = take(8)
    k3, b3, xa, xb = take(4)
    c3 = take(8)
    pack, gather, stage = take(3)
    s, c = lax.axis_index("slab"), lax.axis_index("col")
    where = (s, c, ns, nc)
    rounds = []
    for grid, fields in ex:
        send, recv = take(8), take(8)
        ssem, rsem = take(2)
        rounds.append(Exchange(grid, fields, where, send, recv, ssem, rsem))
    gsend, grecv = take(2)
    ex_a, ex_k, ex_b, ex_u, ex_v = rounds
    load, dens, moduli, fixed, arrived = take(5)
    fetches = [pltpu.make_async_copy(src, dst, arrived.at[i]) for i, (src, dst) in enumerate(
        ((dens_in, dens), (moduli_in, moduli), (fixed_in, fixed), (load_in, load)))]
    for fetch in fetches:
        fetch.start()
    n0, y0, n1, y1 = g0.nz, g0.ny, g1.nz, g1.ny

    def zero(ref):
        rows = ref.shape[0]
        ref[...] = jnp.zeros((rows, LANES), F32)

    barrier = pltpu.get_barrier_semaphore()

    def greet(a, b):
        target = (beside(s, a, ns), beside(c, b, nc))
        pl.semaphore_signal(barrier, inc=1, device_id=target, device_id_type=pl.DeviceIdType.MESH)

    others(ns, nc, greet)

    for ref in (k0, m0, b0, k1):
        zero(ref)

    def fill(get, z):
        d = get(dens, 0, 0)
        value = jnp.zeros((y0, LANES), F32)
        for klass in range(CLASSES):
            value = jnp.where(d == klass, moduli[klass], value)
        keep = 1.0 - get(fixed, 0, 0).astype(F32)
        wide = lambda v: jnp.concatenate(
            [jnp.zeros((g0.oy, LANES), F32), v, jnp.zeros((g0.oy, LANES), F32)], axis=0)
        p = g0.plane(0, z + g0.oz)
        return [(k0, p, wide(value)), (m0, p, wide(keep))] + [
            (b0, g0.plane(comp, z + g0.oz), wide(get(load, comp, 0))) for comp in range(3)]

    for fetch in fetches:
        fetch.wait()
    loop(0, n0, y0, lambda comp, z: rows_of((comp * n0 + z) * y0, y0), fill)
    pl.semaphore_wait(barrier, ns * nc - 1)
    ex_a.start([k0, m0, b0])

    def coarser(src, grid, comp, z, y, count, steps):
        total = None
        for dz in range(2):
            for dy in range(2):
                part = src[pl.ds(grid.row(comp, 2 * z + dz, 2 * y + dy), count, stride=2), :]
                total = part if total is None else total + part
        for step in steps:
            total = pair_sum(total, step)
        return total * F32(0.125)

    for z in range(n1):
        k1[pl.ds(g1.row(0, z, 0), y1), :] = coarser(k0, g0, 0, z, 0, y1, (1,))
    ex_k.start([k1])

    lane4 = lane_iota(4) % 4

    def packed(src, comp, slot):
        value = jnp.zeros((4, LANES), F32)
        for z in range(n1 // 2):
            value = jnp.where(lane4 == z, coarser(src, g1, comp, z, 0, y1 // 2, (2,)), value)
        pack[pl.ds(4 * slot, 4), :] = value

    packed(k1, 0, 3)
    for ref in (ua, ub, b1, va, vb):
        zero(ref)

    level0 = Level(1.0, 1, 0, 0, g0.y, False, g0.plane, k0, c0)
    level1 = Level(0.25, 2, 0, 0, g1.y, False, g1.plane, k1, c1)
    y2, y3 = 4 * nc, 2 * nc
    plane2 = lambda comp, z: rows_of((comp * (ns + 2) + z) * y2, y2)
    plane3 = lambda comp, z: rows_of((comp * (ns + 2) + z) * y3, y3)
    wide2 = lambda comp, z: rows_of((comp * (ns + 2) + z) * (y2 + 16) + 8, y2)
    level2 = Level(0.25**2, 4, 1, 4, y2, True, plane2, k2, c2)
    level3 = Level(0.25**3, 8, 2, 4, y3, True, plane3, k3, c3)
    for ref, comps, plane, rows in ((k2, 1, plane2, y2), (wa, 3, plane2, y2), (wb, 3, plane2, y2),
                                    (k3, 1, plane3, y3), (xa, 3, plane3, y3), (xb, 3, plane3, y3),
                                    (wf, 3, lambda comp, z: rows_of((comp * (ns + 2) + z) * (y2 + 16), y2 + 16), y2 + 16)):
        for comp in range(comps):
            for z in (0, ns + 1):
                ref[plane(comp, z), :] = jnp.zeros((rows, LANES), F32)

    ex_a.finish([k0, m0, b0])
    level0.setup(g0.oz - 2, g0.oz + n0 + 2, m0, b0, ua)
    level0.sweep(g0.oz - 1, g0.oz + n0 + 1, ua, b0, ub)

    def keep0(comp, z, value, field):
        return [(ua, g0.plane(comp, z), value)]

    level0.residual(g0.oz, g0.oz + n0, ub, b0, m0, keep0)
    for comp in range(3):
        for z in range(n1):
            b1[pl.ds(g1.row(comp, z, 0), y1), :] = coarser(ua, g0, comp, z, 0, y1, (1,))
    ex_b.start([b1])

    ex_k.finish([k1])
    level1.setup(g1.oz - 3, g1.oz + n1 + 3, None, None, None)
    ex_b.finish([b1])
    level1.first(g1.oz - 2, g1.oz + n1 + 2, b1, va)
    level1.sweep(g1.oz - 1, g1.oz + n1 + 1, va, b1, vb)

    def keep1(comp, z, value, field):
        return [(va, g1.plane(comp, z), value)]

    level1.residual(g1.oz, g1.oz + n1, vb, b1, None, keep1)
    for comp in range(3):
        packed(va, comp, comp)

    here = pl.ds(pl.multiple_of((s * nc + c) * 16, 16), 16)
    gather[here, :] = pack[...]

    def spread(a, b):
        target = (beside(s, a, ns), beside(c, b, nc))
        pltpu.make_async_remote_copy(
            src_ref=gather.at[here], dst_ref=gather.at[here], send_sem=gsend, recv_sem=grecv,
            device_id=target, device_id_type=pl.DeviceIdType.MESH).start()

    others(ns, nc, spread)
    all_others = pl.ds(0, (ns * nc - 1) * 16)
    everything = pltpu.make_async_remote_copy(
        src_ref=gather.at[all_others], dst_ref=gather.at[all_others], send_sem=gsend, recv_sem=grecv,
        device_id=(beside(s, 1, ns), c), device_id_type=pl.DeviceIdType.MESH)
    everything.wait_recv()
    ex_v.start([vb])
    ex_u.start([ub, m0])

    def assemble(t, carry):
        z, pair = t // (nc // 2), t % (nc // 2)
        first = gather[rows_of(t * 32, 16), :]
        second = gather[rows_of(t * 32 + 16, 16), :]
        for f in range(4):
            value = jnp.concatenate([first[4 * f:4 * f + 4], second[4 * f:4 * f + 4]], axis=0)
            ref, comp = (k2, 0) if f == 3 else (b2, f)
            ref[rows_of((comp * (ns + 2) + z + 1) * y2 + pair * 8, 8), :] = value
        return carry

    if ns * nc <= 32:
        for t in range(ns * nc // 2):
            assemble(t, 0)
    else:
        lax.fori_loop(0, ns * nc // 2, assemble, 0)
    level2.setup(1, ns + 1, None, b2, wa)
    level2.sweep(1, ns + 1, wa, b2, wb)

    def keep2(comp, z, value, field):
        return [(wa, plane2(comp, z), value)]

    level2.residual(1, ns + 1, wb, b2, None, keep2)

    def shrink3(z, carry):
        for src, dst, comp in ((k2, k3, 0), (wa, b3, 0), (wa, b3, 1), (wa, b3, 2)):
            start = (comp * (ns + 2) + z) * y2
            total = src[pl.ds(start, y3, stride=2), :] + src[pl.ds(start + 1, y3, stride=2), :]
            dst[plane3(comp, z), :] = pair_sum(pair_sum(total, 1), 4) * F32(0.125)
        return carry

    lax.fori_loop(1, ns + 1, shrink3, 0)
    level3.setup(1, ns + 1, None, b3, xa)
    old, new = xa, xb
    for turn in range(COARSE_SWEEPS - 1):
        level3.sweep(1, ns + 1, old, b3, new)
        old, new = new, old
    coarse = old

    def twice(value, slot):
        rows = value.shape[0]
        stage[pl.ds(slot, rows, stride=2), :] = value
        stage[pl.ds(slot + 1, rows, stride=2), :] = value
        return slot, 2 * rows

    def staged(spot):
        return stage[pl.ds(spot[0], spot[1]), :]

    def add2(z, carry):
        spots = [twice(coarse[plane3(comp, z), :], comp * y2) for comp in range(3)]
        for comp in range(3):
            p = plane2(comp, z)
            wb[p, :] = wb[p, :] + staged(spots[comp])
        return carry

    lax.fori_loop(1, ns + 1, add2, 0)

    level2.sweep(1, ns + 1, wb, b2, wa)
    level2.sweep(1, ns + 1, wa, b2, wf, wide2)

    ex_v.finish([vb])
    lane8 = lane_iota(8)
    odd = c % 2 == 1

    for i in range(g1.z // 2):
        block, j = s + (i + 2) // 4, (i + 2) % 4
        spots = []
        for comp in range(3):
            at = (comp * (ns + 2) + block) * (y2 + 16) + (c // 2) * 8
            rows = wf[pl.ds(pl.multiple_of(at, 8), 24), :]
            value = jnp.where(odd, rows[10:18], rows[6:14])
            value = jnp.where(lane8 % 4 == j, value, 0.0)
            spots.append(twice(pair_sum(pair_sum(value, 1), 2), (i % 2 * 3 + comp) * 16))
        for comp in range(3):
            grown = staged(spots[comp])
            for dz in range(2):
                p = g1.plane(comp, 2 * i + dz)
                inside = k1[g1.plane(0, 2 * i + dz), :] > 0.0
                va[p, :] = vb[p, :] + jnp.where(inside, grown, 0.0)
    level1.sweep(g1.oz - 3, g1.oz + n1 + 3, va, b1, vb)
    level1.sweep(g1.oz - 2, g1.oz + n1 + 2, vb, b1, va)

    ex_u.finish([ub, m0])

    def add0(i, carry):
        spots = [twice(va[g1.plane(comp, i + g1.oz - 2), :][2:14], comp * g0.y) for comp in range(3)]
        for comp in range(3):
            grown = staged(spots[comp])
            for dz in range(2):
                p = g0.plane(comp, 2 * i + dz)
                ua[p, :] = ub[p, :] + m0[g0.plane(0, 2 * i + dz), :] * grown
        return carry

    lax.fori_loop(0, g0.z // 2, add0, 0)
    level0.sweep(g0.oz - 2, g0.oz + n0 + 2, ua, b0, ub)
    level0.sweep(g0.oz - 1, g0.oz + n0 + 1, ub, b0, ua)

    def emit(comp, z, value, field):
        at = pl.ds(pl.multiple_of((comp * n0 + z - g0.oz) * y0, 8), y0)
        own = slice(g0.oy, g0.oy + y0)
        return [(out_r, at, value[own]), (out_u, at, field[own])]

    level0.residual(g0.oz, g0.oz + n0, ua, b0, m0, emit)

    everything.wait_send()
    for ex_one in rounds:
        ex_one.drain()


def on_device(ns, nc, load, density, moduli, fixed):
    _, nz, ny, nx = load.shape
    g0 = Grid(nz, ny, 4, 4)
    g1 = Grid(nz // 2, ny // 2, 4, 4)
    ex = (
        (g0, ((1, 3), (1, 2), (3, 2))),
        (g1, ((1, 4),)),
        (g1, ((3, 3),)),
        (g0, ((3, 3), (1, 3))),
        (g1, ((3, 4),)),
    )
    buf = lambda rows: pltpu.VMEM((rows, LANES), F32)
    y2, y3 = 4 * nc, 2 * nc
    s2, s3 = (ns + 2) * y2, (ns + 2) * y3
    scratch = [buf(g0.rows)] * 2 + [buf(3 * g0.rows)] * 3 + [buf(g0.rows)] * 8
    scratch += [buf(g1.rows)] + [buf(3 * g1.rows)] * 3 + [buf(g1.rows)] * 8
    scratch += [buf(s2)] + [buf(3 * s2)] * 3 + [buf(3 * (ns + 2) * (y2 + 16))] + [buf(s2)] * 8
    scratch += [buf(s3)] + [buf(3 * s3)] * 3 + [buf(s3)] * 8
    scratch += [buf(16), buf(ns * nc * 16), buf(3 * max(y2, 32))]
    for grid, fields in ex:
        sizes = [message(grid, dz, dy, fields)[1] for dz, dy in DIRS]
        scratch += [buf(n) for n in sizes] * 2
        scratch += [pltpu.SemaphoreType.DMA((8,))] * 2
    scratch += [pltpu.SemaphoreType.DMA] * 2

    def run(*args):
        kernel(ns, nc, g0, g1, ex, *args)

    rows = 3 * nz * ny
    scratch += [buf(rows), pltpu.VMEM((nz * ny, LANES), jnp.int32), pltpu.SMEM((CLASSES,), F32),
                pltpu.VMEM((nz * ny, LANES), jnp.int32), pltpu.SemaphoreType.DMA((4,))]
    used = sum(4 * LANES * ref.shape[0] for ref in scratch if hasattr(ref, "shape"))
    vmem = pl.BlockSpec(memory_space=pltpu.VMEM)
    u, r = pl.pallas_call(
        run,
        out_shape=[jax.ShapeDtypeStruct((rows, nx), F32)] * 2,
        in_specs=[pl.BlockSpec(memory_space=pltpu.HBM)] * 4,
        out_specs=[vmem, vmem],
        scratch_shapes=scratch,
        compiler_params=pltpu.CompilerParams(collective_id=0, has_side_effects=True, vmem_limit_bytes=used + 8 * 1024 * 1024),
        name="vcycle",
    )(load.reshape(rows, nx), density.reshape(nz * ny, nx), moduli, fixed.reshape(nz * ny, nx))
    shape = (3, nz, ny, nx)
    return u.reshape(shape), r.reshape(shape)


def solution(mesh):
    ns, nc = mesh.shape["slab"], mesh.shape["col"]
    placed = (P(None, "slab", "col", None), P("slab", "col", None), P(), P("slab", "col", None))

    def body(load, density, moduli, fixed):
        return on_device(ns, nc, load, density, moduli, fixed)

    return jax.shard_map(
        body,
        mesh=mesh,
        in_specs=placed,
        out_specs=(P(None, "slab", "col", None), P(None, "slab", "col", None)),
        check_vma=False,
    )
```

```python
import math

import jax
import jax.numpy as jnp
from jax import lax
from jax.experimental import pallas as pl
from jax.experimental.pallas import tpu as pltpu
from jax.sharding import PartitionSpec as P

OMEGA = 0.6
COUPLE = 0.05
CLASSES = 8
COARSE_SWEEPS = 8
LANES = 128
F32 = jnp.float32
LIVE = 27
DIRS = ((0, 1), (0, -1), (1, 0), (-1, 0), (1, 1), (1, -1), (-1, 1), (-1, -1))


class Grid:
    def __init__(self, nz, ny, oz, oy):
        self.nz, self.ny, self.oz, self.oy = nz, ny, oz, oy
        self.z, self.y = nz + 2 * oz, ny + 2 * oy
        self.rows = self.z * self.y

    def row(self, comp, z, y):
        return comp * self.rows + (z + self.oz) * self.y + y + self.oy

    def plane(self, comp, z):
        start = comp * self.rows + z * self.y
        if not isinstance(start, int):
            start = pl.multiple_of(start, 8)
        return pl.ds(start, self.y)


def segments(grid, dz, dy, low, depth):
    nz, ny = grid.nz, grid.ny

    def cell(step, d, n):
        return (n - step, -step) if d > 0 else (step - 1, n - 1 + step)

    out = []
    if dz == 0:
        for i in range(low, depth + 1):
            mine, there = cell(i, dy, ny)
            out.append((0, mine, 0, there, nz, True))
    elif dy == 0:
        for i in range(low, depth + 1):
            mine, there = cell(i, dz, nz)
            out.append((mine, 0, there, 0, ny, False))
    else:
        for i in range(1, depth):
            for j in range(max(1, low - i), depth + 1 - i):
                mz, tz = cell(i, dz, nz)
                my, ty = cell(j, dy, ny)
                out.append((mz, my, tz, ty, 1, False))
    return out


def message(grid, dz, dy, fields, pairs):
    runs = [(field, comp, seg) for field, (comps, low, depth) in enumerate(fields) for comp in range(comps)
            for seg in segments(grid, dz, dy, low, depth)]
    width = 2 if pairs else 1
    out, at = [], 0
    for first in range(0, len(runs), width):
        part = runs[first:first + width]
        out.append((part, at))
        at += part[0][2][4]
    return out, -(-at // 8) * 8


def window(grid, comp, z, y, count, along_z):
    start = grid.row(comp, z, y)
    if along_z:
        return pl.ds(start, count, stride=grid.y)
    return pl.ds(start, count)


def beside(here, step, count):
    if not isinstance(step, int):
        return lax.rem(here + step, count)
    if step == 0:
        return here
    if step > 0:
        return jnp.where(here >= count - step, here + (step - count), here + step)
    return jnp.where(here < -step, here + (step + count), here + step)


def others(ns, nc, body):
    if ns * nc <= 32:
        for a in range(ns):
            for b in range(nc):
                if a or b:
                    body(a, b)
        return

    def one(t, carry):
        body(t // nc, t % nc)
        return carry

    lax.fori_loop(1, ns * nc, one, 0)


class Exchange:
    def __init__(self, grid, fields, pairs, where, send, recv, ssem, rsem):
        self.grid, self.fields, self.pairs, self.where = grid, fields, pairs, where
        self.send, self.recv, self.ssem, self.rsem = send, recv, ssem, rsem

    def copy(self, d):
        dz, dy = DIRS[d]
        s, c, ns, nc = self.where
        target = (beside(s, dz, ns), beside(c, dy, nc))
        return pltpu.make_async_remote_copy(
            src_ref=self.send[d], dst_ref=self.recv[d], send_sem=self.ssem.at[d], recv_sem=self.rsem.at[d],
            device_id=target, device_id_type=pl.DeviceIdType.MESH)

    def exists(self, dz, dy):
        s, c, ns, nc = self.where
        ok = None
        for here, d, n in ((s, dz, ns), (c, dy, nc)):
            if d:
                near = here < n - 1 if d > 0 else here > 0
                ok = near if ok is None else jnp.logical_and(ok, near)
        return ok

    def start(self, refs):
        for d, (dz, dy) in enumerate(DIRS):
            parts, _ = message(self.grid, dz, dy, self.fields, self.pairs)

            @pl.when(self.exists(dz, dy))
            def _():
                for runs, at in parts:
                    values = [refs[field][window(self.grid, comp, z, y, count, along), :]
                              for field, comp, (z, y, _, _, count, along) in runs]
                    value = values[0]
                    if len(values) == 2:
                        value = jnp.where(lane_iota(value.shape[0]) % 2 == 0, value, values[1])
                    self.send[d][pl.ds(at, value.shape[0]), :] = value
                self.copy(d).start()

    def finish(self, refs):
        for d, (dz, dy) in enumerate(DIRS):
            parts, _ = message(self.grid, dz, dy, self.fields, self.pairs)

            @pl.when(self.exists(-dz, -dy))
            def _():
                self.copy(d).wait_recv()
                for runs, at in parts:
                    value = self.recv[d][pl.ds(at, runs[0][2][4]), :]
                    values = [value]
                    if len(runs) == 2:
                        even = lane_iota(value.shape[0]) % 2 == 0
                        values = [jnp.where(even, value, right(value, 1)), jnp.where(even, left(value, 1), value)]
                    for (field, comp, (_, _, z, y, count, along)), value in zip(runs, values):
                        refs[field][window(self.grid, comp, z, y, count, along), :] = value

    def drain(self):
        for d, (dz, dy) in enumerate(DIRS):
            @pl.when(self.exists(dz, dy))
            def _():
                self.copy(d).wait_send()


def lane_iota(rows):
    return lax.broadcasted_iota(jnp.int32, (rows, LANES), 1)


def right(v, step):
    return pltpu.roll(v, step % LANES, 1)


def left(v, step):
    return pltpu.roll(v, LANES - step, 1)


def down(v):
    return pltpu.roll(v, 1, 0)


def up(v):
    return pltpu.roll(v, v.shape[0] - 1, 0)


def pair_sum(v, step):
    lane = lane_iota(v.shape[0])
    first = lane % (2 * step) < step
    return v + jnp.where(first, left(v, step), right(v, step))


def rows_of(start, count):
    if not isinstance(start, int):
        start = pl.multiple_of(start, 8)
    return pl.ds(start, count)


def loop(low, high, rows, plane, body):
    count = high - low
    unit = max(u for u in range(1, count + 1) if count % u == 0 and (u == 1 or 3 * u * rows <= 8 * LIVE))

    def step(i, carry):
        base = low + i * unit
        held, todo = {}, []

        def get(ref, comp, off):
            key = (id(ref), comp, off)
            if key not in held:
                held[key] = ref[plane(comp, base + off), :]
            return held[key]

        for j in range(unit):
            todo += body(lambda ref, comp, off, j=j: get(ref, comp, off + j), base + j)
        for ref, at, value in todo:
            ref[at, :] = value
        return carry

    if count == unit:
        step(0, 0)
    else:
        lax.fori_loop(0, count // unit, step, 0)


class Level:
    def __init__(self, scale, xs, zs, group, ny, closed, plane, k, coef):
        self.scale, self.xs, self.zs, self.group, self.ny, self.closed = scale, xs, zs, group, ny, closed
        self.plane, self.k, self.coef = plane, k, coef

    def loop(self, low, high, body):
        loop(low, high, self.ny, self.plane, body)

    def z_sides(self, get):
        after, before = get(1), get(-1)
        if not self.group:
            return after, before
        here = get(0)
        lane = lane_iota(self.ny) % self.group
        turn = self.group - self.zs
        return (jnp.where(lane < turn, left(here, self.zs), right(after, turn)),
                jnp.where(lane >= self.zs, right(here, self.zs), left(before, turn)))

    def setup(self, low, high):
        def body(get, z):
            k = get(self.k, 0, 0)
            lane = lane_iota(self.ny)
            zp, zm = self.z_sides(lambda off: get(self.k, 0, off))
            inx = lane < LANES - self.xs
            inm = lane >= self.xs
            xp = jnp.where(inx, left(k, self.xs), 0.0)
            xm = jnp.where(inm, right(k, self.xs), 0.0)
            yp, ym = up(k), down(k)
            half = F32(0.5 * self.scale)
            if self.closed:
                row = lax.broadcasted_iota(jnp.int32, (self.ny, LANES), 0)
                iny, inw = row < self.ny - 1, row >= 1
                yp, ym = jnp.where(iny, yp, 0.0), jnp.where(inw, ym, 0.0)
            kzp, kzm = half * (k + zp), half * (k + zm)
            kyp, kym = half * (k + yp), half * (k + ym)
            kxp, kxm = half * (k + xp), half * (k + xm)
            total = kzp + kzm + kyp + kym + kxp + kxm
            if self.closed:
                kyp, kym = jnp.where(iny, kyp, 0.0), jnp.where(inw, kym, 0.0)
            kxp, kxm = jnp.where(inx, kxp, 0.0), jnp.where(inm, kxm, 0.0)
            inside = k > 0.0
            diag = jnp.where(inside, total + F32(2.0 * COUPLE) * k, 1.0)
            weight = jnp.where(inside, F32(OMEGA) / diag, 0.0)
            p = self.plane(0, z)
            return [(self.coef[i], p, value) for i, value in
                    enumerate((kzp, kzm, kyp, kym, kxp, kxm, total + F32(COUPLE) * k, weight))]

        self.loop(low, high, body)

    def first(self, low, high, rhs, out, mask=None):
        def body(get, z):
            weight, todo = get(self.coef[7], 0, 0), []
            if mask is not None:
                weight = weight * get(mask, 0, 0)
                todo = [(self.coef[7], self.plane(0, z), weight)]
            return todo + [(out, self.plane(c, z), weight * get(rhs, c, 0)) for c in range(3)]

        self.loop(low, high, body)

    def defect(self, get, u, rhs):
        kzp, kzm, kyp, kym, kxp, kxm, own = [get(self.coef[i], 0, 0) for i in range(7)]
        couple = F32(COUPLE) * get(self.k, 0, 0)
        field = [get(u, c, 0) for c in range(3)]
        shared = couple * (field[0] + field[1] + field[2])
        out = []
        for c in range(3):
            v = field[c]
            zp, zm = self.z_sides(lambda off: get(u, c, off))
            near = (kzp * zp + kzm * zm) + (kyp * up(v) + kym * down(v))
            near = near + (kxp * left(v, self.xs) + kxm * right(v, self.xs))
            out.append((get(rhs, c, 0) - shared) + (near - own * v))
        return field, out

    def sweep(self, low, high, u, rhs, out, out_plane=None):
        place = out_plane or self.plane

        def body(get, z):
            field, delta = self.defect(get, u, rhs)
            weight = get(self.coef[7], 0, 0)
            return [(out, place(c, z), field[c] + weight * delta[c]) for c in range(3)]

        self.loop(low, high, body)

    def residual(self, low, high, u, rhs, mask, emit):
        def body(get, z):
            field, delta = self.defect(get, u, rhs)
            todo = []
            for c in range(3):
                value = delta[c] if mask is None else get(mask, 0, 0) * delta[c]
                todo += emit(c, z, value, field[c])
            return todo

        self.loop(low, high, body)


def kernel(ns, nc, g0, g1, ex, load_in, dens_in, moduli_in, fixed_in, out_u, out_r, *scratch):
    it = iter(scratch)
    take = lambda n: [next(it) for _ in range(n)]
    k0, m0, b0, ua, ub = take(5)
    c0 = take(8)
    k1, b1, va, vb = take(4)
    c1 = take(8)
    k2, b2, wa, wb, wf = take(5)
    c2 = take(8)
    k3, b3, xa, xb = take(4)
    c3 = take(8)
    gk, gb, stage = take(3)
    s, c = lax.axis_index("slab"), lax.axis_index("col")
    where = (s, c, ns, nc)
    rounds = []
    for grid, fields, pairs in ex:
        send, recv = take(8), take(8)
        ssem, rsem = take(2)
        rounds.append(Exchange(grid, fields, pairs, where, send, recv, ssem, rsem))
    ex_s, ex_a, ex_k, ex_b, ex_u, ex_v = rounds
    load, dens, moduli, fixed, arrived = take(5)
    fetches = [pltpu.make_async_copy(src, dst, arrived.at[i]) for i, (src, dst) in enumerate(
        ((dens_in, dens), (moduli_in, moduli), (fixed_in, fixed), (load_in, load)))]
    for fetch in fetches:
        fetch.start()
    n0, y0, n1, y1 = g0.nz, g0.ny, g1.nz, g1.ny

    def zero(ref):
        rows = ref.shape[0]
        ref[...] = jnp.zeros((rows, LANES), F32)

    barrier = pltpu.get_barrier_semaphore()

    def greet(a, b):
        target = (beside(s, a, ns), beside(c, b, nc))
        pl.semaphore_signal(barrier, inc=1, device_id=target, device_id_type=pl.DeviceIdType.MESH)

    others(ns, nc, greet)

    for ref in (k0, m0, b0, k1):
        zero(ref)

    def fill(get, z):
        d = get(dens, 0, 0)
        value = jnp.zeros((y0, LANES), F32)
        for klass in range(CLASSES):
            value = jnp.where(d == klass, moduli[klass], value)
        keep = 1.0 - get(fixed, 0, 0).astype(F32)
        wide = lambda v: jnp.concatenate(
            [jnp.zeros((g0.oy, LANES), F32), v, jnp.zeros((g0.oy, LANES), F32)], axis=0)
        p = g0.plane(0, z + g0.oz)
        return [(k0, p, wide(value)), (m0, p, wide(keep))] + [
            (b0, g0.plane(comp, z + g0.oz), wide(get(load, comp, 0))) for comp in range(3)]

    for fetch in fetches:
        fetch.wait()
    loop(0, n0, y0, lambda comp, z: rows_of((comp * n0 + z) * y0, y0), fill)
    pl.semaphore_wait(barrier, ns * nc - 1)
    ex_s.start([k0])
    ex_a.start([m0, b0])

    def coarser(src, grid, comp, z, y, count, steps):
        total = None
        for dz in range(2):
            for dy in range(2):
                part = src[pl.ds(grid.row(comp, 2 * z + dz, 2 * y + dy), count, stride=2), :]
                total = part if total is None else total + part
        for step in steps:
            total = pair_sum(total, step)
        return total * F32(0.125)

    for z in range(n1):
        k1[pl.ds(g1.row(0, z, 0), y1), :] = coarser(k0, g0, 0, z, 0, y1, (1,))
    ex_k.start([k1])

    lane4 = lane_iota(4) % 4

    here = s * nc + c

    def packed(src, comp):
        value = jnp.zeros((4, LANES), F32)
        for z in range(n1 // 2):
            value = jnp.where(lane4 == z, coarser(src, g1, comp, z, 0, y1 // 2, (2,)), value)
        return value

    def gather(ref, comps, send_sem, recv_sem):
        own = pl.ds(here * comps, comps)

        def spread(a, b):
            pltpu.make_async_remote_copy(
                src_ref=ref.at[own], dst_ref=ref.at[own], send_sem=send_sem, recv_sem=recv_sem,
                device_id=(beside(s, a, ns), beside(c, b, nc)), device_id_type=pl.DeviceIdType.MESH).start()

        others(ns, nc, spread)
        rest = pl.ds(0, (ns * nc - 1) * comps)
        return pltpu.make_async_remote_copy(
            src_ref=ref.at[rest], dst_ref=ref.at[rest], send_sem=send_sem, recv_sem=recv_sem,
            device_id=(beside(s, 1, ns), c), device_id_type=pl.DeviceIdType.MESH)

    def assemble(ref, comps, out):
        def one(t, carry):
            z, pair = t // (nc // 2), t % (nc // 2)
            for comp in range(comps):
                value = jnp.concatenate([ref[2 * t * comps + comp], ref[(2 * t + 1) * comps + comp]], axis=0)
                out[rows_of((comp * (ns + 2) + z + 1) * y2 + pair * 8, 8), :] = value
            return carry

        if ns * nc <= 32:
            for t in range(ns * nc // 2):
                one(t, 0)
        else:
            lax.fori_loop(0, ns * nc // 2, one, 0)

    gk[here] = packed(k1, 0)
    all_k = gather(gk, 1, *take(2))
    for ref in (ua, ub, b1, va, vb):
        zero(ref)

    level0 = Level(1.0, 1, 0, 0, g0.y, False, g0.plane, k0, c0)
    level1 = Level(0.25, 2, 0, 0, g1.y, False, g1.plane, k1, c1)
    y2, y3 = 4 * nc, 2 * nc
    plane2 = lambda comp, z: rows_of((comp * (ns + 2) + z) * y2, y2)
    plane3 = lambda comp, z: rows_of((comp * (ns + 2) + z) * y3, y3)
    wide2 = lambda comp, z: rows_of((comp * (ns + 2) + z) * (y2 + 16) + 8, y2)
    level2 = Level(0.25**2, 4, 1, 4, y2, True, plane2, k2, c2)
    level3 = Level(0.25**3, 8, 2, 4, y3, True, plane3, k3, c3)
    for ref, comps, plane, rows in ((k2, 1, plane2, y2), (wa, 3, plane2, y2), (wb, 3, plane2, y2),
                                    (k3, 1, plane3, y3), (xa, 3, plane3, y3), (xb, 3, plane3, y3),
                                    (wf, 3, lambda comp, z: rows_of((comp * (ns + 2) + z) * (y2 + 16), y2 + 16), y2 + 16)):
        for comp in range(comps):
            for z in (0, ns + 1):
                ref[plane(comp, z), :] = jnp.zeros((rows, LANES), F32)

    ex_s.finish([k0])
    level0.setup(g0.oz - 2, g0.oz + n0 + 2)
    ex_a.finish([m0, b0])
    level0.first(g0.oz - 2, g0.oz + n0 + 2, b0, ua, m0)
    level0.sweep(g0.oz - 1, g0.oz + n0 + 1, ua, b0, ub)

    def keep0(comp, z, value, field):
        return [(ua, g0.plane(comp, z), value)]

    level0.residual(g0.oz, g0.oz + n0, ub, b0, m0, keep0)
    for comp in range(3):
        for z in range(n1):
            b1[pl.ds(g1.row(comp, z, 0), y1), :] = coarser(ua, g0, comp, z, 0, y1, (1,))
    ex_b.start([b1])

    ex_k.finish([k1])
    level1.setup(g1.oz - 3, g1.oz + n1 + 3)
    all_k.wait_recv()
    assemble(gk, 1, k2)
    level2.setup(1, ns + 1)

    def shrink3(pairs):
        def body(z, carry):
            for src, dst, comp in pairs:
                start = (comp * (ns + 2) + z) * y2
                total = src[pl.ds(start, y3, stride=2), :] + src[pl.ds(start + 1, y3, stride=2), :]
                dst[plane3(comp, z), :] = pair_sum(pair_sum(total, 1), 4) * F32(0.125)
            return carry

        if ns <= 4:
            for z in range(1, ns + 1):
                body(z, 0)
        else:
            lax.fori_loop(1, ns + 1, body, 0)

    shrink3([(k2, k3, 0)])
    level3.setup(1, ns + 1)
    ex_b.finish([b1])
    ex_u.start([ub, m0])
    level1.first(g1.oz - 2, g1.oz + n1 + 2, b1, va)
    level1.sweep(g1.oz - 1, g1.oz + n1 + 1, va, b1, vb)

    def keep1(comp, z, value, field):
        return [(va, g1.plane(comp, z), value)]

    level1.residual(g1.oz, g1.oz + n1, vb, b1, None, keep1)
    for comp in range(3):
        gb[here * 3 + comp] = packed(va, comp)
    all_b = gather(gb, 3, *take(2))
    ex_v.start([vb])

    all_b.wait_recv()
    assemble(gb, 3, b2)
    level2.first(1, ns + 1, b2, wa)
    level2.sweep(1, ns + 1, wa, b2, wb)

    def keep2(comp, z, value, field):
        return [(wa, plane2(comp, z), value)]

    level2.residual(1, ns + 1, wb, b2, None, keep2)

    shrink3([(wa, b3, comp) for comp in range(3)])
    level3.first(1, ns + 1, b3, xa)
    old, new = xa, xb
    for turn in range(COARSE_SWEEPS - 1):
        level3.sweep(1, ns + 1, old, b3, new)
        old, new = new, old
    coarse = old

    def twice(value, slot):
        rows = value.shape[0]
        stage[pl.ds(slot, rows, stride=2), :] = value
        stage[pl.ds(slot + 1, rows, stride=2), :] = value
        return slot, 2 * rows

    def staged(spot):
        return stage[pl.ds(spot[0], spot[1]), :]

    def add2(z, carry):
        spots = [twice(coarse[plane3(comp, z), :], comp * y2) for comp in range(3)]
        for comp in range(3):
            p = plane2(comp, z)
            wb[p, :] = wb[p, :] + staged(spots[comp])
        return carry

    lax.fori_loop(1, ns + 1, add2, 0)

    level2.sweep(1, ns + 1, wb, b2, wa)
    level2.sweep(1, ns + 1, wa, b2, wf, wide2)

    ex_v.finish([vb])
    lane8 = lane_iota(8)
    odd = c % 2 == 1

    for i in range(g1.z // 2):
        block, j = s + (i + 2) // 4, (i + 2) % 4
        spots = []
        for comp in range(3):
            at = (comp * (ns + 2) + block) * (y2 + 16) + (c // 2) * 8
            rows = wf[pl.ds(pl.multiple_of(at, 8), 24), :]
            value = jnp.where(odd, rows[10:18], rows[6:14])
            value = jnp.where(lane8 % 4 == j, value, 0.0)
            spots.append(twice(pair_sum(pair_sum(value, 1), 2), (i % 2 * 3 + comp) * 16))
        for comp in range(3):
            grown = staged(spots[comp])
            for dz in range(2):
                p = g1.plane(comp, 2 * i + dz)
                inside = k1[g1.plane(0, 2 * i + dz), :] > 0.0
                va[p, :] = vb[p, :] + jnp.where(inside, grown, 0.0)
    level1.sweep(g1.oz - 3, g1.oz + n1 + 3, va, b1, vb)
    level1.sweep(g1.oz - 2, g1.oz + n1 + 2, vb, b1, va)

    ex_u.finish([ub, m0])

    def add0(i, carry):
        spots = [twice(va[g1.plane(comp, i + g1.oz - 2), :][2:14], comp * g0.y) for comp in range(3)]
        for comp in range(3):
            grown = staged(spots[comp])
            for dz in range(2):
                p = g0.plane(comp, 2 * i + dz)
                ua[p, :] = ub[p, :] + m0[g0.plane(0, 2 * i + dz), :] * grown
        return carry

    lax.fori_loop(0, g0.z // 2, add0, 0)
    level0.sweep(g0.oz - 2, g0.oz + n0 + 2, ua, b0, ub)
    level0.sweep(g0.oz - 1, g0.oz + n0 + 1, ub, b0, ua)

    def emit(comp, z, value, field):
        at = pl.ds(pl.multiple_of((comp * n0 + z - g0.oz) * y0, 8), y0)
        own = slice(g0.oy, g0.oy + y0)
        return [(out_r, at, value[own]), (out_u, at, field[own])]

    level0.residual(g0.oz, g0.oz + n0, ua, b0, m0, emit)

    all_k.wait_send()
    all_b.wait_send()
    for ex_one in rounds:
        ex_one.drain()


def on_device(ns, nc, load, density, moduli, fixed):
    _, nz, ny, nx = load.shape
    g0 = Grid(nz, ny, 4, 4)
    g1 = Grid(nz // 2, ny // 2, 4, 4)
    ex = (
        (g0, ((1, 1, 3),), False),
        (g0, ((1, 1, 2), (3, 1, 2)), False),
        (g1, ((1, 1, 4),), True),
        (g1, ((3, 1, 3),), True),
        (g0, ((3, 2, 3), (1, 3, 3)), False),
        (g1, ((3, 2, 4),), True),
    )
    buf = lambda rows: pltpu.VMEM((rows, LANES), F32)
    y2, y3 = 4 * nc, 2 * nc
    s2, s3 = (ns + 2) * y2, (ns + 2) * y3
    scratch = [buf(g0.rows)] * 2 + [buf(3 * g0.rows)] * 3 + [buf(g0.rows)] * 8
    scratch += [buf(g1.rows)] + [buf(3 * g1.rows)] * 3 + [buf(g1.rows)] * 8
    scratch += [buf(s2)] + [buf(3 * s2)] * 3 + [buf(3 * (ns + 2) * (y2 + 16))] + [buf(s2)] * 8
    scratch += [buf(s3)] + [buf(3 * s3)] * 3 + [buf(s3)] * 8
    scratch += [pltpu.VMEM((ns * nc, 4, LANES), F32), pltpu.VMEM((ns * nc * 3, 4, LANES), F32), buf(3 * max(y2, 32))]
    for grid, fields, pairs in ex:
        sizes = [message(grid, dz, dy, fields, pairs)[1] for dz, dy in DIRS]
        scratch += [buf(n) for n in sizes] * 2
        scratch += [pltpu.SemaphoreType.DMA((8,))] * 2

    def run(*args):
        kernel(ns, nc, g0, g1, ex, *args)

    rows = 3 * nz * ny
    scratch += [buf(rows), pltpu.VMEM((nz * ny, LANES), jnp.int32), pltpu.SMEM((CLASSES,), F32),
                pltpu.VMEM((nz * ny, LANES), jnp.int32), pltpu.SemaphoreType.DMA((4,))]
    scratch += [pltpu.SemaphoreType.DMA] * 4
    used = sum(4 * math.prod(ref.shape) for ref in scratch if hasattr(ref, "shape"))
    vmem = pl.BlockSpec(memory_space=pltpu.VMEM)
    u, r = pl.pallas_call(
        run,
        out_shape=[jax.ShapeDtypeStruct((rows, nx), F32)] * 2,
        in_specs=[pl.BlockSpec(memory_space=pltpu.HBM)] * 4,
        out_specs=[vmem, vmem],
        scratch_shapes=scratch,
        compiler_params=pltpu.CompilerParams(collective_id=0, has_side_effects=True, vmem_limit_bytes=used + 8 * 1024 * 1024),
        name="vcycle",
    )(*[pltpu.with_memory_space_constraint(a, pltpu.HBM) for a in (
        load.reshape(rows, nx), density.reshape(nz * ny, nx), moduli, fixed.reshape(nz * ny, nx))])
    shape = (3, nz, ny, nx)
    return u.reshape(shape), r.reshape(shape)


def solution(mesh):
    ns, nc = mesh.shape["slab"], mesh.shape["col"]
    placed = (P(None, "slab", "col", None), P("slab", "col", None), P(), P("slab", "col", None))

    def body(load, density, moduli, fixed):
        return on_device(ns, nc, load, density, moduli, fixed)

    return jax.shard_map(
        body,
        mesh=mesh,
        in_specs=placed,
        out_specs=(P(None, "slab", "col", None), P(None, "slab", "col", None)),
        check_vma=False,
    )
```

```python
import math

import jax
import jax.numpy as jnp
from jax import lax
from jax.experimental import pallas as pl
from jax.experimental.pallas import tpu as pltpu
from jax.sharding import PartitionSpec as P

OMEGA = 0.6
COUPLE = 0.05
CLASSES = 8
COARSE_SWEEPS = 8
LANES = 128
F32 = jnp.float32
LIVE = 27
DIRS = ((0, 1), (0, -1), (1, 0), (-1, 0), (1, 1), (1, -1), (-1, 1), (-1, -1))


class Grid:
    def __init__(self, nz, ny, oz, oy):
        self.nz, self.ny, self.oz, self.oy = nz, ny, oz, oy
        self.z, self.y = nz + 2 * oz, ny + 2 * oy
        self.rows = self.z * self.y

    def row(self, comp, z, y):
        return comp * self.rows + (z + self.oz) * self.y + y + self.oy

    def plane(self, comp, z):
        start = comp * self.rows + z * self.y
        if not isinstance(start, int):
            start = pl.multiple_of(start, 8)
        return pl.ds(start, self.y)


def segments(grid, dz, dy, low, depth):
    nz, ny = grid.nz, grid.ny

    def cell(step, d, n):
        return (n - step, -step) if d > 0 else (step - 1, n - 1 + step)

    out = []
    if dz == 0:
        for i in range(low, depth + 1):
            mine, there = cell(i, dy, ny)
            out.append((0, mine, 0, there, nz, True))
    elif dy == 0:
        for i in range(low, depth + 1):
            mine, there = cell(i, dz, nz)
            out.append((mine, 0, there, 0, ny, False))
    else:
        for i in range(1, depth):
            for j in range(max(1, low - i), depth + 1 - i):
                mz, tz = cell(i, dz, nz)
                my, ty = cell(j, dy, ny)
                out.append((mz, my, tz, ty, 1, False))
    return out


def message(grid, dz, dy, fields, pairs):
    runs = [(field, comp, seg) for field, (comps, low, depth) in enumerate(fields) for comp in range(comps)
            for seg in segments(grid, dz, dy, low, depth)]
    width = 2 if pairs else 1
    out, at = [], 0
    for first in range(0, len(runs), width):
        part = runs[first:first + width]
        out.append((part, at))
        at += part[0][2][4]
    return out, -(-at // 8) * 8


def window(grid, comp, z, y, count, along_z):
    start = grid.row(comp, z, y)
    if along_z:
        return pl.ds(start, count, stride=grid.y)
    return pl.ds(start, count)


def beside(here, step, count):
    if not isinstance(step, int):
        return lax.rem(here + step, count)
    if step == 0:
        return here
    if step > 0:
        return jnp.where(here >= count - step, here + (step - count), here + step)
    return jnp.where(here < -step, here + (step + count), here + step)


def others(ns, nc, body):
    if ns * nc <= 32:
        for a in range(ns):
            for b in range(nc):
                if a or b:
                    body(a, b)
        return

    def one(t, carry):
        body(t // nc, t % nc)
        return carry

    lax.fori_loop(1, ns * nc, one, 0)


class Exchange:
    def __init__(self, grid, fields, pairs, where, send, recv, ssem, rsem):
        self.grid, self.fields, self.pairs, self.where = grid, fields, pairs, where
        self.send, self.recv, self.ssem, self.rsem = send, recv, ssem, rsem

    def copy(self, d):
        dz, dy = DIRS[d]
        s, c, ns, nc = self.where
        target = (beside(s, dz, ns), beside(c, dy, nc))
        return pltpu.make_async_remote_copy(
            src_ref=self.send[d], dst_ref=self.recv[d], send_sem=self.ssem.at[d], recv_sem=self.rsem.at[d],
            device_id=target, device_id_type=pl.DeviceIdType.MESH)

    def exists(self, dz, dy):
        s, c, ns, nc = self.where
        ok = None
        for here, d, n in ((s, dz, ns), (c, dy, nc)):
            if d:
                near = here < n - 1 if d > 0 else here > 0
                ok = near if ok is None else jnp.logical_and(ok, near)
        return ok

    def start(self, refs):
        for d, (dz, dy) in enumerate(DIRS):
            parts, _ = message(self.grid, dz, dy, self.fields, self.pairs)
            for runs, at in parts:
                values = [refs[field][window(self.grid, comp, z, y, count, along), :]
                          for field, comp, (z, y, _, _, count, along) in runs]
                value = values[0]
                if len(values) == 2:
                    value = jnp.where(lane_iota(value.shape[0]) % 2 == 0, value, values[1])
                self.send[d][pl.ds(at, value.shape[0]), :] = value
        for d, (dz, dy) in enumerate(DIRS):
            @pl.when(self.exists(dz, dy))
            def _():
                self.copy(d).start()

    def finish(self, refs):
        for d, (dz, dy) in enumerate(DIRS):
            @pl.when(self.exists(-dz, -dy))
            def _():
                self.copy(d).wait_recv()
        for d, (dz, dy) in enumerate(DIRS):
            parts, _ = message(self.grid, dz, dy, self.fields, self.pairs)
            here = self.exists(-dz, -dy)
            for runs, at in parts:
                value = jnp.where(here, self.recv[d][pl.ds(at, runs[0][2][4]), :], 0.0)
                values = [value]
                if len(runs) == 2:
                    even = lane_iota(value.shape[0]) % 2 == 0
                    values = [jnp.where(even, value, right(value, 1)), jnp.where(even, left(value, 1), value)]
                for (field, comp, (_, _, z, y, count, along)), value in zip(runs, values):
                    refs[field][window(self.grid, comp, z, y, count, along), :] = value

    def drain(self):
        for d, (dz, dy) in enumerate(DIRS):
            @pl.when(self.exists(dz, dy))
            def _():
                self.copy(d).wait_send()


def lane_iota(rows):
    return lax.broadcasted_iota(jnp.int32, (rows, LANES), 1)


def right(v, step):
    return pltpu.roll(v, step % LANES, 1)


def left(v, step):
    return pltpu.roll(v, LANES - step, 1)


def down(v):
    return pltpu.roll(v, 1, 0)


def up(v):
    return pltpu.roll(v, v.shape[0] - 1, 0)


def pair_sum(v, step):
    lane = lane_iota(v.shape[0])
    first = lane % (2 * step) < step
    return v + jnp.where(first, left(v, step), right(v, step))


def rows_of(start, count):
    if not isinstance(start, int):
        start = pl.multiple_of(start, 8)
    return pl.ds(start, count)


def loop(low, high, rows, plane, body):
    count = high - low
    unit = max(u for u in range(1, count + 1) if count % u == 0 and (u == 1 or 3 * u * rows <= 8 * LIVE))

    def step(i, carry):
        base = low + i * unit
        held, todo = {}, []

        def get(ref, comp, off):
            key = (id(ref), comp, off)
            if key not in held:
                held[key] = ref[plane(comp, base + off), :]
            return held[key]

        for j in range(unit):
            todo += body(lambda ref, comp, off, j=j: get(ref, comp, off + j), base + j)
        for ref, at, value in todo:
            ref[at, :] = value
        return carry

    if count == unit:
        step(0, 0)
    else:
        lax.fori_loop(0, count // unit, step, 0)


class Level:
    def __init__(self, scale, xs, zs, group, ny, closed, plane, k, coef):
        self.scale, self.xs, self.zs, self.group, self.ny, self.closed = scale, xs, zs, group, ny, closed
        self.plane, self.k, self.coef = plane, k, coef

    def loop(self, low, high, body):
        loop(low, high, self.ny, self.plane, body)

    def z_sides(self, get):
        after, before = get(1), get(-1)
        if not self.group:
            return after, before
        here = get(0)
        lane = lane_iota(self.ny) % self.group
        turn = self.group - self.zs
        return (jnp.where(lane < turn, left(here, self.zs), right(after, turn)),
                jnp.where(lane >= self.zs, right(here, self.zs), left(before, turn)))

    def setup(self, low, high):
        def body(get, z):
            k = get(self.k, 0, 0)
            lane = lane_iota(self.ny)
            zp, zm = self.z_sides(lambda off: get(self.k, 0, off))
            inx = lane < LANES - self.xs
            inm = lane >= self.xs
            xp = jnp.where(inx, left(k, self.xs), 0.0)
            xm = jnp.where(inm, right(k, self.xs), 0.0)
            yp, ym = up(k), down(k)
            half = F32(0.5 * self.scale)
            if self.closed:
                row = lax.broadcasted_iota(jnp.int32, (self.ny, LANES), 0)
                iny, inw = row < self.ny - 1, row >= 1
                yp, ym = jnp.where(iny, yp, 0.0), jnp.where(inw, ym, 0.0)
            kzp, kzm = half * (k + zp), half * (k + zm)
            kyp, kym = half * (k + yp), half * (k + ym)
            kxp, kxm = half * (k + xp), half * (k + xm)
            total = kzp + kzm + kyp + kym + kxp + kxm
            if self.closed:
                kyp, kym = jnp.where(iny, kyp, 0.0), jnp.where(inw, kym, 0.0)
            kxp, kxm = jnp.where(inx, kxp, 0.0), jnp.where(inm, kxm, 0.0)
            inside = k > 0.0
            diag = jnp.where(inside, total + F32(2.0 * COUPLE) * k, 1.0)
            weight = jnp.where(inside, F32(OMEGA) / diag, 0.0)
            p = self.plane(0, z)
            return [(self.coef[i], p, value) for i, value in
                    enumerate((kzp, kzm, kyp, kym, kxp, kxm, total + F32(COUPLE) * k, weight))]

        self.loop(low, high, body)

    def first(self, low, high, rhs, out, mask=None):
        def body(get, z):
            weight, todo = get(self.coef[7], 0, 0), []
            if mask is not None:
                weight = weight * get(mask, 0, 0)
                todo = [(self.coef[7], self.plane(0, z), weight)]
            return todo + [(out, self.plane(c, z), weight * get(rhs, c, 0)) for c in range(3)]

        self.loop(low, high, body)

    def defect(self, get, u, rhs):
        kzp, kzm, kyp, kym, kxp, kxm, own = [get(self.coef[i], 0, 0) for i in range(7)]
        couple = F32(COUPLE) * get(self.k, 0, 0)
        field = [get(u, c, 0) for c in range(3)]
        shared = couple * (field[0] + field[1] + field[2])
        out = []
        for c in range(3):
            v = field[c]
            zp, zm = self.z_sides(lambda off: get(u, c, off))
            near = (kzp * zp + kzm * zm) + (kyp * up(v) + kym * down(v))
            near = near + (kxp * left(v, self.xs) + kxm * right(v, self.xs))
            out.append((get(rhs, c, 0) - shared) + (near - own * v))
        return field, out

    def sweep(self, low, high, u, rhs, out, out_plane=None):
        place = out_plane or self.plane

        def body(get, z):
            field, delta = self.defect(get, u, rhs)
            weight = get(self.coef[7], 0, 0)
            return [(out, place(c, z), field[c] + weight * delta[c]) for c in range(3)]

        self.loop(low, high, body)

    def residual(self, low, high, u, rhs, mask, emit):
        def body(get, z):
            field, delta = self.defect(get, u, rhs)
            todo = []
            for c in range(3):
                value = delta[c] if mask is None else get(mask, 0, 0) * delta[c]
                todo += emit(c, z, value, field[c])
            return todo

        self.loop(low, high, body)


def kernel(ns, nc, g0, g1, ex, load_in, dens_in, moduli_in, fixed_in, out_u, out_r, *scratch):
    it = iter(scratch)
    take = lambda n: [next(it) for _ in range(n)]
    k0, m0, b0, ua, ub = take(5)
    c0 = take(8)
    k1, b1, va, vb = take(4)
    c1 = take(8)
    k2, b2, wa, wb, wf = take(5)
    c2 = take(8)
    k3, b3, xa, xb = take(4)
    c3 = take(8)
    gk, gb, stage = take(3)
    s, c = lax.axis_index("slab"), lax.axis_index("col")
    where = (s, c, ns, nc)
    rounds = []
    for grid, fields, pairs in ex:
        send, recv = take(8), take(8)
        ssem, rsem = take(2)
        rounds.append(Exchange(grid, fields, pairs, where, send, recv, ssem, rsem))
    ex_s, ex_a, ex_k, ex_b, ex_u, ex_v = rounds
    load, dens, moduli, fixed, arrived = take(5)
    fetches = [pltpu.make_async_copy(src, dst, arrived.at[i]) for i, (src, dst) in enumerate(
        ((dens_in, dens), (moduli_in, moduli), (fixed_in, fixed), (load_in, load)))]
    for fetch in fetches:
        fetch.start()
    n0, y0, n1, y1 = g0.nz, g0.ny, g1.nz, g1.ny

    def zero(ref):
        rows = ref.shape[0]
        ref[...] = jnp.zeros((rows, LANES), F32)

    barrier = pltpu.get_barrier_semaphore()

    def greet(a, b):
        target = (beside(s, a, ns), beside(c, b, nc))
        pl.semaphore_signal(barrier, inc=1, device_id=target, device_id_type=pl.DeviceIdType.MESH)

    others(ns, nc, greet)

    for ref in (k0, m0, b0, k1):
        zero(ref)

    wide = lambda v: jnp.concatenate(
        [jnp.zeros((g0.oy, LANES), F32), v, jnp.zeros((g0.oy, LANES), F32)], axis=0)
    own_plane = lambda comp, z: rows_of((comp * n0 + z) * y0, y0)

    def fill_stiffness(get, z):
        d = get(dens, 0, 0)
        value = jnp.zeros((y0, LANES), F32)
        for klass in range(CLASSES):
            value = jnp.where(d == klass, moduli[klass], value)
        return [(k0, g0.plane(0, z + g0.oz), wide(value))]

    def fill_rest(get, z):
        keep = 1.0 - get(fixed, 0, 0).astype(F32)
        return [(m0, g0.plane(0, z + g0.oz), wide(keep))] + [
            (b0, g0.plane(comp, z + g0.oz), wide(get(load, comp, 0))) for comp in range(3)]

    for fetch in fetches[:2]:
        fetch.wait()
    loop(0, n0, y0, own_plane, fill_stiffness)
    pl.semaphore_wait(barrier, ns * nc - 1)
    ex_s.start([k0])
    for fetch in fetches[2:]:
        fetch.wait()
    loop(0, n0, y0, own_plane, fill_rest)
    ex_a.start([m0, b0])

    def coarser(src, grid, comp, z, y, count, steps):
        total = None
        for dz in range(2):
            for dy in range(2):
                part = src[pl.ds(grid.row(comp, 2 * z + dz, 2 * y + dy), count, stride=2), :]
                total = part if total is None else total + part
        for step in steps:
            total = pair_sum(total, step)
        return total * F32(0.125)

    for z in range(n1):
        k1[pl.ds(g1.row(0, z, 0), y1), :] = coarser(k0, g0, 0, z, 0, y1, (1,))
    ex_k.start([k1])

    lane4 = lane_iota(4) % 4

    here = s * nc + c

    def packed(src, comp):
        value = jnp.zeros((4, LANES), F32)
        for z in range(n1 // 2):
            value = jnp.where(lane4 == z, coarser(src, g1, comp, z, 0, y1 // 2, (2,)), value)
        return value

    def gather(ref, comps, send_sem, recv_sem):
        own = pl.ds(here * comps, comps)

        def spread(a, b):
            pltpu.make_async_remote_copy(
                src_ref=ref.at[own], dst_ref=ref.at[own], send_sem=send_sem, recv_sem=recv_sem,
                device_id=(beside(s, a, ns), beside(c, b, nc)), device_id_type=pl.DeviceIdType.MESH).start()

        others(ns, nc, spread)
        rest = pl.ds(0, (ns * nc - 1) * comps)
        return pltpu.make_async_remote_copy(
            src_ref=ref.at[rest], dst_ref=ref.at[rest], send_sem=send_sem, recv_sem=recv_sem,
            device_id=(beside(s, 1, ns), c), device_id_type=pl.DeviceIdType.MESH)

    def assemble(ref, comps, out):
        def one(t, carry):
            z, pair = t // (nc // 2), t % (nc // 2)
            for comp in range(comps):
                value = jnp.concatenate([ref[2 * t * comps + comp], ref[(2 * t + 1) * comps + comp]], axis=0)
                out[rows_of((comp * (ns + 2) + z + 1) * y2 + pair * 8, 8), :] = value
            return carry

        if ns * nc <= 32:
            for t in range(ns * nc // 2):
                one(t, 0)
        else:
            lax.fori_loop(0, ns * nc // 2, one, 0)

    gk[here] = packed(k1, 0)
    all_k = gather(gk, 1, *take(2))
    for ref in (ua, ub, b1, va, vb):
        zero(ref)

    level0 = Level(1.0, 1, 0, 0, g0.y, False, g0.plane, k0, c0)
    level1 = Level(0.25, 2, 0, 0, g1.y, False, g1.plane, k1, c1)
    y2, y3 = 4 * nc, 2 * nc
    plane2 = lambda comp, z: rows_of((comp * (ns + 2) + z) * y2, y2)
    plane3 = lambda comp, z: rows_of((comp * (ns + 2) + z) * y3, y3)
    wide2 = lambda comp, z: rows_of((comp * (ns + 2) + z) * (y2 + 16) + 8, y2)
    level2 = Level(0.25**2, 4, 1, 4, y2, True, plane2, k2, c2)
    level3 = Level(0.25**3, 8, 2, 4, y3, True, plane3, k3, c3)
    for ref, comps, plane, rows in ((k2, 1, plane2, y2), (wa, 3, plane2, y2), (wb, 3, plane2, y2),
                                    (k3, 1, plane3, y3), (xa, 3, plane3, y3), (xb, 3, plane3, y3),
                                    (wf, 3, lambda comp, z: rows_of((comp * (ns + 2) + z) * (y2 + 16), y2 + 16), y2 + 16)):
        for comp in range(comps):
            for z in (0, ns + 1):
                ref[plane(comp, z), :] = jnp.zeros((rows, LANES), F32)

    ex_s.finish([k0])
    level0.setup(g0.oz - 2, g0.oz + n0 + 2)
    ex_a.finish([m0, b0])
    level0.first(g0.oz - 2, g0.oz + n0 + 2, b0, ua, m0)
    level0.sweep(g0.oz - 1, g0.oz + n0 + 1, ua, b0, ub)

    def keep0(comp, z, value, field):
        return [(ua, g0.plane(comp, z), value)]

    level0.residual(g0.oz, g0.oz + n0, ub, b0, m0, keep0)
    for comp in range(3):
        for z in range(n1):
            b1[pl.ds(g1.row(comp, z, 0), y1), :] = coarser(ua, g0, comp, z, 0, y1, (1,))
    ex_b.start([b1])

    ex_k.finish([k1])
    level1.setup(g1.oz - 3, g1.oz + n1 + 3)
    all_k.wait_recv()
    assemble(gk, 1, k2)
    level2.setup(1, ns + 1)

    def shrink3(pairs):
        def body(z, carry):
            for src, dst, comp in pairs:
                start = (comp * (ns + 2) + z) * y2
                total = src[pl.ds(start, y3, stride=2), :] + src[pl.ds(start + 1, y3, stride=2), :]
                dst[plane3(comp, z), :] = pair_sum(pair_sum(total, 1), 4) * F32(0.125)
            return carry

        if ns <= 4:
            for z in range(1, ns + 1):
                body(z, 0)
        else:
            lax.fori_loop(1, ns + 1, body, 0)

    shrink3([(k2, k3, 0)])
    level3.setup(1, ns + 1)
    ex_b.finish([b1])
    ex_u.start([ub, m0])
    level1.first(g1.oz - 2, g1.oz + n1 + 2, b1, va)
    level1.sweep(g1.oz - 1, g1.oz + n1 + 1, va, b1, vb)

    ex_v.start([vb])

    def keep1(comp, z, value, field):
        return [(va, g1.plane(comp, z), value)]

    level1.residual(g1.oz, g1.oz + n1, vb, b1, None, keep1)
    for comp in range(3):
        gb[here * 3 + comp] = packed(va, comp)
    all_b = gather(gb, 3, *take(2))
    ex_u.finish([ub, m0])
    ex_v.finish([vb])
    all_k.wait_send()
    for ex_one in rounds:
        ex_one.drain()

    all_b.wait_recv()
    assemble(gb, 3, b2)
    level2.first(1, ns + 1, b2, wa)
    level2.sweep(1, ns + 1, wa, b2, wb)

    def keep2(comp, z, value, field):
        return [(wa, plane2(comp, z), value)]

    level2.residual(1, ns + 1, wb, b2, None, keep2)

    shrink3([(wa, b3, comp) for comp in range(3)])
    level3.first(1, ns + 1, b3, xa)
    old, new = xa, xb
    for turn in range(COARSE_SWEEPS - 1):
        level3.sweep(1, ns + 1, old, b3, new)
        old, new = new, old
    coarse = old

    def twice(value, slot):
        rows = value.shape[0]
        stage[pl.ds(slot, rows, stride=2), :] = value
        stage[pl.ds(slot + 1, rows, stride=2), :] = value
        return slot, 2 * rows

    def staged(spot):
        return stage[pl.ds(spot[0], spot[1]), :]

    def add2(z, carry):
        spots = [twice(coarse[plane3(comp, z), :], comp * y2) for comp in range(3)]
        for comp in range(3):
            p = plane2(comp, z)
            wb[p, :] = wb[p, :] + staged(spots[comp])
        return carry

    lax.fori_loop(1, ns + 1, add2, 0)

    level2.sweep(1, ns + 1, wb, b2, wa)
    level2.sweep(1, ns + 1, wa, b2, wf, wide2)

    lane8 = lane_iota(8)
    odd = c % 2 == 1

    for i in range(g1.z // 2):
        block, j = s + (i + 2) // 4, (i + 2) % 4
        spots = []
        for comp in range(3):
            at = (comp * (ns + 2) + block) * (y2 + 16) + (c // 2) * 8
            rows = wf[pl.ds(pl.multiple_of(at, 8), 24), :]
            value = jnp.where(odd, rows[10:18], rows[6:14])
            value = jnp.where(lane8 % 4 == j, value, 0.0)
            spots.append(twice(pair_sum(pair_sum(value, 1), 2), (i % 2 * 3 + comp) * 16))
        for comp in range(3):
            grown = staged(spots[comp])
            for dz in range(2):
                p = g1.plane(comp, 2 * i + dz)
                inside = k1[g1.plane(0, 2 * i + dz), :] > 0.0
                va[p, :] = vb[p, :] + jnp.where(inside, grown, 0.0)
    level1.sweep(g1.oz - 3, g1.oz + n1 + 3, va, b1, vb)
    level1.sweep(g1.oz - 2, g1.oz + n1 + 2, vb, b1, va)

    def add0(i, carry):
        spots = [twice(va[g1.plane(comp, i + g1.oz - 2), :][2:14], comp * g0.y) for comp in range(3)]
        for comp in range(3):
            grown = staged(spots[comp])
            for dz in range(2):
                p = g0.plane(comp, 2 * i + dz)
                ua[p, :] = ub[p, :] + m0[g0.plane(0, 2 * i + dz), :] * grown
        return carry

    lax.fori_loop(0, g0.z // 2, add0, 0)
    level0.sweep(g0.oz - 2, g0.oz + n0 + 2, ua, b0, ub)
    level0.sweep(g0.oz - 1, g0.oz + n0 + 1, ub, b0, ua)

    def emit(comp, z, value, field):
        at = pl.ds(pl.multiple_of((comp * n0 + z - g0.oz) * y0, 8), y0)
        own = slice(g0.oy, g0.oy + y0)
        return [(out_r, at, value[own]), (out_u, at, field[own])]

    level0.residual(g0.oz, g0.oz + n0, ua, b0, m0, emit)

    all_b.wait_send()


def hand_over(u, r, out_u, out_r, sems):
    copies = [pltpu.make_async_copy(src, dst, sems.at[i]) for i, (src, dst) in enumerate(((u, out_u), (r, out_r)))]
    for one in copies:
        one.start()
    for one in copies:
        one.wait()


def on_device(ns, nc, load, density, moduli, fixed):
    _, nz, ny, nx = load.shape
    g0 = Grid(nz, ny, 4, 4)
    g1 = Grid(nz // 2, ny // 2, 4, 4)
    ex = (
        (g0, ((1, 1, 3),), False),
        (g0, ((1, 1, 2), (3, 1, 2)), False),
        (g1, ((1, 1, 4),), True),
        (g1, ((3, 1, 3),), True),
        (g0, ((3, 2, 3), (1, 3, 3)), False),
        (g1, ((3, 2, 4),), True),
    )
    buf = lambda rows: pltpu.VMEM((rows, LANES), F32)
    y2, y3 = 4 * nc, 2 * nc
    s2, s3 = (ns + 2) * y2, (ns + 2) * y3
    scratch = [buf(g0.rows)] * 2 + [buf(3 * g0.rows)] * 3 + [buf(g0.rows)] * 8
    scratch += [buf(g1.rows)] + [buf(3 * g1.rows)] * 3 + [buf(g1.rows)] * 8
    scratch += [buf(s2)] + [buf(3 * s2)] * 3 + [buf(3 * (ns + 2) * (y2 + 16))] + [buf(s2)] * 8
    scratch += [buf(s3)] + [buf(3 * s3)] * 3 + [buf(s3)] * 8
    scratch += [pltpu.VMEM((ns * nc, 4, LANES), F32), pltpu.VMEM((ns * nc * 3, 4, LANES), F32), buf(3 * max(y2, 32))]
    for grid, fields, pairs in ex:
        sizes = [message(grid, dz, dy, fields, pairs)[1] for dz, dy in DIRS]
        scratch += [buf(n) for n in sizes] * 2
        scratch += [pltpu.SemaphoreType.DMA((8,))] * 2

    def run(*args):
        kernel(ns, nc, g0, g1, ex, *args)

    rows = 3 * nz * ny
    scratch += [buf(rows), pltpu.VMEM((nz * ny, LANES), jnp.int32), pltpu.SMEM((CLASSES,), F32),
                pltpu.VMEM((nz * ny, LANES), jnp.int32), pltpu.SemaphoreType.DMA((4,))]
    scratch += [pltpu.SemaphoreType.DMA] * 4
    used = sum(4 * math.prod(ref.shape) for ref in scratch if hasattr(ref, "shape"))
    vmem = pl.BlockSpec(memory_space=pltpu.VMEM)
    u, r = pl.pallas_call(
        run,
        out_shape=[jax.ShapeDtypeStruct((rows, nx), F32)] * 2,
        in_specs=[pl.BlockSpec(memory_space=pltpu.HBM)] * 4,
        out_specs=[vmem, vmem],
        scratch_shapes=scratch,
        compiler_params=pltpu.CompilerParams(collective_id=0, has_side_effects=True, vmem_limit_bytes=used + 8 * 1024 * 1024),
        name="vcycle",
    )(*[pltpu.with_memory_space_constraint(a, pltpu.HBM) for a in (
        load.reshape(rows, nx), density.reshape(nz * ny, nx), moduli, fixed.reshape(nz * ny, nx))])
    both = pl.BlockSpec(memory_space=pltpu.HBM)
    u, r = pl.pallas_call(
        hand_over,
        out_shape=[jax.ShapeDtypeStruct((rows, nx), F32)] * 2,
        in_specs=[vmem, vmem],
        out_specs=[both, both],
        scratch_shapes=[pltpu.SemaphoreType.DMA((2,))],
        name="hand_over",
    )(*[pltpu.with_memory_space_constraint(a, pltpu.VMEM) for a in (u, r)])
    shape = (3, nz, ny, nx)
    return u.reshape(shape), r.reshape(shape)


def solution(mesh):
    ns, nc = mesh.shape["slab"], mesh.shape["col"]
    placed = (P(None, "slab", "col", None), P("slab", "col", None), P(), P("slab", "col", None))

    def body(load, density, moduli, fixed):
        return on_device(ns, nc, load, density, moduli, fixed)

    return jax.shard_map(
        body,
        mesh=mesh,
        in_specs=placed,
        out_specs=(P(None, "slab", "col", None), P(None, "slab", "col", None)),
        check_vma=False,
    )
```

```python
import math

import jax
import jax.numpy as jnp
from jax import lax
from jax.experimental import pallas as pl
from jax.experimental.pallas import tpu as pltpu
from jax.sharding import PartitionSpec as P

OMEGA = 0.6
COUPLE = 0.05
CLASSES = 8
COARSE_SWEEPS = 8
LANES = 128
F32 = jnp.float32
LIVE = 36
DIRS = ((0, 1), (0, -1), (1, 0), (-1, 0), (1, 1), (1, -1), (-1, 1), (-1, -1))


class Grid:
    def __init__(self, nz, ny, oz, oy):
        self.nz, self.ny, self.oz, self.oy = nz, ny, oz, oy
        self.z, self.y = nz + 2 * oz, ny + 2 * oy
        self.rows = self.z * self.y

    def row(self, comp, z, y):
        return comp * self.rows + (z + self.oz) * self.y + y + self.oy

    def plane(self, comp, z):
        start = comp * self.rows + z * self.y
        if not isinstance(start, int):
            start = pl.multiple_of(start, 8)
        return pl.ds(start, self.y)


def segments(grid, dz, dy, low, depth):
    nz, ny = grid.nz, grid.ny

    def cell(step, d, n):
        return (n - step, -step) if d > 0 else (step - 1, n - 1 + step)

    out = []
    if dz == 0:
        for i in range(low, depth + 1):
            mine, there = cell(i, dy, ny)
            out.append((0, mine, 0, there, nz, True))
    elif dy == 0:
        for i in range(low, depth + 1):
            mine, there = cell(i, dz, nz)
            out.append((mine, 0, there, 0, ny, False))
    else:
        for i in range(1, depth):
            for j in range(max(1, low - i), depth + 1 - i):
                mz, tz = cell(i, dz, nz)
                my, ty = cell(j, dy, ny)
                out.append((mz, my, tz, ty, 1, False))
    return out


def message(grid, dz, dy, fields, pairs):
    runs = [(field, comp, seg) for field, (comps, low, depth) in enumerate(fields) for comp in range(comps)
            for seg in segments(grid, dz, dy, low, depth)]
    width = 2 if pairs else 1
    out, at = [], 0
    for first in range(0, len(runs), width):
        part = runs[first:first + width]
        out.append((part, at))
        at += part[0][2][4]
    return out, -(-at // 8) * 8


def window(grid, comp, z, y, count, along_z):
    start = grid.row(comp, z, y)
    if along_z:
        return pl.ds(start, count, stride=grid.y)
    return pl.ds(start, count)


def beside(here, step, count):
    if not isinstance(step, int):
        return lax.rem(here + step, count)
    if step == 0:
        return here
    if step > 0:
        return jnp.where(here >= count - step, here + (step - count), here + step)
    return jnp.where(here < -step, here + (step + count), here + step)


def others(ns, nc, body):
    if ns * nc <= 32:
        for a in range(ns):
            for b in range(nc):
                if a or b:
                    body(a, b)
        return

    def one(t, carry):
        body(t // nc, t % nc)
        return carry

    lax.fori_loop(1, ns * nc, one, 0)


class Exchange:
    def __init__(self, grid, fields, pairs, where, send, recv, ssem, rsem):
        self.grid, self.fields, self.pairs, self.where = grid, fields, pairs, where
        self.send, self.recv, self.ssem, self.rsem = send, recv, ssem, rsem

    def copy(self, d):
        dz, dy = DIRS[d]
        s, c, ns, nc = self.where
        target = (beside(s, dz, ns), beside(c, dy, nc))
        return pltpu.make_async_remote_copy(
            src_ref=self.send[d], dst_ref=self.recv[d], send_sem=self.ssem.at[d], recv_sem=self.rsem.at[d],
            device_id=target, device_id_type=pl.DeviceIdType.MESH)

    def exists(self, dz, dy):
        s, c, ns, nc = self.where
        ok = None
        for here, d, n in ((s, dz, ns), (c, dy, nc)):
            if d:
                near = here < n - 1 if d > 0 else here > 0
                ok = near if ok is None else jnp.logical_and(ok, near)
        return ok

    def start(self, refs):
        for d, (dz, dy) in enumerate(DIRS):
            parts, _ = message(self.grid, dz, dy, self.fields, self.pairs)
            for runs, at in parts:
                values = [refs[field][window(self.grid, comp, z, y, count, along), :]
                          for field, comp, (z, y, _, _, count, along) in runs]
                value = values[0]
                if len(values) == 2:
                    value = jnp.where(lane_iota(value.shape[0]) % 2 == 0, value, values[1])
                self.send[d][pl.ds(at, value.shape[0]), :] = value
        for d, (dz, dy) in enumerate(DIRS):
            @pl.when(self.exists(dz, dy))
            def _():
                self.copy(d).start()

    def finish(self, refs):
        for d, (dz, dy) in enumerate(DIRS):
            @pl.when(self.exists(-dz, -dy))
            def _():
                self.copy(d).wait_recv()
        for d, (dz, dy) in enumerate(DIRS):
            parts, _ = message(self.grid, dz, dy, self.fields, self.pairs)
            here = self.exists(-dz, -dy)
            for runs, at in parts:
                value = jnp.where(here, self.recv[d][pl.ds(at, runs[0][2][4]), :], 0.0)
                values = [value]
                if len(runs) == 2:
                    even = lane_iota(value.shape[0]) % 2 == 0
                    values = [jnp.where(even, value, right(value, 1)), jnp.where(even, left(value, 1), value)]
                for (field, comp, (_, _, z, y, count, along)), value in zip(runs, values):
                    refs[field][window(self.grid, comp, z, y, count, along), :] = value

    def drain(self):
        for d, (dz, dy) in enumerate(DIRS):
            @pl.when(self.exists(dz, dy))
            def _():
                self.copy(d).wait_send()


def lane_iota(rows):
    return lax.broadcasted_iota(jnp.int32, (rows, LANES), 1)


def right(v, step):
    return pltpu.roll(v, step % LANES, 1)


def left(v, step):
    return pltpu.roll(v, LANES - step, 1)


def down(v):
    return pltpu.roll(v, 1, 0)


def up(v):
    return pltpu.roll(v, v.shape[0] - 1, 0)


def pair_sum(v, step):
    lane = lane_iota(v.shape[0])
    first = lane % (2 * step) < step
    return v + jnp.where(first, left(v, step), right(v, step))


def rows_of(start, count):
    if not isinstance(start, int):
        start = pl.multiple_of(start, 8)
    return pl.ds(start, count)


def loop(low, high, rows, plane, body):
    count = high - low
    unit = max(u for u in range(1, count + 1) if count % u == 0 and (u == 1 or 3 * u * rows <= 8 * LIVE))

    def step(i, carry):
        base = low + i * unit
        held, todo = {}, []

        def get(ref, comp, off):
            key = (id(ref), comp, off)
            if key not in held:
                held[key] = ref[plane(comp, base + off), :]
            return held[key]

        for j in range(unit):
            todo += body(lambda ref, comp, off, j=j: get(ref, comp, off + j), base + j)
        for ref, at, value in todo:
            ref[at, :] = value
        return carry

    if count == unit:
        step(0, 0)
    else:
        lax.fori_loop(0, count // unit, step, 0)


class Level:
    def __init__(self, scale, xs, zs, group, ny, closed, plane, k, coef):
        self.scale, self.xs, self.zs, self.group, self.ny, self.closed = scale, xs, zs, group, ny, closed
        self.plane, self.k, self.coef = plane, k, coef

    def loop(self, low, high, body):
        loop(low, high, self.ny, self.plane, body)

    def z_sides(self, get):
        after, before = get(1), get(-1)
        if not self.group:
            return after, before
        here = get(0)
        lane = lane_iota(self.ny) % self.group
        turn = self.group - self.zs
        return (jnp.where(lane < turn, left(here, self.zs), right(after, turn)),
                jnp.where(lane >= self.zs, right(here, self.zs), left(before, turn)))

    def setup(self, low, high):
        def body(get, z):
            k = get(self.k, 0, 0)
            lane = lane_iota(self.ny)
            zp, zm = self.z_sides(lambda off: get(self.k, 0, off))
            inx = lane < LANES - self.xs
            inm = lane >= self.xs
            xp = jnp.where(inx, left(k, self.xs), 0.0)
            xm = jnp.where(inm, right(k, self.xs), 0.0)
            yp, ym = up(k), down(k)
            half = F32(0.5 * self.scale)
            if self.closed:
                row = lax.broadcasted_iota(jnp.int32, (self.ny, LANES), 0)
                iny, inw = row < self.ny - 1, row >= 1
                yp, ym = jnp.where(iny, yp, 0.0), jnp.where(inw, ym, 0.0)
            kzp, kzm = half * (k + zp), half * (k + zm)
            kyp, kym = half * (k + yp), half * (k + ym)
            kxp, kxm = half * (k + xp), half * (k + xm)
            total = kzp + kzm + kyp + kym + kxp + kxm
            if self.closed:
                kyp, kym = jnp.where(iny, kyp, 0.0), jnp.where(inw, kym, 0.0)
            kxp, kxm = jnp.where(inx, kxp, 0.0), jnp.where(inm, kxm, 0.0)
            inside = k > 0.0
            diag = jnp.where(inside, total + F32(2.0 * COUPLE) * k, 1.0)
            weight = jnp.where(inside, F32(OMEGA) / diag, 0.0)
            p = self.plane(0, z)
            return [(self.coef[i], p, value) for i, value in
                    enumerate((kzp, kzm, kyp, kym, kxp, kxm, total + F32(COUPLE) * k, weight))]

        self.loop(low, high, body)

    def first(self, low, high, rhs, out, mask=None):
        def body(get, z):
            weight, todo = get(self.coef[7], 0, 0), []
            if mask is not None:
                weight = weight * get(mask, 0, 0)
                todo = [(self.coef[7], self.plane(0, z), weight)]
            return todo + [(out, self.plane(c, z), weight * get(rhs, c, 0)) for c in range(3)]

        self.loop(low, high, body)

    def defect(self, get, u, rhs):
        kzp, kzm, kyp, kym, kxp, kxm, own = [get(self.coef[i], 0, 0) for i in range(7)]
        couple = F32(COUPLE) * get(self.k, 0, 0)
        field = [get(u, c, 0) for c in range(3)]
        shared = couple * (field[0] + field[1] + field[2])
        out = []
        for c in range(3):
            v = field[c]
            zp, zm = self.z_sides(lambda off: get(u, c, off))
            near = (kzp * zp + kzm * zm) + (kyp * up(v) + kym * down(v))
            near = near + (kxp * left(v, self.xs) + kxm * right(v, self.xs))
            out.append((get(rhs, c, 0) - shared) + (near - own * v))
        return field, out

    def sweep(self, low, high, u, rhs, out, out_plane=None):
        place = out_plane or self.plane

        def body(get, z):
            field, delta = self.defect(get, u, rhs)
            weight = get(self.coef[7], 0, 0)
            return [(out, place(c, z), field[c] + weight * delta[c]) for c in range(3)]

        self.loop(low, high, body)

    def residual(self, low, high, u, rhs, mask, emit):
        def body(get, z):
            field, delta = self.defect(get, u, rhs)
            todo = []
            for c in range(3):
                value = delta[c] if mask is None else get(mask, 0, 0) * delta[c]
                todo += emit(c, z, value, field[c])
            return todo

        self.loop(low, high, body)


def kernel(ns, nc, g0, g1, ex, load_in, dens_in, moduli_in, fixed_in, out_u, out_r, *scratch):
    it = iter(scratch)
    take = lambda n: [next(it) for _ in range(n)]
    k0, m0, b0, ua, ub = take(5)
    c0 = take(8)
    k1, b1, va, vb = take(4)
    c1 = take(8)
    k2, b2, wa, wb, wf = take(5)
    c2 = take(8)
    k3, b3, xa, xb = take(4)
    c3 = take(8)
    gk, gb, stage = take(3)
    s, c = lax.axis_index("slab"), lax.axis_index("col")
    where = (s, c, ns, nc)
    rounds = []
    for grid, fields, pairs in ex:
        send, recv = take(8), take(8)
        ssem, rsem = take(2)
        rounds.append(Exchange(grid, fields, pairs, where, send, recv, ssem, rsem))
    ex_s, ex_a, ex_k, ex_b, ex_u, ex_v = rounds
    load, dens, moduli, fixed, arrived = take(5)
    fetches = [pltpu.make_async_copy(src, dst, arrived.at[i]) for i, (src, dst) in enumerate(
        ((dens_in, dens), (moduli_in, moduli), (fixed_in, fixed), (load_in, load)))]
    for fetch in fetches:
        fetch.start()
    n0, y0, n1, y1 = g0.nz, g0.ny, g1.nz, g1.ny

    def zero(ref):
        rows = ref.shape[0]
        ref[...] = jnp.zeros((rows, LANES), F32)

    barrier = pltpu.get_barrier_semaphore()

    def greet(a, b):
        target = (beside(s, a, ns), beside(c, b, nc))
        pl.semaphore_signal(barrier, inc=1, device_id=target, device_id_type=pl.DeviceIdType.MESH)

    others(ns, nc, greet)

    for ref in (k0, m0, b0, k1):
        zero(ref)

    wide = lambda v: jnp.concatenate(
        [jnp.zeros((g0.oy, LANES), F32), v, jnp.zeros((g0.oy, LANES), F32)], axis=0)
    own_plane = lambda comp, z: rows_of((comp * n0 + z) * y0, y0)

    def fill_stiffness(get, z):
        d = get(dens, 0, 0)
        value = jnp.zeros((y0, LANES), F32)
        for klass in range(CLASSES):
            value = jnp.where(d == klass, moduli[klass], value)
        return [(k0, g0.plane(0, z + g0.oz), wide(value))]

    def fill_rest(get, z):
        keep = 1.0 - get(fixed, 0, 0).astype(F32)
        return [(m0, g0.plane(0, z + g0.oz), wide(keep))] + [
            (b0, g0.plane(comp, z + g0.oz), wide(get(load, comp, 0))) for comp in range(3)]

    for fetch in fetches[:2]:
        fetch.wait()
    loop(0, n0, y0, own_plane, fill_stiffness)
    pl.semaphore_wait(barrier, ns * nc - 1)
    ex_s.start([k0])
    for fetch in fetches[2:]:
        fetch.wait()
    loop(0, n0, y0, own_plane, fill_rest)
    ex_a.start([m0, b0])

    def coarser(src, grid, comp, z, y, count, steps):
        total = None
        for dz in range(2):
            for dy in range(2):
                part = src[pl.ds(grid.row(comp, 2 * z + dz, 2 * y + dy), count, stride=2), :]
                total = part if total is None else total + part
        for step in steps:
            total = pair_sum(total, step)
        return total * F32(0.125)

    for z in range(n1):
        k1[pl.ds(g1.row(0, z, 0), y1), :] = coarser(k0, g0, 0, z, 0, y1, (1,))
    ex_k.start([k1])

    lane4 = lane_iota(4) % 4

    here = s * nc + c

    def packed(src, comp):
        value = jnp.zeros((4, LANES), F32)
        for z in range(n1 // 2):
            value = jnp.where(lane4 == z, coarser(src, g1, comp, z, 0, y1 // 2, (2,)), value)
        return value

    def gather(ref, comps, send_sem, recv_sem):
        own = pl.ds(here * comps, comps)

        def spread(a, b):
            pltpu.make_async_remote_copy(
                src_ref=ref.at[own], dst_ref=ref.at[own], send_sem=send_sem, recv_sem=recv_sem,
                device_id=(beside(s, a, ns), beside(c, b, nc)), device_id_type=pl.DeviceIdType.MESH).start()

        others(ns, nc, spread)
        rest = pl.ds(0, (ns * nc - 1) * comps)
        return pltpu.make_async_remote_copy(
            src_ref=ref.at[rest], dst_ref=ref.at[rest], send_sem=send_sem, recv_sem=recv_sem,
            device_id=(beside(s, 1, ns), c), device_id_type=pl.DeviceIdType.MESH)

    def assemble(ref, comps, out):
        def one(t, carry):
            z, pair = t // (nc // 2), t % (nc // 2)
            for comp in range(comps):
                value = jnp.concatenate([ref[2 * t * comps + comp], ref[(2 * t + 1) * comps + comp]], axis=0)
                out[rows_of((comp * (ns + 2) + z + 1) * y2 + pair * 8, 8), :] = value
            return carry

        if ns * nc <= 32:
            for t in range(ns * nc // 2):
                one(t, 0)
        else:
            lax.fori_loop(0, ns * nc // 2, one, 0)

    level0 = Level(1.0, 1, 0, 0, g0.y, False, g0.plane, k0, c0)
    level1 = Level(0.25, 2, 0, 0, g1.y, False, g1.plane, k1, c1)
    y2, y3 = 4 * nc, 2 * nc
    plane2 = lambda comp, z: rows_of((comp * (ns + 2) + z) * y2, y2)
    plane3 = lambda comp, z: rows_of((comp * (ns + 2) + z) * y3, y3)
    wide2 = lambda comp, z: rows_of((comp * (ns + 2) + z) * (y2 + 16) + 8, y2)
    level2 = Level(0.25**2, 4, 1, 4, y2, True, plane2, k2, c2)
    level3 = Level(0.25**3, 8, 2, 4, y3, True, plane3, k3, c3)
    ex_s.finish([k0])
    level0.setup(g0.oz - 2, g0.oz + n0 + 2)
    gk[here] = packed(k1, 0)
    all_k = gather(gk, 1, *take(2))
    for ref in (ua, ub, b1, va, vb):
        zero(ref)
    for ref, comps, plane, rows in ((k2, 1, plane2, y2), (wa, 3, plane2, y2), (wb, 3, plane2, y2),
                                    (k3, 1, plane3, y3), (xa, 3, plane3, y3), (xb, 3, plane3, y3),
                                    (wf, 3, lambda comp, z: rows_of((comp * (ns + 2) + z) * (y2 + 16), y2 + 16), y2 + 16)):
        for comp in range(comps):
            for z in (0, ns + 1):
                ref[plane(comp, z), :] = jnp.zeros((rows, LANES), F32)
    ex_a.finish([m0, b0])
    level0.first(g0.oz - 2, g0.oz + n0 + 2, b0, ua, m0)
    level0.sweep(g0.oz - 1, g0.oz + n0 + 1, ua, b0, ub)

    def keep0(comp, z, value, field):
        return [(ua, g0.plane(comp, z), value)]

    level0.residual(g0.oz, g0.oz + n0, ub, b0, m0, keep0)
    for comp in range(3):
        for z in range(n1):
            b1[pl.ds(g1.row(comp, z, 0), y1), :] = coarser(ua, g0, comp, z, 0, y1, (1,))
    ex_b.start([b1])

    ex_k.finish([k1])
    level1.setup(g1.oz - 3, g1.oz + n1 + 3)
    all_k.wait_recv()
    assemble(gk, 1, k2)
    level2.setup(1, ns + 1)

    def shrink3(pairs):
        def body(z, carry):
            for src, dst, comp in pairs:
                start = (comp * (ns + 2) + z) * y2
                total = src[pl.ds(start, y3, stride=2), :] + src[pl.ds(start + 1, y3, stride=2), :]
                dst[plane3(comp, z), :] = pair_sum(pair_sum(total, 1), 4) * F32(0.125)
            return carry

        if ns <= 4:
            for z in range(1, ns + 1):
                body(z, 0)
        else:
            lax.fori_loop(1, ns + 1, body, 0)

    shrink3([(k2, k3, 0)])
    level3.setup(1, ns + 1)
    ex_u.start([ub, m0])
    ex_b.finish([b1])
    level1.first(g1.oz - 2, g1.oz + n1 + 2, b1, va)
    level1.sweep(g1.oz - 1, g1.oz + n1 + 1, va, b1, vb)

    ex_v.start([vb])

    def keep1(comp, z, value, field):
        return [(va, g1.plane(comp, z), value)]

    level1.residual(g1.oz, g1.oz + n1, vb, b1, None, keep1)
    for comp in range(3):
        gb[here * 3 + comp] = packed(va, comp)
    all_b = gather(gb, 3, *take(2))
    ex_u.finish([ub, m0])
    ex_v.finish([vb])
    all_k.wait_send()
    for ex_one in rounds:
        ex_one.drain()

    all_b.wait_recv()
    assemble(gb, 3, b2)
    level2.first(1, ns + 1, b2, wa)
    level2.sweep(1, ns + 1, wa, b2, wb)

    def keep2(comp, z, value, field):
        return [(wa, plane2(comp, z), value)]

    level2.residual(1, ns + 1, wb, b2, None, keep2)

    shrink3([(wa, b3, comp) for comp in range(3)])
    level3.first(1, ns + 1, b3, xa)
    old, new = xa, xb
    for turn in range(COARSE_SWEEPS - 1):
        level3.sweep(1, ns + 1, old, b3, new)
        old, new = new, old
    coarse = old

    def twice(value, slot):
        rows = value.shape[0]
        stage[pl.ds(slot, rows, stride=2), :] = value
        stage[pl.ds(slot + 1, rows, stride=2), :] = value
        return slot, 2 * rows

    def staged(spot):
        return stage[pl.ds(spot[0], spot[1]), :]

    def add2(z, carry):
        spots = [twice(coarse[plane3(comp, z), :], comp * y2) for comp in range(3)]
        for comp in range(3):
            p = plane2(comp, z)
            wb[p, :] = wb[p, :] + staged(spots[comp])
        return carry

    lax.fori_loop(1, ns + 1, add2, 0)

    level2.sweep(1, ns + 1, wb, b2, wa)
    level2.sweep(1, ns + 1, wa, b2, wf, wide2)

    lane8 = lane_iota(8)
    odd = c % 2 == 1

    for i in range(g1.z // 2):
        block, j = s + (i + 2) // 4, (i + 2) % 4
        spots = []
        for comp in range(3):
            at = (comp * (ns + 2) + block) * (y2 + 16) + (c // 2) * 8
            rows = wf[pl.ds(pl.multiple_of(at, 8), 24), :]
            value = jnp.where(odd, rows[10:18], rows[6:14])
            value = jnp.where(lane8 % 4 == j, value, 0.0)
            spots.append(twice(pair_sum(pair_sum(value, 1), 2), (i % 2 * 3 + comp) * 16))
        for comp in range(3):
            grown = staged(spots[comp])
            for dz in range(2):
                p = g1.plane(comp, 2 * i + dz)
                inside = k1[g1.plane(0, 2 * i + dz), :] > 0.0
                va[p, :] = vb[p, :] + jnp.where(inside, grown, 0.0)
    level1.sweep(g1.oz - 3, g1.oz + n1 + 3, va, b1, vb)
    level1.sweep(g1.oz - 2, g1.oz + n1 + 2, vb, b1, va)

    def add0(i, carry):
        spots = [twice(va[g1.plane(comp, i + g1.oz - 2), :][2:14], comp * g0.y) for comp in range(3)]
        for comp in range(3):
            grown = staged(spots[comp])
            for dz in range(2):
                p = g0.plane(comp, 2 * i + dz)
                ua[p, :] = ub[p, :] + m0[g0.plane(0, 2 * i + dz), :] * grown
        return carry

    lax.fori_loop(0, g0.z // 2, add0, 0)
    level0.sweep(g0.oz - 2, g0.oz + n0 + 2, ua, b0, ub)
    level0.sweep(g0.oz - 1, g0.oz + n0 + 1, ub, b0, ua)

    def emit(comp, z, value, field):
        at = pl.ds(pl.multiple_of((comp * n0 + z - g0.oz) * y0, 8), y0)
        own = slice(g0.oy, g0.oy + y0)
        return [(out_r, at, value[own]), (out_u, at, field[own])]

    level0.residual(g0.oz, g0.oz + n0, ua, b0, m0, emit)

    all_b.wait_send()


def hand_over(u, r, out_u, out_r, sems):
    copies = [pltpu.make_async_copy(src, dst, sems.at[i]) for i, (src, dst) in enumerate(((u, out_u), (r, out_r)))]
    for one in copies:
        one.start()
    for one in copies:
        one.wait()


def on_device(ns, nc, load, density, moduli, fixed):
    _, nz, ny, nx = load.shape
    g0 = Grid(nz, ny, 4, 4)
    g1 = Grid(nz // 2, ny // 2, 4, 4)
    ex = (
        (g0, ((1, 1, 3),), False),
        (g0, ((1, 1, 2), (3, 1, 2)), False),
        (g1, ((1, 1, 4),), True),
        (g1, ((3, 1, 3),), True),
        (g0, ((3, 2, 3), (1, 3, 3)), False),
        (g1, ((3, 2, 4),), True),
    )
    buf = lambda rows: pltpu.VMEM((rows, LANES), F32)
    y2, y3 = 4 * nc, 2 * nc
    s2, s3 = (ns + 2) * y2, (ns + 2) * y3
    scratch = [buf(g0.rows)] * 2 + [buf(3 * g0.rows)] * 3 + [buf(g0.rows)] * 8
    scratch += [buf(g1.rows)] + [buf(3 * g1.rows)] * 3 + [buf(g1.rows)] * 8
    scratch += [buf(s2)] + [buf(3 * s2)] * 3 + [buf(3 * (ns + 2) * (y2 + 16))] + [buf(s2)] * 8
    scratch += [buf(s3)] + [buf(3 * s3)] * 3 + [buf(s3)] * 8
    scratch += [pltpu.VMEM((ns * nc, 4, LANES), F32), pltpu.VMEM((ns * nc * 3, 4, LANES), F32), buf(3 * max(y2, 32))]
    for grid, fields, pairs in ex:
        sizes = [message(grid, dz, dy, fields, pairs)[1] for dz, dy in DIRS]
        scratch += [buf(n) for n in sizes] * 2
        scratch += [pltpu.SemaphoreType.DMA((8,))] * 2

    def run(*args):
        kernel(ns, nc, g0, g1, ex, *args)

    rows = 3 * nz * ny
    scratch += [buf(rows), pltpu.VMEM((nz * ny, LANES), jnp.int32), pltpu.SMEM((CLASSES,), F32),
                pltpu.VMEM((nz * ny, LANES), jnp.int32), pltpu.SemaphoreType.DMA((4,))]
    scratch += [pltpu.SemaphoreType.DMA] * 4
    used = sum(4 * math.prod(ref.shape) for ref in scratch if hasattr(ref, "shape"))
    vmem = pl.BlockSpec(memory_space=pltpu.VMEM)
    u, r = pl.pallas_call(
        run,
        out_shape=[jax.ShapeDtypeStruct((rows, nx), F32)] * 2,
        in_specs=[pl.BlockSpec(memory_space=pltpu.HBM)] * 4,
        out_specs=[vmem, vmem],
        scratch_shapes=scratch,
        compiler_params=pltpu.CompilerParams(collective_id=0, has_side_effects=True, vmem_limit_bytes=used + 8 * 1024 * 1024),
        name="vcycle",
    )(*[pltpu.with_memory_space_constraint(a, pltpu.HBM) for a in (
        load.reshape(rows, nx), density.reshape(nz * ny, nx), moduli, fixed.reshape(nz * ny, nx))])
    both = pl.BlockSpec(memory_space=pltpu.HBM)
    u, r = pl.pallas_call(
        hand_over,
        out_shape=[jax.ShapeDtypeStruct((rows, nx), F32)] * 2,
        in_specs=[vmem, vmem],
        out_specs=[both, both],
        scratch_shapes=[pltpu.SemaphoreType.DMA((2,))],
        name="hand_over",
    )(*[pltpu.with_memory_space_constraint(a, pltpu.VMEM) for a in (u, r)])
    shape = (3, nz, ny, nx)
    return u.reshape(shape), r.reshape(shape)


def solution(mesh):
    ns, nc = mesh.shape["slab"], mesh.shape["col"]
    placed = (P(None, "slab", "col", None), P("slab", "col", None), P(), P("slab", "col", None))

    def body(load, density, moduli, fixed):
        return on_device(ns, nc, load, density, moduli, fixed)

    return jax.shard_map(
        body,
        mesh=mesh,
        in_specs=placed,
        out_specs=(P(None, "slab", "col", None), P(None, "slab", "col", None)),
        check_vma=False,
    )
```

```python
import math

import jax
import jax.numpy as jnp
from jax import lax
from jax.experimental import pallas as pl
from jax.experimental.pallas import tpu as pltpu
from jax.sharding import PartitionSpec as P

OMEGA = 0.6
COUPLE = 0.05
CLASSES = 8
COARSE_SWEEPS = 8
LANES = 128
F32 = jnp.float32
LIVE = 48
DIRS = ((0, 1), (0, -1), (1, 0), (-1, 0), (1, 1), (1, -1), (-1, 1), (-1, -1))


class Grid:
    def __init__(self, nz, ny, oz, oy):
        self.nz, self.ny, self.oz, self.oy = nz, ny, oz, oy
        self.z, self.y = nz + 2 * oz, ny + 2 * oy
        self.rows = self.z * self.y

    def row(self, comp, z, y):
        return comp * self.rows + (z + self.oz) * self.y + y + self.oy

    def plane(self, comp, z):
        start = comp * self.rows + z * self.y
        if not isinstance(start, int):
            start = pl.multiple_of(start, 8)
        return pl.ds(start, self.y)


def segments(grid, dz, dy, low, depth):
    nz, ny = grid.nz, grid.ny

    def cell(step, d, n):
        return (n - step, -step) if d > 0 else (step - 1, n - 1 + step)

    out = []
    if dz == 0:
        for i in range(low, depth + 1):
            mine, there = cell(i, dy, ny)
            out.append((0, mine, 0, there, nz, True))
    elif dy == 0:
        for i in range(low, depth + 1):
            mine, there = cell(i, dz, nz)
            out.append((mine, 0, there, 0, ny, False))
    else:
        for i in range(1, depth):
            for j in range(max(1, low - i), depth + 1 - i):
                mz, tz = cell(i, dz, nz)
                my, ty = cell(j, dy, ny)
                out.append((mz, my, tz, ty, 1, False))
    return out


def message(grid, dz, dy, fields, pairs):
    runs = [(field, comp, seg) for field, (comps, low, depth) in enumerate(fields) for comp in range(comps)
            for seg in segments(grid, dz, dy, low, depth)]
    width = 2 if pairs else 1
    out, at = [], 0
    for first in range(0, len(runs), width):
        part = runs[first:first + width]
        out.append((part, at))
        at += part[0][2][4]
    return out, -(-at // 8) * 8


def window(grid, comp, z, y, count, along_z):
    start = grid.row(comp, z, y)
    if along_z:
        return pl.ds(start, count, stride=grid.y)
    return pl.ds(start, count)


def beside(here, step, count):
    if not isinstance(step, int):
        return lax.rem(here + step, count)
    if step == 0:
        return here
    if step > 0:
        return jnp.where(here >= count - step, here + (step - count), here + step)
    return jnp.where(here < -step, here + (step + count), here + step)


def others(ns, nc, body):
    if ns * nc <= 32:
        for a in range(ns):
            for b in range(nc):
                if a or b:
                    body(a, b)
        return

    def one(t, carry):
        body(t // nc, t % nc)
        return carry

    lax.fori_loop(1, ns * nc, one, 0)


class Exchange:
    def __init__(self, grid, fields, pairs, where, send, recv, ssem, rsem):
        self.grid, self.fields, self.pairs, self.where = grid, fields, pairs, where
        self.send, self.recv, self.ssem, self.rsem = send, recv, ssem, rsem

    def copy(self, d):
        dz, dy = DIRS[d]
        s, c, ns, nc = self.where
        target = (beside(s, dz, ns), beside(c, dy, nc))
        return pltpu.make_async_remote_copy(
            src_ref=self.send[d], dst_ref=self.recv[d], send_sem=self.ssem.at[d], recv_sem=self.rsem.at[d],
            device_id=target, device_id_type=pl.DeviceIdType.MESH)

    def exists(self, dz, dy):
        s, c, ns, nc = self.where
        ok = None
        for here, d, n in ((s, dz, ns), (c, dy, nc)):
            if d:
                near = here < n - 1 if d > 0 else here > 0
                ok = near if ok is None else jnp.logical_and(ok, near)
        return ok

    def start(self, refs):
        for d, (dz, dy) in enumerate(DIRS):
            parts, _ = message(self.grid, dz, dy, self.fields, self.pairs)
            for runs, at in parts:
                values = [refs[field][window(self.grid, comp, z, y, count, along), :]
                          for field, comp, (z, y, _, _, count, along) in runs]
                value = values[0]
                if len(values) == 2:
                    value = jnp.where(lane_iota(value.shape[0]) % 2 == 0, value, values[1])
                self.send[d][pl.ds(at, value.shape[0]), :] = value
        for d, (dz, dy) in enumerate(DIRS):
            @pl.when(self.exists(dz, dy))
            def _():
                self.copy(d).start()

    def finish(self, refs):
        for d, (dz, dy) in enumerate(DIRS):
            @pl.when(self.exists(-dz, -dy))
            def _():
                self.copy(d).wait_recv()
        for d, (dz, dy) in enumerate(DIRS):
            parts, _ = message(self.grid, dz, dy, self.fields, self.pairs)
            here = self.exists(-dz, -dy)
            for runs, at in parts:
                value = jnp.where(here, self.recv[d][pl.ds(at, runs[0][2][4]), :], 0.0)
                values = [value]
                if len(runs) == 2:
                    even = lane_iota(value.shape[0]) % 2 == 0
                    values = [jnp.where(even, value, right(value, 1)), jnp.where(even, left(value, 1), value)]
                for (field, comp, (_, _, z, y, count, along)), value in zip(runs, values):
                    refs[field][window(self.grid, comp, z, y, count, along), :] = value

    def drain(self):
        for d, (dz, dy) in enumerate(DIRS):
            @pl.when(self.exists(dz, dy))
            def _():
                self.copy(d).wait_send()


def lane_iota(rows):
    return lax.broadcasted_iota(jnp.int32, (rows, LANES), 1)


def right(v, step):
    return pltpu.roll(v, step % LANES, 1)


def left(v, step):
    return pltpu.roll(v, LANES - step, 1)


def down(v):
    return pltpu.roll(v, 1, 0)


def up(v):
    return pltpu.roll(v, v.shape[0] - 1, 0)


def pair_sum(v, step):
    lane = lane_iota(v.shape[0])
    first = lane % (2 * step) < step
    return v + jnp.where(first, left(v, step), right(v, step))


def rows_of(start, count):
    if not isinstance(start, int):
        start = pl.multiple_of(start, 8)
    return pl.ds(start, count)


def loop(low, high, rows, plane, body):
    count = high - low
    unit = max(u for u in range(1, count + 1) if count % u == 0 and (u == 1 or 3 * u * rows <= 8 * LIVE))

    def step(i, carry):
        base = low + i * unit
        held, todo = {}, []

        def get(ref, comp, off):
            key = (id(ref), comp, off)
            if key not in held:
                held[key] = ref[plane(comp, base + off), :]
            return held[key]

        for j in range(unit):
            todo += body(lambda ref, comp, off, j=j: get(ref, comp, off + j), base + j)
        for ref, at, value in todo:
            ref[at, :] = value
        return carry

    if count == unit:
        step(0, 0)
    else:
        lax.fori_loop(0, count // unit, step, 0)


class Level:
    def __init__(self, scale, xs, zs, group, ny, closed, plane, k, coef):
        self.scale, self.xs, self.zs, self.group, self.ny, self.closed = scale, xs, zs, group, ny, closed
        self.plane, self.k, self.coef = plane, k, coef

    def loop(self, low, high, body):
        loop(low, high, self.ny, self.plane, body)

    def z_sides(self, get):
        after, before = get(1), get(-1)
        if not self.group:
            return after, before
        here = get(0)
        lane = lane_iota(self.ny) % self.group
        turn = self.group - self.zs
        return (jnp.where(lane < turn, left(here, self.zs), right(after, turn)),
                jnp.where(lane >= self.zs, right(here, self.zs), left(before, turn)))

    def setup(self, low, high):
        def body(get, z):
            k = get(self.k, 0, 0)
            lane = lane_iota(self.ny)
            zp, zm = self.z_sides(lambda off: get(self.k, 0, off))
            inx = lane < LANES - self.xs
            inm = lane >= self.xs
            xp = jnp.where(inx, left(k, self.xs), 0.0)
            xm = jnp.where(inm, right(k, self.xs), 0.0)
            yp, ym = up(k), down(k)
            half = F32(0.5 * self.scale)
            if self.closed:
                row = lax.broadcasted_iota(jnp.int32, (self.ny, LANES), 0)
                iny, inw = row < self.ny - 1, row >= 1
                yp, ym = jnp.where(iny, yp, 0.0), jnp.where(inw, ym, 0.0)
            kzp, kzm = half * (k + zp), half * (k + zm)
            kyp, kym = half * (k + yp), half * (k + ym)
            kxp, kxm = half * (k + xp), half * (k + xm)
            total = kzp + kzm + kyp + kym + kxp + kxm
            if self.closed:
                kyp, kym = jnp.where(iny, kyp, 0.0), jnp.where(inw, kym, 0.0)
            kxp, kxm = jnp.where(inx, kxp, 0.0), jnp.where(inm, kxm, 0.0)
            inside = k > 0.0
            diag = jnp.where(inside, total + F32(2.0 * COUPLE) * k, 1.0)
            weight = jnp.where(inside, F32(OMEGA) / diag, 0.0)
            p = self.plane(0, z)
            return [(self.coef[i], p, value) for i, value in
                    enumerate((kzp, kzm, kyp, kym, kxp, kxm, total + F32(COUPLE) * k, weight))]

        self.loop(low, high, body)

    def first(self, low, high, rhs, out, mask=None):
        def body(get, z):
            weight, todo = get(self.coef[7], 0, 0), []
            if mask is not None:
                weight = weight * get(mask, 0, 0)
                todo = [(self.coef[7], self.plane(0, z), weight)]
            return todo + [(out, self.plane(c, z), weight * get(rhs, c, 0)) for c in range(3)]

        self.loop(low, high, body)

    def defect(self, get, u, rhs):
        kzp, kzm, kyp, kym, kxp, kxm, own = [get(self.coef[i], 0, 0) for i in range(7)]
        couple = F32(COUPLE) * get(self.k, 0, 0)
        field = [get(u, c, 0) for c in range(3)]
        shared = couple * (field[0] + field[1] + field[2])
        out = []
        for c in range(3):
            v = field[c]
            zp, zm = self.z_sides(lambda off: get(u, c, off))
            near = (kzp * zp + kzm * zm) + (kyp * up(v) + kym * down(v))
            near = near + (kxp * left(v, self.xs) + kxm * right(v, self.xs))
            out.append((get(rhs, c, 0) - shared) + (near - own * v))
        return field, out

    def sweep(self, low, high, u, rhs, out, out_plane=None):
        place = out_plane or self.plane

        def body(get, z):
            field, delta = self.defect(get, u, rhs)
            weight = get(self.coef[7], 0, 0)
            return [(out, place(c, z), field[c] + weight * delta[c]) for c in range(3)]

        self.loop(low, high, body)

    def residual(self, low, high, u, rhs, mask, emit):
        def body(get, z):
            field, delta = self.defect(get, u, rhs)
            todo = []
            for c in range(3):
                value = delta[c] if mask is None else get(mask, 0, 0) * delta[c]
                todo += emit(c, z, value, field[c])
            return todo

        self.loop(low, high, body)


def kernel(ns, nc, g0, g1, ex, load_in, dens_in, moduli_in, fixed_in, out_u, out_r, *scratch):
    it = iter(scratch)
    take = lambda n: [next(it) for _ in range(n)]
    k0, m0, b0, ua, ub = take(5)
    c0 = take(8)
    k1, b1, va, vb = take(4)
    c1 = take(8)
    k2, b2, wa, wb, wf = take(5)
    c2 = take(8)
    k3, b3, xa, xb = take(4)
    c3 = take(8)
    gk, gb, stage = take(3)
    s, c = lax.axis_index("slab"), lax.axis_index("col")
    where = (s, c, ns, nc)
    rounds = []
    for grid, fields, pairs in ex:
        send, recv = take(8), take(8)
        ssem, rsem = take(2)
        rounds.append(Exchange(grid, fields, pairs, where, send, recv, ssem, rsem))
    ex_s, ex_a, ex_k, ex_b, ex_u, ex_v = rounds
    load, dens, moduli, fixed, arrived = take(5)
    fetches = [pltpu.make_async_copy(src, dst, arrived.at[i]) for i, (src, dst) in enumerate(
        ((dens_in, dens), (moduli_in, moduli), (fixed_in, fixed), (load_in, load)))]
    for fetch in fetches:
        fetch.start()
    n0, y0, n1, y1 = g0.nz, g0.ny, g1.nz, g1.ny

    def zero(ref):
        rows = ref.shape[0]
        ref[...] = jnp.zeros((rows, LANES), F32)

    barrier = pltpu.get_barrier_semaphore()

    def greet(a, b):
        target = (beside(s, a, ns), beside(c, b, nc))
        pl.semaphore_signal(barrier, inc=1, device_id=target, device_id_type=pl.DeviceIdType.MESH)

    others(ns, nc, greet)

    for ref in (k0, m0, b0, k1):
        zero(ref)

    wide = lambda v: jnp.concatenate(
        [jnp.zeros((g0.oy, LANES), F32), v, jnp.zeros((g0.oy, LANES), F32)], axis=0)
    own_plane = lambda comp, z: rows_of((comp * n0 + z) * y0, y0)

    def fill_stiffness(get, z):
        d = get(dens, 0, 0)
        value = jnp.zeros((y0, LANES), F32)
        for klass in range(CLASSES):
            value = jnp.where(d == klass, moduli[klass], value)
        return [(k0, g0.plane(0, z + g0.oz), wide(value))]

    def fill_rest(get, z):
        keep = 1.0 - get(fixed, 0, 0).astype(F32)
        return [(m0, g0.plane(0, z + g0.oz), wide(keep))] + [
            (b0, g0.plane(comp, z + g0.oz), wide(get(load, comp, 0))) for comp in range(3)]

    for fetch in fetches[:2]:
        fetch.wait()
    loop(0, n0, y0, own_plane, fill_stiffness)
    pl.semaphore_wait(barrier, ns * nc - 1)
    ex_s.start([k0])
    for fetch in fetches[2:]:
        fetch.wait()
    loop(0, n0, y0, own_plane, fill_rest)
    ex_a.start([m0, b0])

    def coarser(src, grid, comp, z, y, count, steps):
        total = None
        for dz in range(2):
            for dy in range(2):
                part = src[pl.ds(grid.row(comp, 2 * z + dz, 2 * y + dy), count, stride=2), :]
                total = part if total is None else total + part
        for step in steps:
            total = pair_sum(total, step)
        return total * F32(0.125)

    for z in range(n1):
        k1[pl.ds(g1.row(0, z, 0), y1), :] = coarser(k0, g0, 0, z, 0, y1, (1,))
    ex_k.start([k1])

    lane4 = lane_iota(4) % 4

    here = s * nc + c

    def packed(src, comp):
        value = jnp.zeros((4, LANES), F32)
        for z in range(n1 // 2):
            value = jnp.where(lane4 == z, coarser(src, g1, comp, z, 0, y1 // 2, (2,)), value)
        return value

    def gather(ref, comps, send_sem, recv_sem):
        own = pl.ds(here * comps, comps)

        def spread(a, b):
            pltpu.make_async_remote_copy(
                src_ref=ref.at[own], dst_ref=ref.at[own], send_sem=send_sem, recv_sem=recv_sem,
                device_id=(beside(s, a, ns), beside(c, b, nc)), device_id_type=pl.DeviceIdType.MESH).start()

        others(ns, nc, spread)
        rest = pl.ds(0, (ns * nc - 1) * comps)
        return pltpu.make_async_remote_copy(
            src_ref=ref.at[rest], dst_ref=ref.at[rest], send_sem=send_sem, recv_sem=recv_sem,
            device_id=(beside(s, 1, ns), c), device_id_type=pl.DeviceIdType.MESH)

    def assemble(ref, comps, out):
        def one(t, carry):
            z, pair = t // (nc // 2), t % (nc // 2)
            for comp in range(comps):
                value = jnp.concatenate([ref[2 * t * comps + comp], ref[(2 * t + 1) * comps + comp]], axis=0)
                out[rows_of((comp * (ns + 2) + z + 1) * y2 + pair * 8, 8), :] = value
            return carry

        if ns * nc <= 32:
            for t in range(ns * nc // 2):
                one(t, 0)
        else:
            lax.fori_loop(0, ns * nc // 2, one, 0)

    level0 = Level(1.0, 1, 0, 0, g0.y, False, g0.plane, k0, c0)
    level1 = Level(0.25, 2, 0, 0, g1.y, False, g1.plane, k1, c1)
    y2, y3 = 4 * nc, 2 * nc
    plane2 = lambda comp, z: rows_of((comp * (ns + 2) + z) * y2, y2)
    plane3 = lambda comp, z: rows_of((comp * (ns + 2) + z) * y3, y3)
    wide2 = lambda comp, z: rows_of((comp * (ns + 2) + z) * (y2 + 16) + 8, y2)
    level2 = Level(0.25**2, 4, 1, 4, y2, True, plane2, k2, c2)
    level3 = Level(0.25**3, 8, 2, 4, y3, True, plane3, k3, c3)
    ex_s.finish([k0])
    level0.setup(g0.oz - 2, g0.oz + n0 + 2)
    gk[here] = packed(k1, 0)
    all_k = gather(gk, 1, *take(2))
    for ref in (ua, ub, b1, va, vb):
        zero(ref)
    for ref, comps, plane, rows in ((k2, 1, plane2, y2), (wa, 3, plane2, y2), (wb, 3, plane2, y2),
                                    (k3, 1, plane3, y3), (xa, 3, plane3, y3), (xb, 3, plane3, y3),
                                    (wf, 3, lambda comp, z: rows_of((comp * (ns + 2) + z) * (y2 + 16), y2 + 16), y2 + 16)):
        for comp in range(comps):
            for z in (0, ns + 1):
                ref[plane(comp, z), :] = jnp.zeros((rows, LANES), F32)
    ex_a.finish([m0, b0])
    level0.first(g0.oz - 2, g0.oz + n0 + 2, b0, ua, m0)
    level0.sweep(g0.oz - 1, g0.oz + n0 + 1, ua, b0, ub)

    def keep0(comp, z, value, field):
        return [(ua, g0.plane(comp, z), value)]

    level0.residual(g0.oz, g0.oz + n0, ub, b0, m0, keep0)
    for comp in range(3):
        for z in range(n1):
            b1[pl.ds(g1.row(comp, z, 0), y1), :] = coarser(ua, g0, comp, z, 0, y1, (1,))
    ex_b.start([b1])

    ex_k.finish([k1])
    level1.setup(g1.oz - 3, g1.oz + n1 + 3)
    all_k.wait_recv()
    assemble(gk, 1, k2)
    level2.setup(1, ns + 1)

    def shrink3(pairs):
        def body(z, carry):
            for src, dst, comp in pairs:
                start = (comp * (ns + 2) + z) * y2
                total = src[pl.ds(start, y3, stride=2), :] + src[pl.ds(start + 1, y3, stride=2), :]
                dst[plane3(comp, z), :] = pair_sum(pair_sum(total, 1), 4) * F32(0.125)
            return carry

        if ns <= 4:
            for z in range(1, ns + 1):
                body(z, 0)
        else:
            lax.fori_loop(1, ns + 1, body, 0)

    shrink3([(k2, k3, 0)])
    level3.setup(1, ns + 1)
    ex_u.start([ub, m0])
    ex_b.finish([b1])
    level1.first(g1.oz - 2, g1.oz + n1 + 2, b1, va)
    level1.sweep(g1.oz - 1, g1.oz + n1 + 1, va, b1, vb)

    ex_v.start([vb])

    def keep1(comp, z, value, field):
        return [(va, g1.plane(comp, z), value)]

    level1.residual(g1.oz, g1.oz + n1, vb, b1, None, keep1)
    for comp in range(3):
        gb[here * 3 + comp] = packed(va, comp)
    all_b = gather(gb, 3, *take(2))
    ex_u.finish([ub, m0])
    ex_v.finish([vb])
    all_k.wait_send()
    for ex_one in rounds:
        ex_one.drain()

    all_b.wait_recv()
    assemble(gb, 3, b2)
    level2.first(1, ns + 1, b2, wa)
    level2.sweep(1, ns + 1, wa, b2, wb)

    def keep2(comp, z, value, field):
        return [(wa, plane2(comp, z), value)]

    level2.residual(1, ns + 1, wb, b2, None, keep2)

    shrink3([(wa, b3, comp) for comp in range(3)])
    level3.first(1, ns + 1, b3, xa)
    old, new = xa, xb
    for turn in range(COARSE_SWEEPS - 1):
        level3.sweep(1, ns + 1, old, b3, new)
        old, new = new, old
    coarse = old

    def twice(value, slot):
        rows = value.shape[0]
        stage[pl.ds(slot, rows, stride=2), :] = value
        stage[pl.ds(slot + 1, rows, stride=2), :] = value
        return slot, 2 * rows

    def staged(spot):
        return stage[pl.ds(spot[0], spot[1]), :]

    def add2(z, carry):
        spots = [twice(coarse[plane3(comp, z), :], comp * y2) for comp in range(3)]
        for comp in range(3):
            p = plane2(comp, z)
            wb[p, :] = wb[p, :] + staged(spots[comp])
        return carry

    lax.fori_loop(1, ns + 1, add2, 0)

    level2.sweep(1, ns + 1, wb, b2, wa)
    level2.sweep(1, ns + 1, wa, b2, wf, wide2)

    lane8 = lane_iota(8)
    odd = c % 2 == 1

    for i in range(g1.z // 2):
        block, j = s + (i + 2) // 4, (i + 2) % 4
        spots = []
        for comp in range(3):
            at = (comp * (ns + 2) + block) * (y2 + 16) + (c // 2) * 8
            rows = wf[pl.ds(pl.multiple_of(at, 8), 24), :]
            value = jnp.where(odd, rows[10:18], rows[6:14])
            value = jnp.where(lane8 % 4 == j, value, 0.0)
            spots.append(twice(pair_sum(pair_sum(value, 1), 2), (i % 2 * 3 + comp) * 16))
        for comp in range(3):
            grown = staged(spots[comp])
            for dz in range(2):
                p = g1.plane(comp, 2 * i + dz)
                inside = k1[g1.plane(0, 2 * i + dz), :] > 0.0
                va[p, :] = vb[p, :] + jnp.where(inside, grown, 0.0)
    level1.sweep(g1.oz - 3, g1.oz + n1 + 3, va, b1, vb)
    level1.sweep(g1.oz - 2, g1.oz + n1 + 2, vb, b1, va)

    def add0(i, carry):
        spots = [twice(va[g1.plane(comp, i + g1.oz - 2), :][2:14], comp * g0.y) for comp in range(3)]
        for comp in range(3):
            grown = staged(spots[comp])
            for dz in range(2):
                p = g0.plane(comp, 2 * i + dz)
                ua[p, :] = ub[p, :] + m0[g0.plane(0, 2 * i + dz), :] * grown
        return carry

    lax.fori_loop(0, g0.z // 2, add0, 0)
    level0.sweep(g0.oz - 2, g0.oz + n0 + 2, ua, b0, ub)
    level0.sweep(g0.oz - 1, g0.oz + n0 + 1, ub, b0, ua)

    def emit(comp, z, value, field):
        at = pl.ds(pl.multiple_of((comp * n0 + z - g0.oz) * y0, 8), y0)
        own = slice(g0.oy, g0.oy + y0)
        return [(out_r, at, value[own]), (out_u, at, field[own])]

    level0.residual(g0.oz, g0.oz + n0, ua, b0, m0, emit)

    all_b.wait_send()


def hand_over(u, r, out_u, out_r, sems):
    copies = [pltpu.make_async_copy(src, dst, sems.at[i]) for i, (src, dst) in enumerate(((u, out_u), (r, out_r)))]
    for one in copies:
        one.start()
    for one in copies:
        one.wait()


def on_device(ns, nc, load, density, moduli, fixed):
    _, nz, ny, nx = load.shape
    g0 = Grid(nz, ny, 4, 4)
    g1 = Grid(nz // 2, ny // 2, 4, 4)
    ex = (
        (g0, ((1, 1, 3),), False),
        (g0, ((1, 1, 2), (3, 1, 2)), False),
        (g1, ((1, 1, 4),), True),
        (g1, ((3, 1, 3),), True),
        (g0, ((3, 2, 3), (1, 3, 3)), False),
        (g1, ((3, 2, 4),), True),
    )
    buf = lambda rows: pltpu.VMEM((rows, LANES), F32)
    y2, y3 = 4 * nc, 2 * nc
    s2, s3 = (ns + 2) * y2, (ns + 2) * y3
    scratch = [buf(g0.rows)] * 2 + [buf(3 * g0.rows)] * 3 + [buf(g0.rows)] * 8
    scratch += [buf(g1.rows)] + [buf(3 * g1.rows)] * 3 + [buf(g1.rows)] * 8
    scratch += [buf(s2)] + [buf(3 * s2)] * 3 + [buf(3 * (ns + 2) * (y2 + 16))] + [buf(s2)] * 8
    scratch += [buf(s3)] + [buf(3 * s3)] * 3 + [buf(s3)] * 8
    scratch += [pltpu.VMEM((ns * nc, 4, LANES), F32), pltpu.VMEM((ns * nc * 3, 4, LANES), F32), buf(3 * max(y2, 32))]
    for grid, fields, pairs in ex:
        sizes = [message(grid, dz, dy, fields, pairs)[1] for dz, dy in DIRS]
        scratch += [buf(n) for n in sizes] * 2
        scratch += [pltpu.SemaphoreType.DMA((8,))] * 2

    def run(*args):
        kernel(ns, nc, g0, g1, ex, *args)

    rows = 3 * nz * ny
    scratch += [buf(rows), pltpu.VMEM((nz * ny, LANES), jnp.int32), pltpu.SMEM((CLASSES,), F32),
                pltpu.VMEM((nz * ny, LANES), jnp.int32), pltpu.SemaphoreType.DMA((4,))]
    scratch += [pltpu.SemaphoreType.DMA] * 4
    used = sum(4 * math.prod(ref.shape) for ref in scratch if hasattr(ref, "shape"))
    vmem = pl.BlockSpec(memory_space=pltpu.VMEM)
    u, r = pl.pallas_call(
        run,
        out_shape=[jax.ShapeDtypeStruct((rows, nx), F32)] * 2,
        in_specs=[pl.BlockSpec(memory_space=pltpu.HBM)] * 4,
        out_specs=[vmem, vmem],
        scratch_shapes=scratch,
        compiler_params=pltpu.CompilerParams(collective_id=0, has_side_effects=True, vmem_limit_bytes=used + 8 * 1024 * 1024),
        name="vcycle",
    )(*[pltpu.with_memory_space_constraint(a, pltpu.HBM) for a in (
        load.reshape(rows, nx), density.reshape(nz * ny, nx), moduli, fixed.reshape(nz * ny, nx))])
    both = pl.BlockSpec(memory_space=pltpu.HBM)
    u, r = pl.pallas_call(
        hand_over,
        out_shape=[jax.ShapeDtypeStruct((rows, nx), F32)] * 2,
        in_specs=[vmem, vmem],
        out_specs=[both, both],
        scratch_shapes=[pltpu.SemaphoreType.DMA((2,))],
        name="hand_over",
    )(*[pltpu.with_memory_space_constraint(a, pltpu.VMEM) for a in (u, r)])
    shape = (3, nz, ny, nx)
    return u.reshape(shape), r.reshape(shape)


def solution(mesh):
    ns, nc = mesh.shape["slab"], mesh.shape["col"]
    placed = (P(None, "slab", "col", None), P("slab", "col", None), P(), P("slab", "col", None))

    def body(load, density, moduli, fixed):
        return on_device(ns, nc, load, density, moduli, fixed)

    return jax.shard_map(
        body,
        mesh=mesh,
        in_specs=placed,
        out_specs=(P(None, "slab", "col", None), P(None, "slab", "col", None)),
        check_vma=False,
    )
```

```python
import math

import jax
import jax.numpy as jnp
from jax import lax
from jax.experimental import pallas as pl
from jax.experimental.pallas import tpu as pltpu
from jax.sharding import PartitionSpec as P

OMEGA = 0.6
COUPLE = 0.05
CLASSES = 8
COARSE_SWEEPS = 8
LANES = 128
F32 = jnp.float32
LIVE = 36
DIRS = ((0, 1), (0, -1), (1, 0), (-1, 0), (1, 1), (1, -1), (-1, 1), (-1, -1))


class Grid:
    def __init__(self, nz, ny, oz, oy):
        self.nz, self.ny, self.oz, self.oy = nz, ny, oz, oy
        self.z, self.y = nz + 2 * oz, ny + 2 * oy
        self.rows = self.z * self.y

    def row(self, comp, z, y):
        return comp * self.rows + (z + self.oz) * self.y + y + self.oy

    def plane(self, comp, z):
        start = comp * self.rows + z * self.y
        if not isinstance(start, int):
            start = pl.multiple_of(start, 8)
        return pl.ds(start, self.y)


def segments(grid, dz, dy, low, depth):
    nz, ny = grid.nz, grid.ny

    def cell(step, d, n):
        return (n - step, -step) if d > 0 else (step - 1, n - 1 + step)

    out = []
    if dz == 0:
        for i in range(low, depth + 1):
            mine, there = cell(i, dy, ny)
            out.append((0, mine, 0, there, nz, True))
    elif dy == 0:
        for i in range(low, depth + 1):
            mine, there = cell(i, dz, nz)
            out.append((mine, 0, there, 0, ny, False))
    else:
        for i in range(1, depth):
            for j in range(max(1, low - i), depth + 1 - i):
                mz, tz = cell(i, dz, nz)
                my, ty = cell(j, dy, ny)
                out.append((mz, my, tz, ty, 1, False))
    return out


def message(grid, dz, dy, fields, pairs):
    runs = [(field, comp, seg) for field, (comps, low, depth) in enumerate(fields) for comp in range(comps)
            for seg in segments(grid, dz, dy, low, depth)]
    width = 2 if pairs else 1
    out, at = [], 0
    for first in range(0, len(runs), width):
        part = runs[first:first + width]
        out.append((part, at))
        at += part[0][2][4]
    return out, -(-at // 8) * 8


def window(grid, comp, z, y, count, along_z):
    start = grid.row(comp, z, y)
    if along_z:
        return pl.ds(start, count, stride=grid.y)
    return pl.ds(start, count)


def beside(here, step, count):
    if not isinstance(step, int):
        return lax.rem(here + step, count)
    if step == 0:
        return here
    if step > 0:
        return jnp.where(here >= count - step, here + (step - count), here + step)
    return jnp.where(here < -step, here + (step + count), here + step)


def others(ns, nc, body):
    if ns * nc <= 32:
        for a in range(ns):
            for b in range(nc):
                if a or b:
                    body(a, b)
        return

    def one(t, carry):
        body(t // nc, t % nc)
        return carry

    lax.fori_loop(1, ns * nc, one, 0)


class Exchange:
    def __init__(self, grid, fields, pairs, where, send, recv, ssem, rsem):
        self.grid, self.fields, self.pairs, self.where = grid, fields, pairs, where
        self.send, self.recv, self.ssem, self.rsem = send, recv, ssem, rsem

    def copy(self, d):
        dz, dy = DIRS[d]
        s, c, ns, nc = self.where
        target = (beside(s, dz, ns), beside(c, dy, nc))
        return pltpu.make_async_remote_copy(
            src_ref=self.send[d], dst_ref=self.recv[d], send_sem=self.ssem.at[d], recv_sem=self.rsem.at[d],
            device_id=target, device_id_type=pl.DeviceIdType.MESH)

    def exists(self, dz, dy):
        s, c, ns, nc = self.where
        ok = None
        for here, d, n in ((s, dz, ns), (c, dy, nc)):
            if d:
                near = here < n - 1 if d > 0 else here > 0
                ok = near if ok is None else jnp.logical_and(ok, near)
        return ok

    def start(self, refs):
        for d, (dz, dy) in enumerate(DIRS):
            parts, _ = message(self.grid, dz, dy, self.fields, self.pairs)
            for runs, at in parts:
                values = [refs[field][window(self.grid, comp, z, y, count, along), :]
                          for field, comp, (z, y, _, _, count, along) in runs]
                value = values[0]
                if len(values) == 2:
                    value = jnp.where(lane_iota(value.shape[0]) % 2 == 0, value, values[1])
                self.send[d][pl.ds(at, value.shape[0]), :] = value
        for d, (dz, dy) in enumerate(DIRS):
            @pl.when(self.exists(dz, dy))
            def _():
                self.copy(d).start()

    def finish(self, refs):
        for d, (dz, dy) in enumerate(DIRS):
            @pl.when(self.exists(-dz, -dy))
            def _():
                self.copy(d).wait_recv()
        for d, (dz, dy) in enumerate(DIRS):
            parts, _ = message(self.grid, dz, dy, self.fields, self.pairs)
            here = self.exists(-dz, -dy)
            for runs, at in parts:
                value = jnp.where(here, self.recv[d][pl.ds(at, runs[0][2][4]), :], 0.0)
                values = [value]
                if len(runs) == 2:
                    even = lane_iota(value.shape[0]) % 2 == 0
                    values = [jnp.where(even, value, right(value, 1)), jnp.where(even, left(value, 1), value)]
                for (field, comp, (_, _, z, y, count, along)), value in zip(runs, values):
                    refs[field][window(self.grid, comp, z, y, count, along), :] = value

    def drain(self):
        for d, (dz, dy) in enumerate(DIRS):
            @pl.when(self.exists(dz, dy))
            def _():
                self.copy(d).wait_send()


def lane_iota(rows):
    return lax.broadcasted_iota(jnp.int32, (rows, LANES), 1)


def right(v, step):
    return pltpu.roll(v, step % LANES, 1)


def left(v, step):
    return pltpu.roll(v, LANES - step, 1)


def down(v):
    return pltpu.roll(v, 1, 0)


def up(v):
    return pltpu.roll(v, v.shape[0] - 1, 0)


def pair_sum(v, step):
    lane = lane_iota(v.shape[0])
    first = lane % (2 * step) < step
    return v + jnp.where(first, left(v, step), right(v, step))


def rows_of(start, count):
    if not isinstance(start, int):
        start = pl.multiple_of(start, 8)
    return pl.ds(start, count)


def loop(low, high, rows, plane, body):
    count = high - low
    unit = max(u for u in range(1, count + 1) if count % u == 0 and (u == 1 or 3 * u * rows <= 8 * LIVE))

    def step(i, carry):
        base = low + i * unit
        held, todo = {}, []

        def get(ref, comp, off):
            key = (id(ref), comp, off)
            if key not in held:
                held[key] = ref[plane(comp, base + off), :]
            return held[key]

        for j in range(unit):
            todo += body(lambda ref, comp, off, j=j: get(ref, comp, off + j), base + j)
        for ref, at, value in todo:
            ref[at, :] = value
        return carry

    if count == unit:
        step(0, 0)
    else:
        lax.fori_loop(0, count // unit, step, 0)


class Level:
    def __init__(self, scale, xs, zs, group, ny, closed, plane, k, coef):
        self.scale, self.xs, self.zs, self.group, self.ny, self.closed = scale, xs, zs, group, ny, closed
        self.plane, self.k, self.coef = plane, k, coef

    def loop(self, low, high, body):
        loop(low, high, self.ny, self.plane, body)

    def z_sides(self, get):
        after, before = get(1), get(-1)
        if not self.group:
            return after, before
        here = get(0)
        lane = lane_iota(self.ny) % self.group
        turn = self.group - self.zs
        return (jnp.where(lane < turn, left(here, self.zs), right(after, turn)),
                jnp.where(lane >= self.zs, right(here, self.zs), left(before, turn)))

    def setup(self, low, high):
        def body(get, z):
            k = get(self.k, 0, 0)
            lane = lane_iota(self.ny)
            zp, zm = self.z_sides(lambda off: get(self.k, 0, off))
            inx = lane < LANES - self.xs
            inm = lane >= self.xs
            xp = jnp.where(inx, left(k, self.xs), 0.0)
            xm = jnp.where(inm, right(k, self.xs), 0.0)
            yp, ym = up(k), down(k)
            half = F32(0.5 * self.scale)
            if self.closed:
                row = lax.broadcasted_iota(jnp.int32, (self.ny, LANES), 0)
                iny, inw = row < self.ny - 1, row >= 1
                yp, ym = jnp.where(iny, yp, 0.0), jnp.where(inw, ym, 0.0)
            kzp, kzm = half * (k + zp), half * (k + zm)
            kyp, kym = half * (k + yp), half * (k + ym)
            kxp, kxm = half * (k + xp), half * (k + xm)
            total = kzp + kzm + kyp + kym + kxp + kxm
            if self.closed:
                kyp, kym = jnp.where(iny, kyp, 0.0), jnp.where(inw, kym, 0.0)
            kxp, kxm = jnp.where(inx, kxp, 0.0), jnp.where(inm, kxm, 0.0)
            inside = k > 0.0
            diag = jnp.where(inside, total + F32(2.0 * COUPLE) * k, 1.0)
            weight = jnp.where(inside, F32(OMEGA) / diag, 0.0)
            p = self.plane(0, z)
            return [(self.coef[i], p, value) for i, value in
                    enumerate((kzp, kzm, kyp, kym, kxp, kxm, total + F32(COUPLE) * k, weight))]

        self.loop(low, high, body)

    def first(self, low, high, rhs, out, mask=None):
        def body(get, z):
            weight, todo = get(self.coef[7], 0, 0), []
            if mask is not None:
                weight = weight * get(mask, 0, 0)
                todo = [(self.coef[7], self.plane(0, z), weight)]
            return todo + [(out, self.plane(c, z), weight * get(rhs, c, 0)) for c in range(3)]

        self.loop(low, high, body)

    def defect(self, get, u, rhs):
        kzp, kzm, kyp, kym, kxp, kxm, own = [get(self.coef[i], 0, 0) for i in range(7)]
        couple = F32(COUPLE) * get(self.k, 0, 0)
        field = [get(u, c, 0) for c in range(3)]
        shared = couple * (field[0] + field[1] + field[2])
        out = []
        for c in range(3):
            v = field[c]
            zp, zm = self.z_sides(lambda off: get(u, c, off))
            near = (kzp * zp + kzm * zm) + (kyp * up(v) + kym * down(v))
            near = near + (kxp * left(v, self.xs) + kxm * right(v, self.xs))
            out.append((get(rhs, c, 0) - shared) + (near - own * v))
        return field, out

    def sweep(self, low, high, u, rhs, out, out_plane=None):
        place = out_plane or self.plane

        def body(get, z):
            field, delta = self.defect(get, u, rhs)
            weight = get(self.coef[7], 0, 0)
            return [(out, place(c, z), field[c] + weight * delta[c]) for c in range(3)]

        self.loop(low, high, body)

    def residual(self, low, high, u, rhs, mask, emit):
        def body(get, z):
            field, delta = self.defect(get, u, rhs)
            todo = []
            for c in range(3):
                value = delta[c] if mask is None else get(mask, 0, 0) * delta[c]
                todo += emit(c, z, value, field[c])
            return todo

        self.loop(low, high, body)


def kernel(ns, nc, g0, g1, ex, load_in, dens_in, moduli_in, fixed_in, out_u, out_r, *scratch):
    it = iter(scratch)
    take = lambda n: [next(it) for _ in range(n)]
    k0, m0, b0, ua, ub = take(5)
    c0 = take(8)
    k1, b1, va, vb = take(4)
    c1 = take(8)
    k2, b2, wa, wb, wf = take(5)
    c2 = take(8)
    k3, b3, xa, xb = take(4)
    c3 = take(8)
    gk, gb, stage = take(3)
    s, c = lax.axis_index("slab"), lax.axis_index("col")
    where = (s, c, ns, nc)
    rounds = []
    for grid, fields, pairs in ex:
        send, recv = take(8), take(8)
        ssem, rsem = take(2)
        rounds.append(Exchange(grid, fields, pairs, where, send, recv, ssem, rsem))
    ex_s, ex_a, ex_k, ex_b, ex_u, ex_v = rounds
    load, dens, moduli, fixed, arrived = take(5)
    fetches = [pltpu.make_async_copy(src, dst, arrived.at[i]) for i, (src, dst) in enumerate(
        ((dens_in, dens), (moduli_in, moduli), (fixed_in, fixed), (load_in, load)))]
    for fetch in fetches:
        fetch.start()
    n0, y0, n1, y1 = g0.nz, g0.ny, g1.nz, g1.ny

    def zero(ref):
        rows = ref.shape[0]
        ref[...] = jnp.zeros((rows, LANES), F32)

    barrier = pltpu.get_barrier_semaphore()

    def greet(a, b):
        target = (beside(s, a, ns), beside(c, b, nc))
        pl.semaphore_signal(barrier, inc=1, device_id=target, device_id_type=pl.DeviceIdType.MESH)

    others(ns, nc, greet)

    for ref in (k0, m0, b0, k1):
        zero(ref)

    wide = lambda v: jnp.concatenate(
        [jnp.zeros((g0.oy, LANES), F32), v, jnp.zeros((g0.oy, LANES), F32)], axis=0)
    own_plane = lambda comp, z: rows_of((comp * n0 + z) * y0, y0)

    def fill_stiffness(get, z):
        d = get(dens, 0, 0)
        value = jnp.zeros((y0, LANES), F32)
        for klass in range(CLASSES):
            value = jnp.where(d == klass, moduli[klass], value)
        return [(k0, g0.plane(0, z + g0.oz), wide(value))]

    def fill_rest(get, z):
        keep = 1.0 - get(fixed, 0, 0).astype(F32)
        return [(m0, g0.plane(0, z + g0.oz), wide(keep))] + [
            (b0, g0.plane(comp, z + g0.oz), wide(get(load, comp, 0))) for comp in range(3)]

    for fetch in fetches[:2]:
        fetch.wait()
    loop(0, n0, y0, own_plane, fill_stiffness)
    pl.semaphore_wait(barrier, ns * nc - 1)
    ex_s.start([k0])
    for fetch in fetches[2:]:
        fetch.wait()
    loop(0, n0, y0, own_plane, fill_rest)
    ex_a.start([m0, b0])

    def coarser(src, grid, comp, z, y, count, steps):
        total = None
        for dz in range(2):
            for dy in range(2):
                part = src[pl.ds(grid.row(comp, 2 * z + dz, 2 * y + dy), count, stride=2), :]
                total = part if total is None else total + part
        for step in steps:
            total = pair_sum(total, step)
        return total * F32(0.125)


    lane4 = lane_iota(4) % 4

    here = s * nc + c

    def packed(src, comp):
        value = jnp.zeros((4, LANES), F32)
        for z in range(n1 // 2):
            value = jnp.where(lane4 == z, coarser(src, g1, comp, z, 0, y1 // 2, (2,)), value)
        return value

    def gather(ref, comps, send_sem, recv_sem):
        own = pl.ds(here * comps, comps)

        def spread(a, b):
            pltpu.make_async_remote_copy(
                src_ref=ref.at[own], dst_ref=ref.at[own], send_sem=send_sem, recv_sem=recv_sem,
                device_id=(beside(s, a, ns), beside(c, b, nc)), device_id_type=pl.DeviceIdType.MESH).start()

        others(ns, nc, spread)
        rest = pl.ds(0, (ns * nc - 1) * comps)
        return pltpu.make_async_remote_copy(
            src_ref=ref.at[rest], dst_ref=ref.at[rest], send_sem=send_sem, recv_sem=recv_sem,
            device_id=(beside(s, 1, ns), c), device_id_type=pl.DeviceIdType.MESH)

    def assemble(ref, comps, out):
        def one(t, carry):
            z, pair = t // (nc // 2), t % (nc // 2)
            for comp in range(comps):
                value = jnp.concatenate([ref[2 * t * comps + comp], ref[(2 * t + 1) * comps + comp]], axis=0)
                out[rows_of((comp * (ns + 2) + z + 1) * y2 + pair * 8, 8), :] = value
            return carry

        if ns * nc <= 32:
            for t in range(ns * nc // 2):
                one(t, 0)
        else:
            lax.fori_loop(0, ns * nc // 2, one, 0)

    level0 = Level(1.0, 1, 0, 0, g0.y, False, g0.plane, k0, c0)
    level1 = Level(0.25, 2, 0, 0, g1.y, False, g1.plane, k1, c1)
    y2, y3 = 4 * nc, 2 * nc
    plane2 = lambda comp, z: rows_of((comp * (ns + 2) + z) * y2, y2)
    plane3 = lambda comp, z: rows_of((comp * (ns + 2) + z) * y3, y3)
    wide2 = lambda comp, z: rows_of((comp * (ns + 2) + z) * (y2 + 16) + 8, y2)
    level2 = Level(0.25**2, 4, 1, 4, y2, True, plane2, k2, c2)
    level3 = Level(0.25**3, 8, 2, 4, y3, True, plane3, k3, c3)
    ex_s.finish([k0])
    level0.setup(g0.oz - 2, g0.oz + n0 + 2)
    for z in range(n1):
        k1[pl.ds(g1.row(0, z, 0), y1), :] = coarser(k0, g0, 0, z, 0, y1, (1,))
    ex_k.start([k1])
    gk[here] = packed(k1, 0)
    all_k = gather(gk, 1, *take(2))
    for ref in (ua, ub, b1, va, vb):
        zero(ref)
    for ref, comps, plane, rows in ((k2, 1, plane2, y2), (wa, 3, plane2, y2), (wb, 3, plane2, y2),
                                    (k3, 1, plane3, y3), (xa, 3, plane3, y3), (xb, 3, plane3, y3),
                                    (wf, 3, lambda comp, z: rows_of((comp * (ns + 2) + z) * (y2 + 16), y2 + 16), y2 + 16)):
        for comp in range(comps):
            for z in (0, ns + 1):
                ref[plane(comp, z), :] = jnp.zeros((rows, LANES), F32)
    ex_a.finish([m0, b0])
    level0.first(g0.oz - 2, g0.oz + n0 + 2, b0, ua, m0)
    level0.sweep(g0.oz - 1, g0.oz + n0 + 1, ua, b0, ub)

    def keep0(comp, z, value, field):
        return [(ua, g0.plane(comp, z), value)]

    level0.residual(g0.oz, g0.oz + n0, ub, b0, m0, keep0)
    for comp in range(3):
        for z in range(n1):
            b1[pl.ds(g1.row(comp, z, 0), y1), :] = coarser(ua, g0, comp, z, 0, y1, (1,))
    ex_b.start([b1])

    ex_k.finish([k1])
    level1.setup(g1.oz - 3, g1.oz + n1 + 3)
    all_k.wait_recv()
    assemble(gk, 1, k2)
    level2.setup(1, ns + 1)

    def shrink3(pairs):
        def body(z, carry):
            for src, dst, comp in pairs:
                start = (comp * (ns + 2) + z) * y2
                total = src[pl.ds(start, y3, stride=2), :] + src[pl.ds(start + 1, y3, stride=2), :]
                dst[plane3(comp, z), :] = pair_sum(pair_sum(total, 1), 4) * F32(0.125)
            return carry

        if ns <= 4:
            for z in range(1, ns + 1):
                body(z, 0)
        else:
            lax.fori_loop(1, ns + 1, body, 0)

    shrink3([(k2, k3, 0)])
    level3.setup(1, ns + 1)
    ex_u.start([ub, m0])
    ex_b.finish([b1])
    level1.first(g1.oz - 2, g1.oz + n1 + 2, b1, va)
    level1.sweep(g1.oz - 1, g1.oz + n1 + 1, va, b1, vb)

    ex_v.start([vb])

    def keep1(comp, z, value, field):
        return [(va, g1.plane(comp, z), value)]

    level1.residual(g1.oz, g1.oz + n1, vb, b1, None, keep1)
    for comp in range(3):
        gb[here * 3 + comp] = packed(va, comp)
    all_b = gather(gb, 3, *take(2))
    ex_u.finish([ub, m0])
    ex_v.finish([vb])
    all_k.wait_send()
    for ex_one in rounds:
        ex_one.drain()

    all_b.wait_recv()
    assemble(gb, 3, b2)
    level2.first(1, ns + 1, b2, wa)
    level2.sweep(1, ns + 1, wa, b2, wb)

    def keep2(comp, z, value, field):
        return [(wa, plane2(comp, z), value)]

    level2.residual(1, ns + 1, wb, b2, None, keep2)

    shrink3([(wa, b3, comp) for comp in range(3)])
    level3.first(1, ns + 1, b3, xa)
    old, new = xa, xb
    for turn in range(COARSE_SWEEPS - 1):
        level3.sweep(1, ns + 1, old, b3, new)
        old, new = new, old
    coarse = old

    def twice(value, slot):
        rows = value.shape[0]
        stage[pl.ds(slot, rows, stride=2), :] = value
        stage[pl.ds(slot + 1, rows, stride=2), :] = value
        return slot, 2 * rows

    def staged(spot):
        return stage[pl.ds(spot[0], spot[1]), :]

    def add2(z, carry):
        spots = [twice(coarse[plane3(comp, z), :], comp * y2) for comp in range(3)]
        for comp in range(3):
            p = plane2(comp, z)
            wb[p, :] = wb[p, :] + staged(spots[comp])
        return carry

    lax.fori_loop(1, ns + 1, add2, 0)

    level2.sweep(1, ns + 1, wb, b2, wa)
    level2.sweep(1, ns + 1, wa, b2, wf, wide2)

    lane8 = lane_iota(8)
    odd = c % 2 == 1

    for i in range(g1.z // 2):
        block, j = s + (i + 2) // 4, (i + 2) % 4
        spots = []
        for comp in range(3):
            at = (comp * (ns + 2) + block) * (y2 + 16) + (c // 2) * 8
            rows = wf[pl.ds(pl.multiple_of(at, 8), 24), :]
            value = jnp.where(odd, rows[10:18], rows[6:14])
            value = jnp.where(lane8 % 4 == j, value, 0.0)
            spots.append(twice(pair_sum(pair_sum(value, 1), 2), (i % 2 * 3 + comp) * 16))
        for comp in range(3):
            grown = staged(spots[comp])
            for dz in range(2):
                p = g1.plane(comp, 2 * i + dz)
                inside = k1[g1.plane(0, 2 * i + dz), :] > 0.0
                va[p, :] = vb[p, :] + jnp.where(inside, grown, 0.0)
    level1.sweep(g1.oz - 3, g1.oz + n1 + 3, va, b1, vb)
    level1.sweep(g1.oz - 2, g1.oz + n1 + 2, vb, b1, va)

    def add0(i, carry):
        spots = [twice(va[g1.plane(comp, i + g1.oz - 2), :][2:14], comp * g0.y) for comp in range(3)]
        for comp in range(3):
            grown = staged(spots[comp])
            for dz in range(2):
                p = g0.plane(comp, 2 * i + dz)
                ua[p, :] = ub[p, :] + m0[g0.plane(0, 2 * i + dz), :] * grown
        return carry

    lax.fori_loop(0, g0.z // 2, add0, 0)
    level0.sweep(g0.oz - 2, g0.oz + n0 + 2, ua, b0, ub)
    level0.sweep(g0.oz - 1, g0.oz + n0 + 1, ub, b0, ua)

    def emit(comp, z, value, field):
        at = pl.ds(pl.multiple_of((comp * n0 + z - g0.oz) * y0, 8), y0)
        own = slice(g0.oy, g0.oy + y0)
        return [(out_r, at, value[own]), (out_u, at, field[own])]

    level0.residual(g0.oz, g0.oz + n0, ua, b0, m0, emit)

    all_b.wait_send()


def hand_over(u, r, out_u, out_r, sems):
    copies = [pltpu.make_async_copy(src, dst, sems.at[i]) for i, (src, dst) in enumerate(((u, out_u), (r, out_r)))]
    for one in copies:
        one.start()
    for one in copies:
        one.wait()


def on_device(ns, nc, load, density, moduli, fixed):
    _, nz, ny, nx = load.shape
    g0 = Grid(nz, ny, 4, 4)
    g1 = Grid(nz // 2, ny // 2, 4, 4)
    ex = (
        (g0, ((1, 1, 3),), False),
        (g0, ((1, 1, 2), (3, 1, 2)), False),
        (g1, ((1, 1, 4),), True),
        (g1, ((3, 1, 3),), True),
        (g0, ((3, 2, 3), (1, 3, 3)), False),
        (g1, ((3, 2, 4),), True),
    )
    buf = lambda rows: pltpu.VMEM((rows, LANES), F32)
    y2, y3 = 4 * nc, 2 * nc
    s2, s3 = (ns + 2) * y2, (ns + 2) * y3
    scratch = [buf(g0.rows)] * 2 + [buf(3 * g0.rows)] * 3 + [buf(g0.rows)] * 8
    scratch += [buf(g1.rows)] + [buf(3 * g1.rows)] * 3 + [buf(g1.rows)] * 8
    scratch += [buf(s2)] + [buf(3 * s2)] * 3 + [buf(3 * (ns + 2) * (y2 + 16))] + [buf(s2)] * 8
    scratch += [buf(s3)] + [buf(3 * s3)] * 3 + [buf(s3)] * 8
    scratch += [pltpu.VMEM((ns * nc, 4, LANES), F32), pltpu.VMEM((ns * nc * 3, 4, LANES), F32), buf(3 * max(y2, 32))]
    for grid, fields, pairs in ex:
        sizes = [message(grid, dz, dy, fields, pairs)[1] for dz, dy in DIRS]
        scratch += [buf(n) for n in sizes] * 2
        scratch += [pltpu.SemaphoreType.DMA((8,))] * 2

    def run(*args):
        kernel(ns, nc, g0, g1, ex, *args)

    rows = 3 * nz * ny
    scratch += [buf(rows), pltpu.VMEM((nz * ny, LANES), jnp.int32), pltpu.SMEM((CLASSES,), F32),
                pltpu.VMEM((nz * ny, LANES), jnp.int32), pltpu.SemaphoreType.DMA((4,))]
    scratch += [pltpu.SemaphoreType.DMA] * 4
    used = sum(4 * math.prod(ref.shape) for ref in scratch if hasattr(ref, "shape"))
    vmem = pl.BlockSpec(memory_space=pltpu.VMEM)
    u, r = pl.pallas_call(
        run,
        out_shape=[jax.ShapeDtypeStruct((rows, nx), F32)] * 2,
        in_specs=[pl.BlockSpec(memory_space=pltpu.HBM)] * 4,
        out_specs=[vmem, vmem],
        scratch_shapes=scratch,
        compiler_params=pltpu.CompilerParams(collective_id=0, has_side_effects=True, vmem_limit_bytes=used + 8 * 1024 * 1024),
        name="vcycle",
    )(*[pltpu.with_memory_space_constraint(a, pltpu.HBM) for a in (
        load.reshape(rows, nx), density.reshape(nz * ny, nx), moduli, fixed.reshape(nz * ny, nx))])
    both = pl.BlockSpec(memory_space=pltpu.HBM)
    u, r = pl.pallas_call(
        hand_over,
        out_shape=[jax.ShapeDtypeStruct((rows, nx), F32)] * 2,
        in_specs=[vmem, vmem],
        out_specs=[both, both],
        scratch_shapes=[pltpu.SemaphoreType.DMA((2,))],
        name="hand_over",
    )(*[pltpu.with_memory_space_constraint(a, pltpu.VMEM) for a in (u, r)])
    shape = (3, nz, ny, nx)
    return u.reshape(shape), r.reshape(shape)


def solution(mesh):
    ns, nc = mesh.shape["slab"], mesh.shape["col"]
    placed = (P(None, "slab", "col", None), P("slab", "col", None), P(), P("slab", "col", None))

    def body(load, density, moduli, fixed):
        return on_device(ns, nc, load, density, moduli, fixed)

    return jax.shard_map(
        body,
        mesh=mesh,
        in_specs=placed,
        out_specs=(P(None, "slab", "col", None), P(None, "slab", "col", None)),
        check_vma=False,
    )
```
